128 devices in a mesh: dp: 16 (over y, z), cores: 8 (over x, core).
Axes of the slice: x: 4, y: 4, z: 4, core: 2. Of those that a mesh axis runs over, the one named last changes fastest.
Arguments:
- item_digits: int32 [3, 65536], P(None, ('dp', 'cores')), may hold values from 0 to 2047, as said below
- first_core: bfloat16 [2048, 512], replicated, may hold values from -6 to 6
- middle_core: bfloat16 [32768, 512], P(('dp', 'cores')), may hold values from -0.75 to 0.75
- last_core: bfloat16 [1024, 512], replicated, may hold values from -0.75 to 0.75
- w_proj: bfloat16 [512, 2048], replicated, may hold values from -0.25 to 0.25
- w_out: bfloat16 [512, 512], replicated, may hold values from -0.25 to 0.25
- layer_grad: bfloat16 [65536, 512], P(('dp', 'cores')), may hold values from -6 to 6
Outputs:
- layer_out: bfloat16 [65536, 512], P(('dp', 'cores'))
- grad_first: float32 [2048, 512], replicated
- grad_middle: float32 [32768, 512], P(('dp', 'cores'))
- grad_last: float32 [1024, 512], replicated
- grad_proj: float32 [512, 2048], replicated
- grad_out: float32 [512, 512], replicated
The draws below stay inside these ranges and needn't reach their ends.
Inputs may be any that keep to these rules, and one draw needn't show every extreme that they name: `item_digits`: row 0 lies below 2048, row 1 below 512, row 2 below 1024. An event's owner is its row 1 value divided by 4 (rounded down), the device holding its middle slice. Every history has exactly 8 events of one owner, the same owner for all histories, and its other events spread as evenly as possible over the other owners.
All inputs are finite; a program needn't handle non-finite values.
Results may differ from the reference program's by a relative error of at most 0.017.
Values may be sent and summed in bfloat16 or wider, within the bound.
A program may use at most 192 MiB of HBM per device.

```python
import math
import jax
import jax.numpy as jnp
from jax import lax

D1 = 8
D2 = 8
D3 = 8
D = 512
RANK = 64
HEADS = 4
P1 = 2048
P2 = 512
P3 = 1024
TOK_DEV = 512
HISTS = 128
TOKENS = 65536
CAP = 8


def draw_item_digits(key, part):
    key = jax.random.fold_in(key, 7)
    keys = jax.random.split(key, 5)
    slices = P2 // HISTS
    popular = jax.random.randint(keys[0], (), 0, HISTS).astype(jnp.int32)
    others = jnp.arange(TOK_DEV - CAP, dtype=jnp.int32) % (HISTS - 1)
    others = others + (others >= popular).astype(jnp.int32)
    base = jnp.concatenate([jnp.zeros((CAP,), jnp.int32) + popular, others])
    row_keys = jax.random.split(keys[1], HISTS)

    def shuffle(row_key):
        return jax.random.permutation(row_key, base)
    owner = jax.vmap(shuffle)(row_keys).reshape(-1)
    middle_index = owner * slices + jax.random.randint(keys[2], (TOKENS,), 0, slices)
    first_index = jax.random.randint(keys[3], (TOKENS,), 0, P1)
    last_index = jax.random.randint(keys[4], (TOKENS,), 0, P3)
    return jnp.stack([first_index, middle_index, last_index]).astype(jnp.int32)


def shard_levels(rng, extent, cuts, least, high):
    def one(dim, parts):
        steps = jax.random.uniform(jax.random.fold_in(jax.random.fold_in(rng, 6), dim), (parts,), jnp.float32, least / len(cuts), high / len(cuts))
        return jnp.repeat(jnp.exp(steps), extent[dim] // parts).reshape((-1,) + (1,) * (len(extent) - dim - 1))

    gain = one(*cuts[0])
    for cut in cuts[1:]:
        gain = gain * one(*cut)
    return gain


def gaussian(rng, shape, width, most, cuts=(), kind=jnp.bfloat16):
    array = jax.random.normal(rng, shape, jnp.float32) * width
    if len(cuts) > 0:
        array = shard_levels(rng, shape, cuts, -0.22, 0.18) * array
    return jnp.clip(array, min=-most, max=most).astype(kind)


def setup_inputs(seed: int = 0) -> dict:
    key_list = jax.random.split(jax.random.key(seed), 8)
    item_digits = draw_item_digits(jax.random.fold_in(key_list[7], 71), 0)
    first_core = gaussian(key_list[1], (P1, D1 * RANK), 1.0, 6.0)
    middle_core = gaussian(key_list[2], (P2 * RANK, D2 * RANK), RANK ** -0.5, 0.75, ((0, 128),))
    last_core = gaussian(key_list[3], (P3, RANK * D3), RANK ** -0.5, 0.75)
    w_proj = gaussian(key_list[4], (D, 4 * D), D ** -0.5, 0.25)
    w_out = gaussian(key_list[5], (D, D), D ** -0.5, 0.25)
    layer_grad = gaussian(key_list[6], (TOKENS, D), 1.0, 6.0, ((0, 128),))
    return {"item_digits": item_digits, "first_core": first_core, "middle_core": middle_core, "last_core": last_core, "w_proj": w_proj, "w_out": w_out, "layer_grad": layer_grad}


def layer_norm(values_in):
    center = values_in - lax.optimization_barrier(jnp.mean(values_in, axis=-1, keepdims=True))
    spread = lax.optimization_barrier(jnp.mean(center * center, axis=-1, keepdims=True))
    return center * lax.rsqrt(spread + 1e-05)

def hstu_layer(embedded, w_proj, w_out):
    length = embedded.shape[0]
    row_width = embedded.shape[1]
    head_size = row_width // HEADS
    rows_f = embedded.astype(jnp.float32)
    normed = layer_norm(rows_f).astype(jnp.bfloat16)
    activated = jax.nn.silu(jnp.dot(normed, w_proj, preferred_element_type=jnp.float32))
    gate_u = activated[:, :row_width].astype(jnp.bfloat16)
    values = activated[:, row_width:2 * row_width].astype(jnp.bfloat16)
    queries = activated[:, 2 * row_width:3 * row_width].astype(jnp.bfloat16)
    key_heads = activated[:, 3 * row_width:].astype(jnp.bfloat16)
    query_f = queries.astype(jnp.float32).reshape(length, HEADS, head_size)
    key_f = key_heads.astype(jnp.float32).reshape(length, HEADS, head_size)
    value_f = values.astype(jnp.float32).reshape(length, HEADS, head_size)
    scores = jnp.einsum('qhd,khd->hqk', query_f, key_f) * (1.0 / math.sqrt(head_size))
    places = jnp.arange(length, dtype=jnp.int32)
    causal = places[:, None] >= places[None, :]
    attn_weights = jnp.where(causal[None], jax.nn.silu(scores), 0.0).astype(jnp.bfloat16)
    mixed_heads = jnp.einsum('hqk,khd->qhd', attn_weights.astype(jnp.float32), value_f).reshape(length, row_width)
    gated_rows = (layer_norm(mixed_heads) * gate_u.astype(jnp.float32)).astype(jnp.bfloat16)
    return (jnp.dot(gated_rows, w_out, preferred_element_type=jnp.float32) + rows_f).astype(jnp.bfloat16)

def reference(item_digits, first_core, middle_core, last_core, w_proj, w_out, layer_grad):
    middle_view = middle_core.reshape(P2, RANK, D2 * RANK)
    digits_view = item_digits.reshape(3, HISTS, TOK_DEV).transpose(1, 0, 2)
    grads_view = layer_grad.reshape(HISTS, TOK_DEV, D)

    def one_history(carry, inputs):
        sum_first, sum_middle, sum_last, sum_proj, sum_out = carry
        digits, cotangent = inputs
        first_index = digits[0]
        middle_index = digits[1]
        last_index = digits[2]
        first_rows = first_core[first_index].reshape(TOK_DEV, D1, RANK).astype(jnp.float32)
        middle_rows = middle_view[middle_index].astype(jnp.float32)
        partial_rows = jnp.einsum('nar,nrq->naq', first_rows, middle_rows).astype(jnp.bfloat16)
        last_rows = last_core[last_index].reshape(TOK_DEV, RANK, D3).astype(jnp.float32)
        partial_four = partial_rows.astype(jnp.float32).reshape(TOK_DEV, D1, D2, RANK)
        embedded = jnp.einsum('nabs,nsc->nabc', partial_four, last_rows).reshape(TOK_DEV, D).astype(jnp.bfloat16)
        layer_rows, pullback = jax.vjp(hstu_layer, embedded, w_proj, w_out)
        row_grad, proj_grad, out_grad = pullback(cotangent)
        row_four = row_grad.astype(jnp.float32).reshape(TOK_DEV, D1, D2, D3)
        partial_grad = jnp.einsum('nabc,nsc->nabs', row_four, last_rows).astype(jnp.bfloat16)
        last_terms = jnp.einsum('nabs,nabc->nsc', partial_four, row_four).reshape(TOK_DEV, RANK * D3)
        grad_flat = partial_grad.astype(jnp.float32).reshape(TOK_DEV, D1, D2 * RANK)
        middle_terms = jnp.einsum('nar,naq->nrq', first_rows, grad_flat)
        first_terms = jnp.einsum('naq,nrq->nar', grad_flat, middle_rows).reshape(TOK_DEV, D1 * RANK)
        sum_first = sum_first + jax.ops.segment_sum(first_terms, first_index, num_segments=P1)
        sum_middle = sum_middle + jax.ops.segment_sum(middle_terms, middle_index, num_segments=P2)
        sum_last = sum_last + jax.ops.segment_sum(last_terms, last_index, num_segments=P3)
        sum_proj = sum_proj + proj_grad.astype(jnp.float32)
        sum_out = sum_out + out_grad.astype(jnp.float32)
        return ((sum_first, sum_middle, sum_last, sum_proj, sum_out), layer_rows)
    start = (jnp.zeros((P1, D1 * RANK), jnp.float32), jnp.zeros((P2, RANK, D2 * RANK), jnp.float32), jnp.zeros((P3, RANK * D3), jnp.float32), jnp.zeros((D, 4 * D), jnp.float32), jnp.zeros((D, D), jnp.float32))
    totals, outputs = lax.scan(one_history, start, (digits_view, grads_view))
    grad_first, grad_middle, grad_last, grad_proj, grad_out = totals
    return (outputs.reshape(TOKENS, D), grad_first, grad_middle.reshape(P2 * RANK, D2 * RANK), grad_last, grad_proj, grad_out)
```

```python
import functools
import math

import jax
import jax.numpy as jnp
from jax import lax
from jax.experimental import pallas as pl
from jax.experimental.pallas import tpu as pltpu
from jax.sharding import PartitionSpec as P

AXES = ("dp", "cores")
BF = jnp.bfloat16
F32 = jnp.float32
I32 = jnp.int32
EVENTS = 512
OWNERS = 128
VMEM_LIMIT = 56 * 1024 * 1024


def iota(shape, dim):
    return lax.broadcasted_iota(I32, shape, dim)


def dot(a, b, ca=1, cb=0):
    return lax.dot_general(a, b, (((ca,), (cb,)), ((), ())), preferred_element_type=F32)


def bdot(a, b, ca, cb):
    return lax.dot_general(a, b, (((ca,), (cb,)), ((0,), (0,))), preferred_element_type=F32)


def half_turn(x):
    return pltpu.roll(x, 64, x.ndim - 1)


def low_lanes(shape):
    return iota(shape, len(shape) - 1) % 128 < 64


def one_hot(flag):
    return jnp.where(flag, 1.0, 0.0).astype(BF)


def prep_kernel(dig_ref, msg_ref, slot_row_ref, slot_col_ref):
    digits = dig_ref[...]
    padded = jnp.concatenate([digits, jnp.zeros((5, EVENTS), I32)], axis=0).astype(F32)
    cols = jnp.transpose(padded).astype(I32)
    owner_row = digits[1:2, :] >> 2
    owner_col = cols[:, 1:2] >> 2
    same = owner_row == owner_col
    sub = iota((EVENTS, EVENTS), 0)
    lane = iota((EVENTS, EVENTS), 1)
    rank_col = jnp.sum(jnp.where(same & (lane < sub), 1.0, 0.0), axis=1, keepdims=True).astype(I32)
    rank_row = jnp.sum(jnp.where(same & (sub < lane), 1.0, 0.0), axis=0, keepdims=True).astype(I32)
    slot_row_ref[...] = jnp.broadcast_to(rank_row * OWNERS + owner_row, (8, EVENTS))
    slot_col_ref[...] = jnp.broadcast_to(rank_col * OWNERS + owner_col, (EVENTS, 128))
    place = iota((EVENTS, 128), 1)
    inner = place % 32
    value = jnp.where(inner < 8, cols[:, 0:1], jnp.where(inner < 16, cols[:, 1:2], cols[:, 2:3])) + 1
    part = jnp.where(place < 32, value >> 4, value & 15)
    ok = (inner % 8 == rank_col) & (inner < 24) & (place < 64)
    table = jnp.where(ok, part, 0).astype(F32).astype(BF)
    pick = one_hot(iota((OWNERS, EVENTS), 0) == owner_row)
    sums = dot(pick, table)
    whole = sums * 16.0 + pltpu.roll(sums, 96, 1)
    msg_ref[...] = jnp.where(iota((OWNERS, 128), 1) < 24, whole, 0.0).astype(I32).reshape(OWNERS, 1, 128)


def prep(digits):
    return pl.pallas_call(
        prep_kernel,
        out_shape=(
            jax.ShapeDtypeStruct((OWNERS, 1, 128), I32),
            jax.ShapeDtypeStruct((8, EVENTS), I32),
            jax.ShapeDtypeStruct((EVENTS, 128), I32),
        ),
        compiler_params=pltpu.CompilerParams(vmem_limit_bytes=VMEM_LIMIT),
        name="prep",
    )(digits)


def index_columns(arrived, half):
    lane = iota((OWNERS, 128), 1)
    out = []
    for digit in range(3):
        parts = []
        for t in range(4):
            mine = lane == digit * 8 + half * 4 + t
            parts.append(jnp.sum(jnp.where(mine, arrived, 0).astype(F32), axis=1, keepdims=True))
        out.append(jnp.concatenate(parts, axis=0).astype(I32) - 1)
    return out


def slice_masks(middle_col):
    local = jnp.where(middle_col < 0, -1, middle_col & 3)
    group = iota((512, 128), 1) // 64
    return local == group, local == group + 2


def build_kernel(arrived_ref, first_ref, middle_ref, last_ref, built_ref, spread_ref, part_ref, lt_ref, fs, ps, ls):
    half = pl.program_id(0)
    arrived = arrived_ref[...].reshape(OWNERS, 128)
    first_col, middle_col, last_col = index_columns(arrived, half)
    low = low_lanes((128, 128))
    rows = dot(one_hot(first_col == iota((512, 2048), 1)), first_ref[...])
    mask0, mask1 = slice_masks(middle_col)
    for t in range(4):
        m0 = mask0[t * 128 : (t + 1) * 128]
        m1 = mask1[t * 128 : (t + 1) * 128]
        for pair in range(4):
            x = rows[t * 128 : (t + 1) * 128, pair * 128 : (pair + 1) * 128]
            turned = half_turn(x)
            for odd in range(2):
                both = jnp.where(low, turned, x) if odd else jnp.where(low, x, turned)
                at = pl.ds(t * 1024 + pair * 2 + odd, 128, stride=8)
                fs[0, at, :] = jnp.where(m0, both, 0.0)
                fs[1, at, :] = jnp.where(m1, both, 0.0)
    source = iota((512, 512), 0)
    perm = one_hot(iota((512, 512), 1) == (source % 8) * 64 + source // 8)
    rows = dot(one_hot(last_col == iota((512, 1024), 1)), last_ref[...]).astype(BF)
    rows = dot(rows, perm)
    for t in range(4):
        for pair in range(4):
            x = rows[t * 128 : (t + 1) * 128, pair * 128 : (pair + 1) * 128]
            turned = half_turn(x)
            for odd in range(2):
                both = jnp.where(low, turned, x) if odd else jnp.where(low, x, turned)
                keep = jnp.where(low, 0.0, both) if t % 2 else jnp.where(low, both, 0.0)
                ls[t // 2, pl.ds((t % 2) * 8 + pair * 2 + odd, 128, stride=16), :] = keep

    def spread_step(i, carry):
        at = pl.ds(pl.multiple_of(i * 512, 512), 512)
        spread_ref[at, 0:128] = fs[0, at, :].astype(BF)
        spread_ref[at, 128:256] = fs[1, at, :].astype(BF)
        ps[at, :] = dot(spread_ref[at, :], middle_ref[...])
        return carry

    lax.fori_loop(0, 8, spread_step, 0)

    group = 16
    low = low_lanes((group * 8, 128))

    def combine(i, carry):
        srcs = pl.ds(pl.multiple_of(i * group, group), group)
        for pair in range(4):
            lanes = slice(pair * 128, (pair + 1) * 128)
            v = [ps[pl.ds(pl.multiple_of(t * 1024 + i * group * 8, 8), group * 8), lanes] for t in range(4)]
            w = [half_turn(x) for x in v]
            for side in range(2):
                v0, v1 = v[2 * side], v[2 * side + 1]
                w0, w1 = w[2 * side], w[2 * side + 1]
                even = jnp.where(low, v0, w1).reshape(group, 8, 128)
                odd = jnp.where(low, w0, v1).reshape(group, 8, 128)
                part_ref[srcs, pair * 16 : (pair + 1) * 16, side * 128 : (side + 1) * 128] = jnp.concatenate(
                    [even, odd], axis=1
                ).astype(BF)
        wide = pl.ds(pl.multiple_of(i * group * 16, group * 16), group * 16)
        zero = jnp.zeros((group, 16, 128), BF)
        lt_ref[srcs, 0:16, 0:128] = ls[0, wide, :].reshape(group, 16, 128).astype(BF)
        lt_ref[srcs, 0:16, 128:256] = zero
        lt_ref[srcs, 16:32, 0:128] = zero
        lt_ref[srcs, 16:32, 128:256] = ls[1, wide, :].reshape(group, 16, 128).astype(BF)
        out = bdot(lt_ref[srcs], part_ref[srcs], 2, 2)
        tile = jnp.concatenate([out[:, 0:16, :], out[:, 16:32, :]], axis=2)
        built_ref[srcs, 0] = tile.astype(BF)
        return carry

    lax.fori_loop(0, OWNERS // group, combine, 0)


def build(arrived, first_core, middle_core, last_core):
    return pl.pallas_call(
        build_kernel,
        grid=(2,),
        in_specs=[
            pl.BlockSpec((OWNERS, 1, 128), lambda h: (0, 0, 0)),
            pl.BlockSpec((2048, 512), lambda h: (0, 0)),
            pl.BlockSpec((256, 512), lambda h: (0, 0)),
            pl.BlockSpec((1024, 512), lambda h: (0, 0)),
        ],
        out_specs=(
            pl.BlockSpec((OWNERS, 1, 16, 128), lambda h: (0, h, 0, 0)),
            pl.BlockSpec((4096, 256), lambda h: (h, 0)),
            pl.BlockSpec((OWNERS, 64, 256), lambda h: (h, 0, 0)),
            pl.BlockSpec((OWNERS, 32, 256), lambda h: (h, 0, 0)),
        ),
        out_shape=(
            jax.ShapeDtypeStruct((OWNERS, 2, 16, 128), BF),
            jax.ShapeDtypeStruct((8192, 256), BF),
            jax.ShapeDtypeStruct((2 * OWNERS, 64, 256), BF),
            jax.ShapeDtypeStruct((2 * OWNERS, 32, 256), BF),
        ),
        scratch_shapes=[
            pltpu.VMEM((2, 4096, 128), F32),
            pltpu.VMEM((4096, 512), F32),
            pltpu.VMEM((2, 2048, 128), F32),
        ],
        compiler_params=pltpu.CompilerParams(vmem_limit_bytes=VMEM_LIMIT),
        name="build",
    )(arrived, first_core, middle_core, last_core)


def sigmoid(x):
    return 1.0 / (1.0 + jnp.exp(-x))


def norm_stats(x):
    center = x - jnp.mean(x, axis=-1, keepdims=True)
    spread = jnp.mean(center * center, axis=-1, keepdims=True)
    scale = lax.rsqrt(spread + 1e-05)
    return center * scale, scale


def norm_grad(ct, y, scale):
    return scale * (ct - jnp.mean(ct, axis=-1, keepdims=True) - y * jnp.mean(ct * y, axis=-1, keepdims=True))


def layer_kernel(
    recv_ref, slot_row_ref, slot_col_ref, proj_ref, out_ref, grad_ref,
    rows_ref, sent_ref, dproj_ref, dout_ref,
    tiles, slots, emb, normed, y_in, z, act, mixed, y_mid, gated, dz, dmixed, work, sc_in, sc_mid,
):
    low = low_lanes((256 // 2, 128))
    step = 128

    def widen(i, carry):
        srcs = pl.ds(pl.multiple_of(i * 32, 32), 32)
        tiles[pl.ds(pl.multiple_of(i * 1024, 1024), 1024), :] = recv_ref[srcs].reshape(1024, 128).astype(F32)
        return carry

    lax.fori_loop(0, 4, widen, 0)
    for half in range(2):
        for tlo in range(2):
            for pair in range(4):
                base = half * 16 + tlo * 8 + pair * 2
                y0 = tiles[pl.ds(base, 128, stride=32), :]
                y1 = tiles[pl.ds(base + 1, 128, stride=32), :]
                lanes = slice(pair * 128, (pair + 1) * 128)
                k0 = half * 4 + tlo
                slots[k0 * 128 : (k0 + 1) * 128, lanes] = jnp.where(low, y0, half_turn(y1)).astype(BF)
                k1 = k0 + 2
                slots[k1 * 128 : (k1 + 1) * 128, lanes] = jnp.where(low, half_turn(y0), y1).astype(BF)
    source = iota((512, 512), 0)
    target = iota((512, 512), 1)
    flip = one_hot(target == (source % 8) * 64 + ((source // 8) % 8) * 8 + source // 64)
    pick = one_hot(slot_col_ref[:, 0:1] == iota((EVENTS, 1024), 1))
    emb[...] = dot(dot(pick, slots[...]).astype(BF), flip)

    def project(i, carry):
        at = pl.ds(pl.multiple_of(i * step, step), step)
        y, scale = norm_stats(emb[at, :])
        y_in[at, :] = y
        sc_in[at, :] = jnp.broadcast_to(scale, (step, 128))
        normed[at, :] = y.astype(BF)
        for block in range(4):
            lanes = slice(block * 512, (block + 1) * 512)
            value = dot(normed[at, :], proj_ref[:, lanes])
            z[at, lanes] = value
            act[at, lanes] = (value * sigmoid(value)).astype(BF)
        return carry

    lax.fori_loop(0, EVENTS // step, project, 0)
    scaling = 1.0 / math.sqrt(128.0)

    def scores_of(head, rows, base):
        q = act[rows, pl.ds(pl.multiple_of(1024 + head * 128, 128), 128)]
        k = act[:, pl.ds(pl.multiple_of(1536 + head * 128, 128), 128)]
        s = dot(q, k, 1, 1) * scaling
        causal = base + iota((step, EVENTS), 0) >= iota((step, EVENTS), 1)
        return s, causal

    def attend(j, carry):
        head = j // 4
        base = pl.multiple_of((j % 4) * step, step)
        rows = pl.ds(base, step)
        cols = pl.ds(pl.multiple_of(head * 128, 128), 128)
        s, causal = scores_of(head, rows, base)
        weights = jnp.where(causal, s * sigmoid(s), 0.0).astype(BF)
        v = act[:, pl.ds(pl.multiple_of(512 + head * 128, 128), 128)]
        mixed[rows, cols] = dot(weights, v)
        return carry

    lax.fori_loop(0, 16, attend, 0)

    def finish(i, carry):
        at = pl.ds(pl.multiple_of(i * step, step), step)
        y, scale = norm_stats(mixed[at, :])
        u = act[at, 0:512].astype(F32)
        gate = (y * u).astype(BF)
        gated[at, :] = gate
        g = grad_ref[at, :]
        rows_ref[at, :] = (dot(gate, out_ref[...]) + emb[at, :]).astype(BF)
        d_gate = dot(g, out_ref[...], 1, 1).astype(BF).astype(F32)
        d_u = (d_gate * y).astype(BF).astype(F32)
        zu = z[at, 0:512]
        sig = sigmoid(zu)
        dz[at, 0:512] = (d_u * (sig * (1.0 + zu * (1.0 - sig)))).astype(BF)
        dmixed[at, :] = norm_grad(d_gate * u, y, scale).astype(BF)
        return carry

    lax.fori_loop(0, EVENTS // step, finish, 0)
    dout_ref[...] = dot(gated[...], grad_ref[...], 0, 0).astype(BF)

    def attend_grad(head, carry):
        cols = pl.ds(pl.multiple_of(head * 128, 128), 128)
        vcols = pl.ds(pl.multiple_of(512 + head * 128, 128), 128)
        qcols = pl.ds(pl.multiple_of(1024 + head * 128, 128), 128)
        kcols = pl.ds(pl.multiple_of(1536 + head * 128, 128), 128)
        d_v = jnp.zeros((EVENTS, 128), F32)
        d_k = jnp.zeros((EVENTS, 128), F32)
        for block in range(4):
            base = block * step
            rows = slice(base, base + step)
            s, causal = scores_of(head, rows, base)
            sig = sigmoid(s)
            weights = jnp.where(causal, s * sig, 0.0).astype(BF)
            dm = dmixed[rows, cols]
            d_w = dot(dm, act[:, vcols], 1, 1).astype(BF).astype(F32)
            d_s = jnp.where(causal, d_w * (sig * (1.0 + s * (1.0 - sig))) * scaling, 0.0).astype(BF)
            d_v += dot(weights, dm, 0, 0)
            d_k += dot(d_s, act[rows, qcols], 0, 0)
            d_q = dot(d_s, act[:, kcols])
            work[rows, :] = d_q

        def through(ct, where):
            value = z[:, where]
            sig = sigmoid(value)
            dz[:, where] = (ct.astype(BF).astype(F32) * (sig * (1.0 + value * (1.0 - sig)))).astype(BF)

        through(work[...], qcols)
        through(d_v, vcols)
        through(d_k, kcols)
        return carry

    lax.fori_loop(0, 4, attend_grad, 0)

    for block in range(4):
        lanes = slice(block * 512, (block + 1) * 512)
        dproj_ref[:, lanes] = dot(normed[...], dz[:, lanes], 0, 0).astype(BF)

    back = one_hot(source == (target % 8) * 64 + ((target // 8) % 8) * 8 + target // 64)

    def close(i, carry):
        at = pl.ds(pl.multiple_of(i * step, step), step)
        d_normed = dot(dz[at, :], proj_ref[...], 1, 1).astype(BF).astype(F32)
        d_rows = norm_grad(d_normed, y_in[at, :], sc_in[at, 0:1]) + grad_ref[at, :].astype(F32)
        gated[at, :] = d_rows.astype(BF)
        return carry

    lax.fori_loop(0, EVENTS // step, close, 0)
    turned = dot(gated[...], back).astype(BF)
    for half in range(2):
        for tlo in range(2):
            found = []
            for thi in range(2):
                k = half * 4 + thi * 2 + tlo
                place = one_hot(iota((128, EVENTS), 0) + k * 128 == slot_row_ref[0:1, :])
                found.append(dot(place, turned))
            for pair in range(4):
                lanes = slice(pair * 128, (pair + 1) * 128)
                x0, x1 = found[0][:, lanes], found[1][:, lanes]
                base = half * 16 + tlo * 8 + pair * 2
                tiles[pl.ds(base, 128, stride=32), :] = jnp.where(low, x0, half_turn(x1))
                tiles[pl.ds(base + 1, 128, stride=32), :] = jnp.where(low, half_turn(x0), x1)

    def narrow(i, carry):
        srcs = pl.ds(pl.multiple_of(i * 32, 32), 32)
        sent_ref[srcs] = tiles[pl.ds(pl.multiple_of(i * 1024, 1024), 1024), :].astype(BF).reshape(32, 2, 16, 128)
        return carry

    lax.fori_loop(0, 4, narrow, 0)


def layer(recv, slot_row, slot_col, w_proj, w_out, layer_grad):
    vm = pltpu.VMEM
    return pl.pallas_call(
        layer_kernel,
        out_shape=(
            jax.ShapeDtypeStruct((EVENTS, 512), BF),
            jax.ShapeDtypeStruct((OWNERS, 2, 16, 128), BF),
            jax.ShapeDtypeStruct((512, 2048), BF),
            jax.ShapeDtypeStruct((512, 512), BF),
        ),
        scratch_shapes=[
            vm((4096, 128), F32),
            vm((1024, 512), BF),
            vm((EVENTS, 512), F32),
            vm((EVENTS, 512), BF),
            vm((EVENTS, 512), F32),
            vm((EVENTS, 2048), F32),
            vm((EVENTS, 2048), BF),
            vm((EVENTS, 512), F32),
            vm((EVENTS, 512), F32),
            vm((EVENTS, 512), BF),
            vm((EVENTS, 2048), BF),
            vm((EVENTS, 512), BF),
            vm((EVENTS, 128), F32),
            vm((EVENTS, 128), F32),
            vm((EVENTS, 128), F32),
        ],
        compiler_params=pltpu.CompilerParams(vmem_limit_bytes=VMEM_LIMIT),
        name="layer",
    )(recv, slot_row, slot_col, w_proj, w_out, layer_grad)


def core_grad_kernel(
    arrived_ref, tile_ref, spread_ref, part_ref, lt_ref, middle_ref,
    first_out, middle_out, last_out,
    flipped, pg, ls, ss, fterm, lterm, first_acc, last_acc,
):
    half = pl.program_id(0)
    arrived = arrived_ref[...].reshape(OWNERS, 128)
    flipped[...] = jnp.transpose(arrived.astype(F32)).astype(I32) - 1
    _, middle_col, _ = index_columns(arrived, half)
    mask0, mask1 = slice_masks(middle_col)
    group = 16
    low = low_lanes((group, 8, 128))
    own = (iota((group, 16, 128), 1) // 8) == (iota((group, 16, 128), 2) // 64)

    def events(i, carry):
        srcs = pl.ds(pl.multiple_of(i * group, group), group)
        tile = tile_ref[srcs, 0]
        g = jnp.concatenate([tile[:, :, 0:64], tile[:, :, 64:128]], axis=1)
        wide = pl.ds(pl.multiple_of(i * group * 16, group * 16), group * 16)
        terms = bdot(g, part_ref[srcs], 2, 1)
        for side in range(2):
            x = terms[:, side * 16 : (side + 1) * 16, side * 128 : (side + 1) * 128]
            x = jnp.where(own, x, 0.0).reshape(group * 16, 128)
            ls[side, wide, :] = x + half_turn(x)
        grads = bdot(g, lt_ref[srcs], 1, 1)
        for pair in range(4):
            lanes = slice(pair * 128, (pair + 1) * 128)
            for side in range(2):
                even = grads[:, pair * 16 : pair * 16 + 8, side * 128 : (side + 1) * 128]
                odd = grads[:, pair * 16 + 8 : pair * 16 + 16, side * 128 : (side + 1) * 128]
                v0 = jnp.where(low, even, half_turn(odd))
                v1 = jnp.where(low, half_turn(even), odd)
                for t, v in ((2 * side, v0), (2 * side + 1, v1)):
                    at = pl.ds(pl.multiple_of(t * 1024 + i * group * 8, group * 8), group * 8)
                    pg[at, lanes] = v.reshape(group * 8, 128).astype(BF)
        return carry

    lax.fori_loop(0, OWNERS // group, events, 0)
    low = low_lanes((128, 128))
    middle_part = jnp.zeros((256, 512), F32)
    for t in range(4):
        at = slice(t * 1024, (t + 1) * 1024)
        middle_part += dot(spread_ref[at, :], pg[at, :], 0, 0)
        back = dot(pg[at, :], middle_ref[...], 1, 1)
        ss[0] = back[:, 0:128]
        ss[1] = back[:, 128:256]
        rows = slice(t * 128, (t + 1) * 128)
        m0, m1 = mask0[rows], mask1[rows]
        for pair in range(4):
            lanes = slice(pair * 128, (pair + 1) * 128)
            found = []
            for odd in range(2):
                where = pl.ds(pair * 2 + odd, 128, stride=8)
                x = jnp.where(m0, ss[0, where, :], 0.0) + jnp.where(m1, ss[1, where, :], 0.0)
                found.append(x + half_turn(x))
            fterm[rows, lanes] = jnp.where(low, found[0], found[1]).astype(BF)
            base = (t % 2) * 8 + pair * 2
            y0 = ls[t // 2, pl.ds(base, 128, stride=16), :]
            y1 = ls[t // 2, pl.ds(base + 1, 128, stride=16), :]
            lterm[rows, lanes] = jnp.where(low, y0, y1).astype(BF)

    source = iota((512, 512), 0)
    perm = one_hot(iota((512, 512), 1) == (source % 64) * 8 + source // 64)
    lterm[...] = dot(lterm[...], perm).astype(BF)

    def index_row(digit):
        return jnp.concatenate([flipped[pl.ds(digit * 8 + half * 4 + t, 1), :] for t in range(4)], axis=1)

    first_row = index_row(0)
    last_row = index_row(2)

    @pl.when(half == 0)
    def _():
        middle_out[...] = middle_part
        first_acc[...] = jnp.zeros_like(first_acc)
        last_acc[...] = jnp.zeros_like(last_acc)

    @pl.when(half == 1)
    def _():
        middle_out[...] += middle_part

    def scatter_first(i, carry):
        at = pl.ds(pl.multiple_of(i * 256, 256), 256)
        place = one_hot(iota((256, 512), 0) + i * 256 == first_row)
        first_acc[at, :] += dot(place, fterm[...])
        return carry

    def scatter_last(i, carry):
        at = pl.ds(pl.multiple_of(i * 256, 256), 256)
        place = one_hot(iota((256, 512), 0) + i * 256 == last_row)
        last_acc[at, :] += dot(place, lterm[...])
        return carry

    lax.fori_loop(0, 8, scatter_first, 0)
    lax.fori_loop(0, 4, scatter_last, 0)

    @pl.when(half == 1)
    def _():
        first_out[...] = first_acc[...].astype(BF)
        last_out[...] = last_acc[...].astype(BF)


def core_grads(arrived, tiles, spread, part, lt, middle_core):
    vm = pltpu.VMEM
    return pl.pallas_call(
        core_grad_kernel,
        grid=(2,),
        in_specs=[
            pl.BlockSpec((OWNERS, 1, 128), lambda h: (0, 0, 0)),
            pl.BlockSpec((OWNERS, 1, 16, 128), lambda h: (0, h, 0, 0)),
            pl.BlockSpec((4096, 256), lambda h: (h, 0)),
            pl.BlockSpec((OWNERS, 64, 256), lambda h: (h, 0, 0)),
            pl.BlockSpec((OWNERS, 32, 256), lambda h: (h, 0, 0)),
            pl.BlockSpec((256, 512), lambda h: (0, 0)),
        ],
        out_specs=(
            pl.BlockSpec((2048, 512), lambda h: (0, 0)),
            pl.BlockSpec((256, 512), lambda h: (0, 0)),
            pl.BlockSpec((1024, 512), lambda h: (0, 0)),
        ),
        out_shape=(
            jax.ShapeDtypeStruct((2048, 512), BF),
            jax.ShapeDtypeStruct((256, 512), F32),
            jax.ShapeDtypeStruct((1024, 512), BF),
        ),
        scratch_shapes=[
            vm((128, 128), I32),
            vm((4096, 512), BF),
            vm((2, 2048, 128), F32),
            vm((2, 1024, 128), F32),
            vm((512, 512), BF),
            vm((512, 512), BF),
            vm((2048, 512), F32),
            vm((1024, 512), F32),
        ],
        compiler_params=pltpu.CompilerParams(vmem_limit_bytes=VMEM_LIMIT),
        name="core_grads",
    )(arrived, tiles, spread, part, lt, middle_core)


def exchange(x):
    return lax.all_to_all(x, AXES, split_axis=0, concat_axis=0, tiled=True)


def per_device(item_digits, first_core, middle_core, last_core, w_proj, w_out, layer_grad):
    message, slot_row, slot_col = prep(item_digits)
    arrived = exchange(message)
    built, spread, part, lt = build(arrived, first_core, middle_core, last_core)
    recv = exchange(built)
    layer_rows, sent, proj_grad, out_grad = layer(recv, slot_row, slot_col, w_proj, w_out, layer_grad)
    tiles = exchange(sent)
    first_part, grad_middle, last_part = core_grads(arrived, tiles, spread, part, lt, middle_core)
    grad_first, grad_last, proj_total, out_total = lax.psum(
        tuple(x.astype(F32) for x in (first_part, last_part, proj_grad, out_grad)), AXES
    )
    return (layer_rows, grad_first, grad_middle, grad_last, proj_total, out_total)


def solution(mesh):
    return jax.shard_map(
        per_device,
        mesh=mesh,
        in_specs=(
            P(None, AXES),
            P(),
            P(AXES, None),
            P(),
            P(),
            P(),
            P(AXES, None),
        ),
        out_specs=(P(AXES, None), P(), P(AXES, None), P(), P(), P()),
        check_vma=False,
    )
```

```python
import functools
import math

import jax
import jax.numpy as jnp
from jax import lax
from jax.experimental import pallas as pl
from jax.experimental.pallas import tpu as pltpu
from jax.sharding import PartitionSpec as P

AXES = ("dp", "cores")
BF = jnp.bfloat16
F32 = jnp.float32
I32 = jnp.int32
EVENTS = 512
OWNERS = 128
VMEM_LIMIT = 56 * 1024 * 1024
MESH = pl.DeviceIdType.MESH


def iota(shape, dim):
    return lax.broadcasted_iota(I32, shape, dim)


def dot(a, b, ca=1, cb=0):
    return lax.dot_general(a, b, (((ca,), (cb,)), ((), ())), preferred_element_type=F32)


def bdot(a, b, ca, cb):
    return lax.dot_general(a, b, (((ca,), (cb,)), ((0,), (0,))), preferred_element_type=F32)


def half_turn(x):
    return pltpu.roll(x, 64, x.ndim - 1)


def low_lanes(shape):
    return iota(shape, len(shape) - 1) % 128 < 64


def one_hot(flag):
    return jnp.where(flag, 1.0, 0.0).astype(BF)


def prep_kernel(dig_ref, arrived_ref, slot_row_ref, slot_col_ref, message, stage, send_sem, recv_sem):
    dp = lax.axis_index("dp")
    cores = lax.axis_index("cores")
    barrier = pltpu.get_barrier_semaphore()
    row_mates = [(lax.rem(cores + i, 8), (dp, lax.rem(cores + i, 8))) for i in range(1, 8)]
    column_mates = [(lax.rem(dp + i, 16), (lax.rem(dp + i, 16), cores)) for i in range(1, 16)]
    for _, who in row_mates + column_mates:
        pl.semaphore_signal(barrier, inc=1, device_id=who, device_id_type=MESH)
    digits = dig_ref[...]
    padded = jnp.concatenate([digits, jnp.zeros((5, EVENTS), I32)], axis=0).astype(F32)
    cols = jnp.transpose(padded).astype(I32)
    owner_row = digits[1:2, :] >> 2
    owner_col = cols[:, 1:2] >> 2
    same = owner_row == owner_col
    sub = iota((EVENTS, EVENTS), 0)
    lane = iota((EVENTS, EVENTS), 1)
    rank_col = jnp.sum(jnp.where(same & (lane < sub), 1.0, 0.0), axis=1, keepdims=True).astype(I32)
    rank_row = jnp.sum(jnp.where(same & (sub < lane), 1.0, 0.0), axis=0, keepdims=True).astype(I32)
    slot_row_ref[...] = jnp.broadcast_to(rank_row * OWNERS + owner_row, (8, EVENTS))
    slot_col_ref[...] = jnp.broadcast_to(rank_col * OWNERS + owner_col, (EVENTS, 128))
    place = iota((EVENTS, 128), 1)
    inner = place % 32
    value = jnp.where(inner < 8, cols[:, 0:1], jnp.where(inner < 16, cols[:, 1:2], cols[:, 2:3])) + 1
    part = jnp.where(place < 32, value >> 4, value & 15)
    ok = (inner % 8 == rank_col) & (inner < 24) & (place < 64)
    table = jnp.where(ok, part, 0).astype(F32).astype(BF)
    pick = one_hot(iota((OWNERS, EVENTS), 0) == (owner_row & 7) * 16 + (owner_row >> 3))
    sums = dot(pick, table)
    whole = sums * 16.0 + pltpu.roll(sums, 96, 1)
    whole = jnp.where(iota((OWNERS, 128), 1) < 24, whole, 0.0).astype(I32)
    message[...] = whole.reshape(8, 16, 1, 128)
    pl.semaphore_wait(barrier, 22)

    def start(number, src, dst, who):
        copy = pltpu.make_async_remote_copy(
            src_ref=src,
            dst_ref=dst,
            send_sem=send_sem.at[number],
            recv_sem=recv_sem.at[number],
            device_id=who,
            device_id_type=MESH,
        )
        copy.start()
        return copy

    first = [start(n, message.at[c], stage.at[cores], who) for n, (c, who) in enumerate(row_mates)]
    stage[cores] = message[cores]
    for copy in first:
        copy.wait_recv()
    second = [
        start(7 + n, stage.at[:, d], arrived_ref.at[dp], who) for n, (d, who) in enumerate(column_mates)
    ]
    arrived_ref[dp] = stage[:, dp]
    for copy in second:
        copy.wait_recv()
    for copy in first + second:
        copy.wait_send()


def prep(digits):
    return pl.pallas_call(
        prep_kernel,
        out_shape=(
            jax.ShapeDtypeStruct((16, 8, 1, 128), I32),
            jax.ShapeDtypeStruct((8, EVENTS), I32),
            jax.ShapeDtypeStruct((EVENTS, 128), I32),
        ),
        scratch_shapes=[
            pltpu.VMEM((8, 16, 1, 128), I32),
            pltpu.VMEM((8, 16, 1, 128), I32),
            pltpu.SemaphoreType.DMA((22,)),
            pltpu.SemaphoreType.DMA((22,)),
        ],
        compiler_params=pltpu.CompilerParams(
            collective_id=1, has_side_effects=True, vmem_limit_bytes=VMEM_LIMIT
        ),
        name="prep",
    )(digits)


def index_columns(arrived, half):
    lane = iota((OWNERS, 128), 1)
    out = []
    for digit in range(3):
        parts = []
        for t in range(4):
            mine = lane == digit * 8 + half * 4 + t
            parts.append(jnp.sum(jnp.where(mine, arrived, 0).astype(F32), axis=1, keepdims=True))
        out.append(jnp.concatenate(parts, axis=0).astype(I32) - 1)
    return out


def slice_masks(middle_col):
    local = jnp.where(middle_col < 0, -1, middle_col & 3)
    group = iota((512, 128), 1) // 64
    return local == group, local == group + 2


def build_kernel(arrived_ref, first_ref, middle_ref, last_ref, built_ref, spread_ref, part_ref, lt_ref, fs, ps, ls):
    half = pl.program_id(0)
    arrived = arrived_ref[...].reshape(OWNERS, 128)
    first_col, middle_col, last_col = index_columns(arrived, half)
    low = low_lanes((128, 128))
    rows = dot(one_hot(first_col == iota((512, 2048), 1)), first_ref[...])
    mask0, mask1 = slice_masks(middle_col)
    for t in range(4):
        m0 = mask0[t * 128 : (t + 1) * 128]
        m1 = mask1[t * 128 : (t + 1) * 128]
        for pair in range(4):
            x = rows[t * 128 : (t + 1) * 128, pair * 128 : (pair + 1) * 128]
            turned = half_turn(x)
            for odd in range(2):
                both = jnp.where(low, turned, x) if odd else jnp.where(low, x, turned)
                at = pl.ds(t * 1024 + pair * 2 + odd, 128, stride=8)
                fs[0, at, :] = jnp.where(m0, both, 0.0)
                fs[1, at, :] = jnp.where(m1, both, 0.0)
    source = iota((512, 512), 0)
    perm = one_hot(iota((512, 512), 1) == (source % 8) * 64 + source // 8)
    rows = dot(one_hot(last_col == iota((512, 1024), 1)), last_ref[...]).astype(BF)
    rows = dot(rows, perm)
    for t in range(4):
        for pair in range(4):
            x = rows[t * 128 : (t + 1) * 128, pair * 128 : (pair + 1) * 128]
            turned = half_turn(x)
            for odd in range(2):
                both = jnp.where(low, turned, x) if odd else jnp.where(low, x, turned)
                keep = jnp.where(low, 0.0, both) if t % 2 else jnp.where(low, both, 0.0)
                ls[t // 2, pl.ds((t % 2) * 8 + pair * 2 + odd, 128, stride=16), :] = keep

    def spread_step(i, carry):
        at = pl.ds(pl.multiple_of(i * 512, 512), 512)
        spread_ref[at, 0:128] = fs[0, at, :].astype(BF)
        spread_ref[at, 128:256] = fs[1, at, :].astype(BF)
        ps[at, :] = dot(spread_ref[at, :], middle_ref[...])
        return carry

    lax.fori_loop(0, 8, spread_step, 0)

    group = 16
    low = low_lanes((group * 8, 128))

    def combine(i, carry):
        srcs = pl.ds(pl.multiple_of(i * group, group), group)
        for pair in range(4):
            lanes = slice(pair * 128, (pair + 1) * 128)
            v = [ps[pl.ds(pl.multiple_of(t * 1024 + i * group * 8, 8), group * 8), lanes] for t in range(4)]
            w = [half_turn(x) for x in v]
            for side in range(2):
                v0, v1 = v[2 * side], v[2 * side + 1]
                w0, w1 = w[2 * side], w[2 * side + 1]
                even = jnp.where(low, v0, w1).reshape(group, 8, 128)
                odd = jnp.where(low, w0, v1).reshape(group, 8, 128)
                part_ref[srcs, pair * 16 : (pair + 1) * 16, side * 128 : (side + 1) * 128] = jnp.concatenate(
                    [even, odd], axis=1
                ).astype(BF)
        wide = pl.ds(pl.multiple_of(i * group * 16, group * 16), group * 16)
        zero = jnp.zeros((group, 16, 128), BF)
        lt_ref[srcs, 0:16, 0:128] = ls[0, wide, :].reshape(group, 16, 128).astype(BF)
        lt_ref[srcs, 0:16, 128:256] = zero
        lt_ref[srcs, 16:32, 0:128] = zero
        lt_ref[srcs, 16:32, 128:256] = ls[1, wide, :].reshape(group, 16, 128).astype(BF)
        out = bdot(lt_ref[srcs], part_ref[srcs], 2, 2)
        tile = jnp.concatenate([out[:, 0:16, :], out[:, 16:32, :]], axis=2)
        built_ref[srcs, 0] = tile.astype(BF)
        return carry

    lax.fori_loop(0, OWNERS // group, combine, 0)


def build(arrived, first_core, middle_core, last_core):
    return pl.pallas_call(
        build_kernel,
        grid=(2,),
        in_specs=[
            pl.BlockSpec((OWNERS, 1, 128), lambda h: (0, 0, 0)),
            pl.BlockSpec((2048, 512), lambda h: (0, 0)),
            pl.BlockSpec((256, 512), lambda h: (0, 0)),
            pl.BlockSpec((1024, 512), lambda h: (0, 0)),
        ],
        out_specs=(
            pl.BlockSpec((OWNERS, 1, 16, 128), lambda h: (0, h, 0, 0)),
            pl.BlockSpec((4096, 256), lambda h: (h, 0)),
            pl.BlockSpec((OWNERS, 64, 256), lambda h: (h, 0, 0)),
            pl.BlockSpec((OWNERS, 32, 256), lambda h: (h, 0, 0)),
        ),
        out_shape=(
            jax.ShapeDtypeStruct((OWNERS, 2, 16, 128), BF),
            jax.ShapeDtypeStruct((8192, 256), BF),
            jax.ShapeDtypeStruct((2 * OWNERS, 64, 256), BF),
            jax.ShapeDtypeStruct((2 * OWNERS, 32, 256), BF),
        ),
        scratch_shapes=[
            pltpu.VMEM((2, 4096, 128), F32),
            pltpu.VMEM((4096, 512), F32),
            pltpu.VMEM((2, 2048, 128), F32),
        ],
        compiler_params=pltpu.CompilerParams(vmem_limit_bytes=VMEM_LIMIT),
        name="build",
    )(arrived, first_core, middle_core, last_core)


def sigmoid(x):
    return 1.0 / (1.0 + jnp.exp(-x))


def norm_stats(x):
    center = x - jnp.mean(x, axis=-1, keepdims=True)
    spread = jnp.mean(center * center, axis=-1, keepdims=True)
    scale = lax.rsqrt(spread + 1e-05)
    return center * scale, scale


def norm_grad(ct, y, scale):
    return scale * (ct - jnp.mean(ct, axis=-1, keepdims=True) - y * jnp.mean(ct * y, axis=-1, keepdims=True))


def layer_kernel(
    recv_ref, slot_row_ref, slot_col_ref, proj_ref, out_ref, grad_ref,
    rows_ref, sent_ref, dproj_ref, dout_ref,
    tiles, slots, emb, normed, y_in, z, act, mixed, y_mid, gated, dz, dmixed, work, sc_in, sc_mid,
):
    low = low_lanes((256 // 2, 128))
    step = 128

    def widen(i, carry):
        srcs = pl.ds(pl.multiple_of(i * 32, 32), 32)
        tiles[pl.ds(pl.multiple_of(i * 1024, 1024), 1024), :] = recv_ref[srcs].reshape(1024, 128).astype(F32)
        return carry

    lax.fori_loop(0, 4, widen, 0)
    for half in range(2):
        for tlo in range(2):
            for pair in range(4):
                base = half * 16 + tlo * 8 + pair * 2
                y0 = tiles[pl.ds(base, 128, stride=32), :]
                y1 = tiles[pl.ds(base + 1, 128, stride=32), :]
                lanes = slice(pair * 128, (pair + 1) * 128)
                k0 = half * 4 + tlo
                slots[k0 * 128 : (k0 + 1) * 128, lanes] = jnp.where(low, y0, half_turn(y1)).astype(BF)
                k1 = k0 + 2
                slots[k1 * 128 : (k1 + 1) * 128, lanes] = jnp.where(low, half_turn(y0), y1).astype(BF)
    source = iota((512, 512), 0)
    target = iota((512, 512), 1)
    flip = one_hot(target == (source % 8) * 64 + ((source // 8) % 8) * 8 + source // 64)
    pick = one_hot(slot_col_ref[:, 0:1] == iota((EVENTS, 1024), 1))
    emb[...] = dot(dot(pick, slots[...]).astype(BF), flip)

    def project(i, carry):
        at = pl.ds(pl.multiple_of(i * step, step), step)
        y, scale = norm_stats(emb[at, :])
        y_in[at, :] = y
        sc_in[at, :] = jnp.broadcast_to(scale, (step, 128))
        normed[at, :] = y.astype(BF)
        for block in range(4):
            lanes = slice(block * 512, (block + 1) * 512)
            value = dot(normed[at, :], proj_ref[:, lanes])
            z[at, lanes] = value
            act[at, lanes] = (value * sigmoid(value)).astype(BF)
        return carry

    lax.fori_loop(0, EVENTS // step, project, 0)
    scaling = 1.0 / math.sqrt(128.0)

    def scores_of(head, rows, base):
        q = act[rows, pl.ds(pl.multiple_of(1024 + head * 128, 128), 128)]
        k = act[:, pl.ds(pl.multiple_of(1536 + head * 128, 128), 128)]
        s = dot(q, k, 1, 1) * scaling
        causal = base + iota((step, EVENTS), 0) >= iota((step, EVENTS), 1)
        return s, causal

    def attend(j, carry):
        head = j // 4
        base = pl.multiple_of((j % 4) * step, step)
        rows = pl.ds(base, step)
        cols = pl.ds(pl.multiple_of(head * 128, 128), 128)
        s, causal = scores_of(head, rows, base)
        weights = jnp.where(causal, s * sigmoid(s), 0.0).astype(BF)
        v = act[:, pl.ds(pl.multiple_of(512 + head * 128, 128), 128)]
        mixed[rows, cols] = dot(weights, v)
        return carry

    lax.fori_loop(0, 16, attend, 0)

    def finish(i, carry):
        at = pl.ds(pl.multiple_of(i * step, step), step)
        y, scale = norm_stats(mixed[at, :])
        u = act[at, 0:512].astype(F32)
        gate = (y * u).astype(BF)
        gated[at, :] = gate
        g = grad_ref[at, :]
        rows_ref[at, :] = (dot(gate, out_ref[...]) + emb[at, :]).astype(BF)
        d_gate = dot(g, out_ref[...], 1, 1).astype(BF).astype(F32)
        d_u = (d_gate * y).astype(BF).astype(F32)
        zu = z[at, 0:512]
        sig = sigmoid(zu)
        dz[at, 0:512] = (d_u * (sig * (1.0 + zu * (1.0 - sig)))).astype(BF)
        dmixed[at, :] = norm_grad(d_gate * u, y, scale).astype(BF)
        return carry

    lax.fori_loop(0, EVENTS // step, finish, 0)
    dout_ref[...] = dot(gated[...], grad_ref[...], 0, 0).astype(BF)

    def attend_grad(head, carry):
        cols = pl.ds(pl.multiple_of(head * 128, 128), 128)
        vcols = pl.ds(pl.multiple_of(512 + head * 128, 128), 128)
        qcols = pl.ds(pl.multiple_of(1024 + head * 128, 128), 128)
        kcols = pl.ds(pl.multiple_of(1536 + head * 128, 128), 128)
        d_v = jnp.zeros((EVENTS, 128), F32)
        d_k = jnp.zeros((EVENTS, 128), F32)
        for block in range(4):
            base = block * step
            rows = slice(base, base + step)
            s, causal = scores_of(head, rows, base)
            sig = sigmoid(s)
            weights = jnp.where(causal, s * sig, 0.0).astype(BF)
            dm = dmixed[rows, cols]
            d_w = dot(dm, act[:, vcols], 1, 1).astype(BF).astype(F32)
            d_s = jnp.where(causal, d_w * (sig * (1.0 + s * (1.0 - sig))) * scaling, 0.0).astype(BF)
            d_v += dot(weights, dm, 0, 0)
            d_k += dot(d_s, act[rows, qcols], 0, 0)
            d_q = dot(d_s, act[:, kcols])
            work[rows, :] = d_q

        def through(ct, where):
            value = z[:, where]
            sig = sigmoid(value)
            dz[:, where] = (ct.astype(BF).astype(F32) * (sig * (1.0 + value * (1.0 - sig)))).astype(BF)

        through(work[...], qcols)
        through(d_v, vcols)
        through(d_k, kcols)
        return carry

    lax.fori_loop(0, 4, attend_grad, 0)

    for block in range(4):
        lanes = slice(block * 512, (block + 1) * 512)
        dproj_ref[lanes, :] = dot(normed[...], dz[:, lanes], 0, 0).astype(BF)

    back = one_hot(source == (target % 8) * 64 + ((target // 8) % 8) * 8 + target // 64)

    def close(i, carry):
        at = pl.ds(pl.multiple_of(i * step, step), step)
        d_normed = dot(dz[at, :], proj_ref[...], 1, 1).astype(BF).astype(F32)
        d_rows = norm_grad(d_normed, y_in[at, :], sc_in[at, 0:1]) + grad_ref[at, :].astype(F32)
        gated[at, :] = d_rows.astype(BF)
        return carry

    lax.fori_loop(0, EVENTS // step, close, 0)
    turned = dot(gated[...], back).astype(BF)
    for half in range(2):
        for tlo in range(2):
            found = []
            for thi in range(2):
                k = half * 4 + thi * 2 + tlo
                place = one_hot(iota((128, EVENTS), 0) + k * 128 == slot_row_ref[0:1, :])
                found.append(dot(place, turned))
            for pair in range(4):
                lanes = slice(pair * 128, (pair + 1) * 128)
                x0, x1 = found[0][:, lanes], found[1][:, lanes]
                base = half * 16 + tlo * 8 + pair * 2
                tiles[pl.ds(base, 128, stride=32), :] = jnp.where(low, x0, half_turn(x1))
                tiles[pl.ds(base + 1, 128, stride=32), :] = jnp.where(low, half_turn(x0), x1)

    def narrow(i, carry):
        srcs = pl.ds(pl.multiple_of(i * 32, 32), 32)
        sent_ref[srcs] = tiles[pl.ds(pl.multiple_of(i * 1024, 1024), 1024), :].astype(BF).reshape(32, 2, 16, 128)
        return carry

    lax.fori_loop(0, 4, narrow, 0)


def layer(recv, slot_row, slot_col, w_proj, w_out, layer_grad):
    vm = pltpu.VMEM
    return pl.pallas_call(
        layer_kernel,
        out_shape=(
            jax.ShapeDtypeStruct((EVENTS, 512), BF),
            jax.ShapeDtypeStruct((OWNERS, 2, 16, 128), BF),
            jax.ShapeDtypeStruct((2048, 512), BF),
            jax.ShapeDtypeStruct((512, 512), BF),
        ),
        scratch_shapes=[
            vm((4096, 128), F32),
            vm((1024, 512), BF),
            vm((EVENTS, 512), F32),
            vm((EVENTS, 512), BF),
            vm((EVENTS, 512), F32),
            vm((EVENTS, 2048), F32),
            vm((EVENTS, 2048), BF),
            vm((EVENTS, 512), F32),
            vm((EVENTS, 512), F32),
            vm((EVENTS, 512), BF),
            vm((EVENTS, 2048), BF),
            vm((EVENTS, 512), BF),
            vm((EVENTS, 128), F32),
            vm((EVENTS, 128), F32),
            vm((EVENTS, 128), F32),
        ],
        compiler_params=pltpu.CompilerParams(vmem_limit_bytes=VMEM_LIMIT),
        name="layer",
    )(recv, slot_row, slot_col, w_proj, w_out, layer_grad)


def core_grad_kernel(
    arrived_ref, tile_ref, spread_ref, part_ref, lt_ref, middle_ref,
    first_out, middle_out, last_out,
    flipped, pg, ls, ss, fterm, lterm, first_acc, last_acc,
):
    half = pl.program_id(0)
    arrived = arrived_ref[...].reshape(OWNERS, 128)
    flipped[...] = jnp.transpose(arrived.astype(F32)).astype(I32) - 1
    _, middle_col, _ = index_columns(arrived, half)
    mask0, mask1 = slice_masks(middle_col)
    group = 16
    low = low_lanes((group, 8, 128))
    own = (iota((group, 16, 128), 1) // 8) == (iota((group, 16, 128), 2) // 64)

    def events(i, carry):
        srcs = pl.ds(pl.multiple_of(i * group, group), group)
        tile = tile_ref[srcs, 0]
        g = jnp.concatenate([tile[:, :, 0:64], tile[:, :, 64:128]], axis=1)
        wide = pl.ds(pl.multiple_of(i * group * 16, group * 16), group * 16)
        terms = bdot(g, part_ref[srcs], 2, 1)
        for side in range(2):
            x = terms[:, side * 16 : (side + 1) * 16, side * 128 : (side + 1) * 128]
            x = jnp.where(own, x, 0.0).reshape(group * 16, 128)
            ls[side, wide, :] = x + half_turn(x)
        grads = bdot(g, lt_ref[srcs], 1, 1)
        for pair in range(4):
            lanes = slice(pair * 128, (pair + 1) * 128)
            for side in range(2):
                even = grads[:, pair * 16 : pair * 16 + 8, side * 128 : (side + 1) * 128]
                odd = grads[:, pair * 16 + 8 : pair * 16 + 16, side * 128 : (side + 1) * 128]
                v0 = jnp.where(low, even, half_turn(odd))
                v1 = jnp.where(low, half_turn(even), odd)
                for t, v in ((2 * side, v0), (2 * side + 1, v1)):
                    at = pl.ds(pl.multiple_of(t * 1024 + i * group * 8, group * 8), group * 8)
                    pg[at, lanes] = v.reshape(group * 8, 128).astype(BF)
        return carry

    lax.fori_loop(0, OWNERS // group, events, 0)
    low = low_lanes((128, 128))
    middle_part = jnp.zeros((256, 512), F32)
    for t in range(4):
        at = slice(t * 1024, (t + 1) * 1024)
        middle_part += dot(spread_ref[at, :], pg[at, :], 0, 0)
        back = dot(pg[at, :], middle_ref[...], 1, 1)
        ss[0] = back[:, 0:128]
        ss[1] = back[:, 128:256]
        rows = slice(t * 128, (t + 1) * 128)
        m0, m1 = mask0[rows], mask1[rows]
        for pair in range(4):
            lanes = slice(pair * 128, (pair + 1) * 128)
            found = []
            for odd in range(2):
                where = pl.ds(pair * 2 + odd, 128, stride=8)
                x = jnp.where(m0, ss[0, where, :], 0.0) + jnp.where(m1, ss[1, where, :], 0.0)
                found.append(x + half_turn(x))
            fterm[rows, lanes] = jnp.where(low, found[0], found[1]).astype(BF)
            base = (t % 2) * 8 + pair * 2
            y0 = ls[t // 2, pl.ds(base, 128, stride=16), :]
            y1 = ls[t // 2, pl.ds(base + 1, 128, stride=16), :]
            lterm[rows, lanes] = jnp.where(low, y0, y1).astype(BF)

    source = iota((512, 512), 0)
    perm = one_hot(iota((512, 512), 1) == (source % 64) * 8 + source // 64)
    lterm[...] = dot(lterm[...], perm).astype(BF)

    def index_row(digit):
        return jnp.concatenate([flipped[pl.ds(digit * 8 + half * 4 + t, 1), :] for t in range(4)], axis=1)

    first_row = index_row(0)
    last_row = index_row(2)

    @pl.when(half == 0)
    def _():
        middle_out[...] = middle_part
        first_acc[...] = jnp.zeros_like(first_acc)
        last_acc[...] = jnp.zeros_like(last_acc)

    @pl.when(half == 1)
    def _():
        middle_out[...] += middle_part

    def scatter_first(i, carry):
        at = pl.ds(pl.multiple_of(i * 256, 256), 256)
        place = one_hot(iota((256, 512), 0) + i * 256 == first_row)
        first_acc[at, :] += dot(place, fterm[...])
        return carry

    def scatter_last(i, carry):
        at = pl.ds(pl.multiple_of(i * 256, 256), 256)
        place = one_hot(iota((256, 512), 0) + i * 256 == last_row)
        last_acc[at, :] += dot(place, lterm[...])
        return carry

    lax.fori_loop(0, 8, scatter_first, 0)
    lax.fori_loop(0, 4, scatter_last, 0)

    @pl.when(half == 1)
    def _():
        first_out[...] = first_acc[...].astype(BF)
        last_out[...] = last_acc[...].astype(BF)


def core_grads(arrived, tiles, spread, part, lt, middle_core):
    vm = pltpu.VMEM
    return pl.pallas_call(
        core_grad_kernel,
        grid=(2,),
        in_specs=[
            pl.BlockSpec((OWNERS, 1, 128), lambda h: (0, 0, 0)),
            pl.BlockSpec((OWNERS, 1, 16, 128), lambda h: (0, h, 0, 0)),
            pl.BlockSpec((4096, 256), lambda h: (h, 0)),
            pl.BlockSpec((OWNERS, 64, 256), lambda h: (h, 0, 0)),
            pl.BlockSpec((OWNERS, 32, 256), lambda h: (h, 0, 0)),
            pl.BlockSpec((256, 512), lambda h: (0, 0)),
        ],
        out_specs=(
            pl.BlockSpec((2048, 512), lambda h: (0, 0)),
            pl.BlockSpec((256, 512), lambda h: (0, 0)),
            pl.BlockSpec((1024, 512), lambda h: (0, 0)),
        ),
        out_shape=(
            jax.ShapeDtypeStruct((2048, 512), BF),
            jax.ShapeDtypeStruct((256, 512), F32),
            jax.ShapeDtypeStruct((1024, 512), BF),
        ),
        scratch_shapes=[
            vm((128, 128), I32),
            vm((4096, 512), BF),
            vm((2, 2048, 128), F32),
            vm((2, 1024, 128), F32),
            vm((512, 512), BF),
            vm((512, 512), BF),
            vm((2048, 512), F32),
            vm((1024, 512), F32),
        ],
        compiler_params=pltpu.CompilerParams(vmem_limit_bytes=VMEM_LIMIT),
        name="core_grads",
    )(arrived, tiles, spread, part, lt, middle_core)


class Place:
    def __init__(self):
        dp = lax.axis_index("dp")
        cores = lax.axis_index("cores")
        self.at = (cores // 2, dp // 4, lax.rem(dp, 4))
        self.core = lax.rem(cores, 2)

    def along(self, dim, offset):
        at = list(self.at)
        at[dim] = lax.rem(at[dim] + offset, 4)
        return at[dim], (at[1] * 4 + at[2], at[0] * 2 + self.core)

    def sibling(self):
        x, y, z = self.at
        return (y * 4 + z, x * 2 + 1 - self.core)


ORDERS = ((0, 1, 2), (1, 2, 0), (2, 0, 1))
SIZES = (256, 64, 16)


def reduce_kernel(
    first_ref, proj_ref, last_ref, out_ref,
    total0, total1, total2,
    rest, pair0, pair1, pair2, sum0, sum1, sum2,
    got00, got01, got02, got10, got11, got12, got20, got21, got22, send_sem, recv_sem,
):
    place = Place()
    core = place.core
    barrier = pltpu.get_barrier_semaphore()
    partners = [place.sibling()] + [place.along(d, o)[1] for d in range(3) for o in (1, 2, 3)]
    for who in partners:
        pl.semaphore_signal(barrier, inc=1, device_id=who, device_id_type=MESH)
    for block in range(12):
        row = (block // 3) * 512
        lanes = slice((block % 3) * 128, (block % 3 + 1) * 128)
        if block < 8:
            value = last_ref[(block // 4) * 512 : (block // 4 + 1) * 512, (block % 4) * 128 : (block % 4 + 1) * 128]
        else:
            value = out_ref[:, (block % 4) * 128 : (block % 4 + 1) * 128]
        rest[row : row + 512, lanes] = value
    source = (first_ref, proj_ref, rest)
    total = (total0, total1, total2)
    pair = (pair0, pair1, pair2)
    sums = (sum0, sum1, sum2)
    got = ((got00, got01, got02), (got10, got11, got12), (got20, got21, got22))
    pl.semaphore_wait(barrier, len(partners))
    pending = []

    def start(part, stage, slot, src, dst, who):
        copy = pltpu.make_async_remote_copy(
            src_ref=src,
            dst_ref=dst,
            send_sem=send_sem.at[part, stage, slot],
            recv_sem=recv_sem.at[part, stage, slot],
            device_id=who,
            device_id_type=MESH,
        )
        copy.start()
        pending.append(copy)
        return copy

    def rows(start_row, size):
        return pl.ds(pl.multiple_of(start_row, 16), size)

    base = [core * 1024 for _ in range(3)]
    flight = {}
    for slot in (1, 2, 3, 0):
        for part in range(3):
            quarter, _ = place.along(ORDERS[part][0], slot)
            flight[part, slot] = start(
                part, 0, slot,
                source[part].at[rows((1 - core) * 1024 + quarter * 256, 256)],
                pair[part].at[rows(quarter * 256, 256)],
                place.sibling(),
            )
    moving = {}
    for slot in (1, 2, 3, 0):
        for part in range(3):
            quarter, who = place.along(ORDERS[part][0], slot)
            flight[part, slot].wait_recv()
            at = rows(quarter * 256, 256)
            mine = source[part][rows(core * 1024 + quarter * 256, 256), :].astype(F32)
            sums[part][at, :] = (mine + pair[part][at, :].astype(F32)).astype(BF)
            if slot:
                moving[part, slot] = start(part, 1, slot, sums[part].at[at], got[part][0].at[slot - 1], who)
    offset = [0, 0, 0]
    for level in range(3):
        size = SIZES[level]
        following = {}
        for part in range(3):
            mine = place.at[ORDERS[part][level]]
            offset[part] = offset[part] + mine * size
            for slot in (1, 2, 3):
                moving[part, slot].wait_recv()
            at = rows(offset[part], size)
            value = sums[part][at, :].astype(F32)
            for slot in range(3):
                value = value + got[part][level][slot].astype(F32)
            if level < 2:
                sums[part][at, :] = value.astype(BF)
                for slot in (1, 2, 3):
                    quarter, who = place.along(ORDERS[part][level + 1], slot)
                    src = sums[part].at[rows(offset[part] + quarter * SIZES[level + 1], SIZES[level + 1])]
                    following[part, slot] = start(part, level + 2, slot, src, got[part][level + 1].at[slot - 1], who)
            else:
                where = rows(core * 1024 + offset[part], size)
                total[part][where, :] = value.astype(BF)
                for slot in (1, 2, 3):
                    who = place.along(ORDERS[part][2], slot)[1]
                    ref = total[part].at[where]
                    following[part, slot] = start(part, 4, slot, ref, ref, who)
        moving = following
    final = []
    for level in (1, 0):
        following = {}
        for part in range(3):
            mine = place.at[ORDERS[part][level + 1]]
            offset[part] = offset[part] - mine * SIZES[level + 1]
            for slot in (1, 2, 3):
                moving[part, slot].wait_recv()
            where = rows(core * 1024 + offset[part], SIZES[level])
            ref = total[part].at[where]
            for slot in (1, 2, 3):
                who = place.along(ORDERS[part][level], slot)[1]
                following[part, slot] = start(part, 6 - level, slot - 0, ref, ref, who)
            if level == 0:
                final.append(start(part, 7, 0, ref, ref, place.sibling()))
        moving = following
    for slot in (1, 3, 2):
        for part in range(3):
            moving[part, slot].wait_recv()
            quarter = place.along(ORDERS[part][0], 4 - slot)[0]
            ref = total[part].at[rows(core * 1024 + quarter * 256, 256)]
            final.append(start(part, 7, slot, ref, ref, place.sibling()))
    for copy in final:
        copy.wait_recv()
    for copy in pending:
        copy.wait_send()


def reduce_all(first_part, proj_grad, last_part, out_grad, ident):
    vm = pltpu.VMEM
    widths = (512, 512, 384)
    return pl.pallas_call(
        reduce_kernel,
        out_shape=tuple(jax.ShapeDtypeStruct((2048, w), BF) for w in widths),
        in_specs=[pl.BlockSpec(memory_space=vm)] * 4,
        out_specs=tuple(pl.BlockSpec(memory_space=vm) for _ in widths),
        scratch_shapes=[vm((2048, 384), BF)]
        + [vm((1024, w), BF) for w in widths]
        + [vm((1024, w), BF) for w in widths]
        + [vm((3, size, w), BF) for w in widths for size in SIZES]
        + [pltpu.SemaphoreType.DMA((3, 8, 4))] * 2,
        compiler_params=pltpu.CompilerParams(
            collective_id=ident, has_side_effects=True, vmem_limit_bytes=VMEM_LIMIT
        ),
        name="reduce_all",
    )(first_part, proj_grad, last_part, out_grad)


def widen_kernel(a_ref, b_ref, c_ref, first_ref, last_ref, proj_ref, out_ref):
    step = pl.program_id(0)
    first_ref[...] = a_ref[...].astype(F32)
    proj_ref[...] = b_ref[...].astype(F32)
    block0 = step * 3
    for k in range(3):
        block = block0 + k
        value = c_ref[:, k * 128 : (k + 1) * 128].astype(F32)
        for lane in range(4):

            @pl.when((block < 8) & (block % 4 == lane))
            def _():
                last_ref[pl.ds(pl.multiple_of((block // 4) * 512, 512), 512), lane * 128 : (lane + 1) * 128] = value

            @pl.when((block >= 8) & (block % 4 == lane))
            def _():
                out_ref[:, lane * 128 : (lane + 1) * 128] = value


def widen(a, b, c):
    return pl.pallas_call(
        widen_kernel,
        grid=(4,),
        in_specs=[pl.BlockSpec((512, w), lambda i: (i, 0)) for w in (512, 512, 384)],
        out_specs=(
            pl.BlockSpec((512, 512), lambda i: (i, 0)),
            pl.BlockSpec((1024, 512), lambda i: (0, 0)),
            pl.BlockSpec((512, 512), lambda i: (0, i)),
            pl.BlockSpec((512, 512), lambda i: (0, 0)),
        ),
        out_shape=(
            jax.ShapeDtypeStruct((2048, 512), F32),
            jax.ShapeDtypeStruct((1024, 512), F32),
            jax.ShapeDtypeStruct((512, 2048), F32),
            jax.ShapeDtypeStruct((512, 512), F32),
        ),
        compiler_params=pltpu.CompilerParams(vmem_limit_bytes=VMEM_LIMIT),
        name="widen",
    )(a, b, c)


def exchange(x):
    return lax.all_to_all(x, AXES, split_axis=0, concat_axis=0, tiled=True)


def per_device(item_digits, first_core, middle_core, last_core, w_proj, w_out, layer_grad):
    arrived, slot_row, slot_col = prep(item_digits)
    arrived = arrived.reshape(OWNERS, 1, 128)
    built, spread, part, lt = build(arrived, first_core, middle_core, last_core)
    recv = exchange(built)
    layer_rows, sent, proj_grad, out_grad = layer(recv, slot_row, slot_col, w_proj, w_out, layer_grad)
    tiles = exchange(sent)
    first_part, grad_middle, last_part = core_grads(arrived, tiles, spread, part, lt, middle_core)
    totals = reduce_all(first_part, proj_grad, last_part, out_grad, 2)
    grad_first, grad_last, proj_total, out_total = widen(*totals)
    return (layer_rows, grad_first, grad_middle, grad_last, proj_total, out_total)


def solution(mesh):
    return jax.shard_map(
        per_device,
        mesh=mesh,
        in_specs=(
            P(None, AXES),
            P(),
            P(AXES, None),
            P(),
            P(),
            P(),
            P(AXES, None),
        ),
        out_specs=(P(AXES, None), P(), P(AXES, None), P(), P(), P()),
        check_vma=False,
    )
```

```python
import functools
import math

import jax
import jax.numpy as jnp
from jax import lax
from jax.experimental import pallas as pl
from jax.experimental.pallas import tpu as pltpu
from jax.sharding import PartitionSpec as P

AXES = ("dp", "cores")
BF = jnp.bfloat16
F32 = jnp.float32
I32 = jnp.int32
EVENTS = 512
OWNERS = 128
VMEM_LIMIT = 56 * 1024 * 1024
MESH = pl.DeviceIdType.MESH


def iota(shape, dim):
    return lax.broadcasted_iota(I32, shape, dim)


def dot(a, b, ca=1, cb=0):
    return lax.dot_general(a, b, (((ca,), (cb,)), ((), ())), preferred_element_type=F32)


def bdot(a, b, ca, cb):
    return lax.dot_general(a, b, (((ca,), (cb,)), ((0,), (0,))), preferred_element_type=F32)


def half_turn(x):
    return pltpu.roll(x, 64, x.ndim - 1)


def low_lanes(shape):
    return iota(shape, len(shape) - 1) % 128 < 64


def one_hot(flag):
    return jnp.where(flag, 1.0, 0.0).astype(BF)


def prep_kernel(dig_ref, arrived_ref, slot_row_ref, slot_col_ref, message, stage, send_sem, recv_sem):
    dp = lax.axis_index("dp")
    cores = lax.axis_index("cores")
    barrier = pltpu.get_barrier_semaphore()
    row_mates = [(lax.rem(cores + i, 8), (dp, lax.rem(cores + i, 8))) for i in range(1, 8)]
    column_mates = [(lax.rem(dp + i, 16), (lax.rem(dp + i, 16), cores)) for i in range(1, 16)]
    for _, who in row_mates + column_mates:
        pl.semaphore_signal(barrier, inc=1, device_id=who, device_id_type=MESH)
    digits = dig_ref[...]
    padded = jnp.concatenate([digits, jnp.zeros((5, EVENTS), I32)], axis=0).astype(F32)
    cols = jnp.transpose(padded).astype(I32)
    owner_row = digits[1:2, :] >> 2
    owner_col = cols[:, 1:2] >> 2
    same = owner_row == owner_col
    sub = iota((EVENTS, EVENTS), 0)
    lane = iota((EVENTS, EVENTS), 1)
    rank_col = jnp.sum(jnp.where(same & (lane < sub), 1.0, 0.0), axis=1, keepdims=True).astype(I32)
    rank_row = jnp.sum(jnp.where(same & (sub < lane), 1.0, 0.0), axis=0, keepdims=True).astype(I32)
    slot_row_ref[...] = jnp.broadcast_to(rank_row * OWNERS + owner_row, (8, EVENTS))
    slot_col_ref[...] = jnp.broadcast_to(rank_col * OWNERS + owner_col, (EVENTS, 128))
    place = iota((EVENTS, 128), 1)
    inner = place % 32
    value = jnp.where(inner < 8, cols[:, 0:1], jnp.where(inner < 16, cols[:, 1:2], cols[:, 2:3])) + 1
    part = jnp.where(place < 32, value >> 4, value & 15)
    ok = (inner % 8 == rank_col) & (inner < 24) & (place < 64)
    table = jnp.where(ok, part, 0).astype(F32).astype(BF)
    pick = one_hot(iota((OWNERS, EVENTS), 0) == (owner_row & 7) * 16 + (owner_row >> 3))
    sums = dot(pick, table)
    whole = sums * 16.0 + pltpu.roll(sums, 96, 1)
    whole = jnp.where(iota((OWNERS, 128), 1) < 24, whole, 0.0).astype(I32)
    message[...] = whole.reshape(8, 16, 1, 128)
    pl.semaphore_wait(barrier, 22)

    def start(number, src, dst, who):
        copy = pltpu.make_async_remote_copy(
            src_ref=src,
            dst_ref=dst,
            send_sem=send_sem.at[number],
            recv_sem=recv_sem.at[number],
            device_id=who,
            device_id_type=MESH,
        )
        copy.start()
        return copy

    first = [start(n, message.at[c], stage.at[cores], who) for n, (c, who) in enumerate(row_mates)]
    stage[cores] = message[cores]
    for copy in first:
        copy.wait_recv()
    second = [
        start(7 + n, stage.at[:, d], arrived_ref.at[dp], who) for n, (d, who) in enumerate(column_mates)
    ]
    arrived_ref[dp] = stage[:, dp]
    for copy in second:
        copy.wait_recv()
    for copy in first + second:
        copy.wait_send()


def prep(digits):
    return pl.pallas_call(
        prep_kernel,
        out_shape=(
            jax.ShapeDtypeStruct((16, 8, 1, 128), I32),
            jax.ShapeDtypeStruct((8, EVENTS), I32),
            jax.ShapeDtypeStruct((EVENTS, 128), I32),
        ),
        scratch_shapes=[
            pltpu.VMEM((8, 16, 1, 128), I32),
            pltpu.VMEM((8, 16, 1, 128), I32),
            pltpu.SemaphoreType.DMA((22,)),
            pltpu.SemaphoreType.DMA((22,)),
        ],
        compiler_params=pltpu.CompilerParams(
            collective_id=1, has_side_effects=True, vmem_limit_bytes=VMEM_LIMIT
        ),
        name="prep",
    )(digits)


def index_columns(arrived, half):
    lane = iota((OWNERS, 128), 1)
    out = []
    for digit in range(3):
        parts = []
        for t in range(4):
            mine = lane == digit * 8 + half * 4 + t
            parts.append(jnp.sum(jnp.where(mine, arrived, 0).astype(F32), axis=1, keepdims=True))
        out.append(jnp.concatenate(parts, axis=0).astype(I32) - 1)
    return out


def slice_masks(middle_col):
    local = jnp.where(middle_col < 0, -1, middle_col & 3)
    group = iota((512, 128), 1) // 64
    return local == group, local == group + 2


def build_kernel(arrived_ref, first_ref, middle_ref, last_ref, built_ref, spread_ref, part_ref, lt_ref, fs, ps, ls):
    half = pl.program_id(0)
    arrived = arrived_ref[...].reshape(OWNERS, 128)
    first_col, middle_col, last_col = index_columns(arrived, half)
    low = low_lanes((128, 128))
    rows = dot(one_hot(first_col == iota((512, 2048), 1)), first_ref[...])
    mask0, mask1 = slice_masks(middle_col)
    for t in range(4):
        m0 = mask0[t * 128 : (t + 1) * 128]
        m1 = mask1[t * 128 : (t + 1) * 128]
        for pair in range(4):
            x = rows[t * 128 : (t + 1) * 128, pair * 128 : (pair + 1) * 128]
            turned = half_turn(x)
            for odd in range(2):
                both = jnp.where(low, turned, x) if odd else jnp.where(low, x, turned)
                at = pl.ds(t * 1024 + pair * 2 + odd, 128, stride=8)
                fs[0, at, :] = jnp.where(m0, both, 0.0)
                fs[1, at, :] = jnp.where(m1, both, 0.0)
    source = iota((512, 512), 0)
    perm = one_hot(iota((512, 512), 1) == (source % 8) * 64 + source // 8)
    rows = dot(one_hot(last_col == iota((512, 1024), 1)), last_ref[...]).astype(BF)
    rows = dot(rows, perm)
    for t in range(4):
        for pair in range(4):
            x = rows[t * 128 : (t + 1) * 128, pair * 128 : (pair + 1) * 128]
            turned = half_turn(x)
            for odd in range(2):
                both = jnp.where(low, turned, x) if odd else jnp.where(low, x, turned)
                keep = jnp.where(low, 0.0, both) if t % 2 else jnp.where(low, both, 0.0)
                ls[t // 2, pl.ds((t % 2) * 8 + pair * 2 + odd, 128, stride=16), :] = keep

    def spread_step(i, carry):
        at = pl.ds(pl.multiple_of(i * 512, 512), 512)
        spread_ref[at, 0:128] = fs[0, at, :].astype(BF)
        spread_ref[at, 128:256] = fs[1, at, :].astype(BF)
        ps[at, :] = dot(spread_ref[at, :], middle_ref[...])
        return carry

    lax.fori_loop(0, 8, spread_step, 0)

    group = 16
    low = low_lanes((group * 8, 128))

    def combine(i, carry):
        srcs = pl.ds(pl.multiple_of(i * group, group), group)
        for pair in range(4):
            lanes = slice(pair * 128, (pair + 1) * 128)
            v = [ps[pl.ds(pl.multiple_of(t * 1024 + i * group * 8, 8), group * 8), lanes] for t in range(4)]
            w = [half_turn(x) for x in v]
            for side in range(2):
                v0, v1 = v[2 * side], v[2 * side + 1]
                w0, w1 = w[2 * side], w[2 * side + 1]
                even = jnp.where(low, v0, w1).reshape(group, 8, 128)
                odd = jnp.where(low, w0, v1).reshape(group, 8, 128)
                part_ref[srcs, pair * 16 : (pair + 1) * 16, side * 128 : (side + 1) * 128] = jnp.concatenate(
                    [even, odd], axis=1
                ).astype(BF)
        wide = pl.ds(pl.multiple_of(i * group * 16, group * 16), group * 16)
        zero = jnp.zeros((group, 16, 128), BF)
        lt_ref[srcs, 0:16, 0:128] = ls[0, wide, :].reshape(group, 16, 128).astype(BF)
        lt_ref[srcs, 0:16, 128:256] = zero
        lt_ref[srcs, 16:32, 0:128] = zero
        lt_ref[srcs, 16:32, 128:256] = ls[1, wide, :].reshape(group, 16, 128).astype(BF)
        out = bdot(lt_ref[srcs], part_ref[srcs], 2, 2)
        tile = jnp.concatenate([out[:, 0:16, :], out[:, 16:32, :]], axis=2)
        built_ref[srcs, 0] = tile.astype(BF)
        return carry

    lax.fori_loop(0, OWNERS // group, combine, 0)


def build(arrived, first_core, middle_core, last_core):
    return pl.pallas_call(
        build_kernel,
        grid=(2,),
        in_specs=[
            pl.BlockSpec((OWNERS, 1, 128), lambda h: (0, 0, 0)),
            pl.BlockSpec((2048, 512), lambda h: (0, 0)),
            pl.BlockSpec((256, 512), lambda h: (0, 0)),
            pl.BlockSpec((1024, 512), lambda h: (0, 0)),
        ],
        out_specs=(
            pl.BlockSpec((OWNERS, 1, 16, 128), lambda h: (0, h, 0, 0)),
            pl.BlockSpec((4096, 256), lambda h: (h, 0)),
            pl.BlockSpec((OWNERS, 64, 256), lambda h: (h, 0, 0)),
            pl.BlockSpec((OWNERS, 32, 256), lambda h: (h, 0, 0)),
        ),
        out_shape=(
            jax.ShapeDtypeStruct((OWNERS, 2, 16, 128), BF),
            jax.ShapeDtypeStruct((8192, 256), BF),
            jax.ShapeDtypeStruct((2 * OWNERS, 64, 256), BF),
            jax.ShapeDtypeStruct((2 * OWNERS, 32, 256), BF),
        ),
        scratch_shapes=[
            pltpu.VMEM((2, 4096, 128), F32),
            pltpu.VMEM((4096, 512), F32),
            pltpu.VMEM((2, 2048, 128), F32),
        ],
        compiler_params=pltpu.CompilerParams(vmem_limit_bytes=VMEM_LIMIT),
        name="build",
    )(arrived, first_core, middle_core, last_core)


def sigmoid(x):
    return 0.5 * jnp.tanh(0.5 * x) + 0.5


def norm_stats(x):
    center = x - jnp.mean(x, axis=-1, keepdims=True)
    spread = jnp.mean(center * center, axis=-1, keepdims=True)
    scale = lax.rsqrt(spread + 1e-05)
    return center * scale, scale


def norm_grad(ct, y, scale):
    return scale * (ct - jnp.mean(ct, axis=-1, keepdims=True) - y * jnp.mean(ct * y, axis=-1, keepdims=True))


def layer_kernel(
    recv_ref, slot_row_ref, slot_col_ref, proj_ref, out_ref, grad_ref,
    rows_ref, sent_ref, dproj_ref, dout_ref,
    tiles, slots, emb, normed, y_in, z, act, mixed, y_mid, gated, dz, dmixed, work, work_v, work_k, sc_in,
):
    low = low_lanes((256 // 2, 128))
    step = 128

    def widen(i, carry):
        srcs = pl.ds(pl.multiple_of(i * 32, 32), 32)
        tiles[pl.ds(pl.multiple_of(i * 1024, 1024), 1024), :] = recv_ref[srcs].reshape(1024, 128).astype(F32)
        return carry

    lax.fori_loop(0, 4, widen, 0)
    for half in range(2):
        for tlo in range(2):
            for pair in range(4):
                base = half * 16 + tlo * 8 + pair * 2
                y0 = tiles[pl.ds(base, 128, stride=32), :]
                y1 = tiles[pl.ds(base + 1, 128, stride=32), :]
                lanes = slice(pair * 128, (pair + 1) * 128)
                k0 = half * 4 + tlo
                slots[k0 * 128 : (k0 + 1) * 128, lanes] = jnp.where(low, y0, half_turn(y1)).astype(BF)
                k1 = k0 + 2
                slots[k1 * 128 : (k1 + 1) * 128, lanes] = jnp.where(low, half_turn(y0), y1).astype(BF)
    source = iota((512, 512), 0)
    target = iota((512, 512), 1)
    flip = one_hot(target == (source % 8) * 64 + ((source // 8) % 8) * 8 + source // 64)
    pick = one_hot(slot_col_ref[:, 0:1] == iota((EVENTS, 1024), 1))
    emb[...] = dot(dot(pick, slots[...]).astype(BF), flip)

    def project(i, carry):
        at = pl.ds(pl.multiple_of(i * step, step), step)
        y, scale = norm_stats(emb[at, :])
        y_in[at, :] = y
        sc_in[at, :] = jnp.broadcast_to(scale, (step, 128))
        normed[at, :] = y.astype(BF)
        for block in range(4):
            lanes = slice(block * 512, (block + 1) * 512)
            value = dot(normed[at, :], proj_ref[:, lanes])
            z[at, lanes] = value
            act[at, lanes] = (value * sigmoid(value)).astype(BF)
        return carry

    lax.fori_loop(0, EVENTS // step, project, 0)
    scaling = 1.0 / math.sqrt(128.0)

    def scores_of(head, block):
        end = (block + 1) * step
        q = act[block * step : end, pl.ds(pl.multiple_of(1024 + head * 128, 128), 128)]
        k = act[0:end, pl.ds(pl.multiple_of(1536 + head * 128, 128), 128)]
        s = dot(q, k, 1, 1) * scaling
        causal = block * step + iota((step, end), 0) >= iota((step, end), 1)
        return s, causal

    def attend(head, carry):
        cols = pl.ds(pl.multiple_of(head * 128, 128), 128)
        for block in range(4):
            end = (block + 1) * step
            s, causal = scores_of(head, block)
            weights = jnp.where(causal, s * sigmoid(s), 0.0).astype(BF)
            v = act[0:end, pl.ds(pl.multiple_of(512 + head * 128, 128), 128)]
            mixed[block * step : end, cols] = dot(weights, v)
        return carry

    lax.fori_loop(0, 4, attend, 0)

    def finish(i, carry):
        at = pl.ds(pl.multiple_of(i * step, step), step)
        y, scale = norm_stats(mixed[at, :])
        u = act[at, 0:512].astype(F32)
        gate = (y * u).astype(BF)
        gated[at, :] = gate
        g = grad_ref[at, :]
        rows_ref[at, :] = (dot(gate, out_ref[...]) + emb[at, :]).astype(BF)
        d_gate = dot(g, out_ref[...], 1, 1).astype(BF).astype(F32)
        d_u = (d_gate * y).astype(BF).astype(F32)
        zu = z[at, 0:512]
        sig = sigmoid(zu)
        dz[at, 0:512] = (d_u * (sig * (1.0 + zu * (1.0 - sig)))).astype(BF)
        dmixed[at, :] = norm_grad(d_gate * u, y, scale).astype(BF)
        return carry

    lax.fori_loop(0, EVENTS // step, finish, 0)
    dout_ref[...] = dot(gated[...], grad_ref[...], 0, 0).astype(BF)

    def attend_grad(head, carry):
        cols = pl.ds(pl.multiple_of(head * 128, 128), 128)
        vcols = pl.ds(pl.multiple_of(512 + head * 128, 128), 128)
        qcols = pl.ds(pl.multiple_of(1024 + head * 128, 128), 128)
        kcols = pl.ds(pl.multiple_of(1536 + head * 128, 128), 128)
        for block in (3, 2, 1, 0):
            end = (block + 1) * step
            rows = slice(block * step, end)
            s, causal = scores_of(head, block)
            sig = sigmoid(s)
            weights = jnp.where(causal, s * sig, 0.0).astype(BF)
            dm = dmixed[rows, cols]
            d_w = dot(dm, act[0:end, vcols], 1, 1).astype(BF).astype(F32)
            d_s = jnp.where(causal, d_w * (sig * (1.0 + s * (1.0 - sig))) * scaling, 0.0).astype(BF)
            v_part = dot(weights, dm, 0, 0)
            k_part = dot(d_s, act[rows, qcols], 0, 0)
            if block == 3:
                work_v[...] = v_part
                work_k[...] = k_part
            else:
                work_v[0:end, :] += v_part
                work_k[0:end, :] += k_part
            work[rows, :] = dot(d_s, act[0:end, kcols])

        def through(ct, where):
            value = z[:, where]
            sig = sigmoid(value)
            dz[:, where] = (ct.astype(BF).astype(F32) * (sig * (1.0 + value * (1.0 - sig)))).astype(BF)

        through(work[...], qcols)
        through(work_v[...], vcols)
        through(work_k[...], kcols)
        return carry

    lax.fori_loop(0, 4, attend_grad, 0)

    for block in range(4):
        lanes = slice(block * 512, (block + 1) * 512)
        dproj_ref[lanes, :] = dot(normed[...], dz[:, lanes], 0, 0).astype(BF)

    back = one_hot(source == (target % 8) * 64 + ((target // 8) % 8) * 8 + target // 64)

    def close(i, carry):
        at = pl.ds(pl.multiple_of(i * step, step), step)
        d_normed = dot(dz[at, :], proj_ref[...], 1, 1).astype(BF).astype(F32)
        d_rows = norm_grad(d_normed, y_in[at, :], sc_in[at, 0:1]) + grad_ref[at, :].astype(F32)
        gated[at, :] = d_rows.astype(BF)
        return carry

    lax.fori_loop(0, EVENTS // step, close, 0)
    turned = dot(gated[...], back).astype(BF)
    for half in range(2):
        for tlo in range(2):
            found = []
            for thi in range(2):
                k = half * 4 + thi * 2 + tlo
                place = one_hot(iota((128, EVENTS), 0) + k * 128 == slot_row_ref[0:1, :])
                found.append(dot(place, turned))
            for pair in range(4):
                lanes = slice(pair * 128, (pair + 1) * 128)
                x0, x1 = found[0][:, lanes], found[1][:, lanes]
                base = half * 16 + tlo * 8 + pair * 2
                tiles[pl.ds(base, 128, stride=32), :] = jnp.where(low, x0, half_turn(x1))
                tiles[pl.ds(base + 1, 128, stride=32), :] = jnp.where(low, half_turn(x0), x1)

    def narrow(i, carry):
        srcs = pl.ds(pl.multiple_of(i * 32, 32), 32)
        sent_ref[srcs] = tiles[pl.ds(pl.multiple_of(i * 1024, 1024), 1024), :].astype(BF).reshape(32, 2, 16, 128)
        return carry

    lax.fori_loop(0, 4, narrow, 0)


def layer(recv, slot_row, slot_col, w_proj, w_out, layer_grad):
    vm = pltpu.VMEM
    return pl.pallas_call(
        layer_kernel,
        out_shape=(
            jax.ShapeDtypeStruct((EVENTS, 512), BF),
            jax.ShapeDtypeStruct((OWNERS, 2, 16, 128), BF),
            jax.ShapeDtypeStruct((2048, 512), BF),
            jax.ShapeDtypeStruct((512, 512), BF),
        ),
        scratch_shapes=[
            vm((4096, 128), F32),
            vm((1024, 512), BF),
            vm((EVENTS, 512), F32),
            vm((EVENTS, 512), BF),
            vm((EVENTS, 512), F32),
            vm((EVENTS, 2048), F32),
            vm((EVENTS, 2048), BF),
            vm((EVENTS, 512), F32),
            vm((EVENTS, 512), F32),
            vm((EVENTS, 512), BF),
            vm((EVENTS, 2048), BF),
            vm((EVENTS, 512), BF),
            vm((EVENTS, 128), F32),
            vm((EVENTS, 128), F32),
            vm((EVENTS, 128), F32),
            vm((EVENTS, 128), F32),
        ],
        compiler_params=pltpu.CompilerParams(vmem_limit_bytes=VMEM_LIMIT),
        name="layer",
    )(recv, slot_row, slot_col, w_proj, w_out, layer_grad)


def core_grad_kernel(
    arrived_ref, tile_ref, spread_ref, part_ref, lt_ref, middle_ref,
    first_out, middle_out, last_out,
    flipped, pg, ls, ss, fterm, lterm, first_acc, last_acc,
):
    half = pl.program_id(0)
    arrived = arrived_ref[...].reshape(OWNERS, 128)
    flipped[...] = jnp.transpose(arrived.astype(F32)).astype(I32) - 1
    _, middle_col, _ = index_columns(arrived, half)
    mask0, mask1 = slice_masks(middle_col)
    group = 16
    low = low_lanes((group, 8, 128))
    own = (iota((group, 16, 128), 1) // 8) == (iota((group, 16, 128), 2) // 64)

    def events(i, carry):
        srcs = pl.ds(pl.multiple_of(i * group, group), group)
        tile = tile_ref[srcs, 0]
        g = jnp.concatenate([tile[:, :, 0:64], tile[:, :, 64:128]], axis=1)
        wide = pl.ds(pl.multiple_of(i * group * 16, group * 16), group * 16)
        terms = bdot(g, part_ref[srcs], 2, 1)
        for side in range(2):
            x = terms[:, side * 16 : (side + 1) * 16, side * 128 : (side + 1) * 128]
            x = jnp.where(own, x, 0.0).reshape(group * 16, 128)
            ls[side, wide, :] = x + half_turn(x)
        grads = bdot(g, lt_ref[srcs], 1, 1)
        for pair in range(4):
            lanes = slice(pair * 128, (pair + 1) * 128)
            for side in range(2):
                even = grads[:, pair * 16 : pair * 16 + 8, side * 128 : (side + 1) * 128]
                odd = grads[:, pair * 16 + 8 : pair * 16 + 16, side * 128 : (side + 1) * 128]
                v0 = jnp.where(low, even, half_turn(odd))
                v1 = jnp.where(low, half_turn(even), odd)
                for t, v in ((2 * side, v0), (2 * side + 1, v1)):
                    at = pl.ds(pl.multiple_of(t * 1024 + i * group * 8, group * 8), group * 8)
                    pg[at, lanes] = v.reshape(group * 8, 128).astype(BF)
        return carry

    lax.fori_loop(0, OWNERS // group, events, 0)
    low = low_lanes((128, 128))
    middle_part = jnp.zeros((256, 512), F32)
    for t in range(4):
        at = slice(t * 1024, (t + 1) * 1024)
        middle_part += dot(spread_ref[at, :], pg[at, :], 0, 0)
        back = dot(pg[at, :], middle_ref[...], 1, 1)
        ss[0] = back[:, 0:128]
        ss[1] = back[:, 128:256]
        rows = slice(t * 128, (t + 1) * 128)
        m0, m1 = mask0[rows], mask1[rows]
        for pair in range(4):
            lanes = slice(pair * 128, (pair + 1) * 128)
            found = []
            for odd in range(2):
                where = pl.ds(pair * 2 + odd, 128, stride=8)
                x = jnp.where(m0, ss[0, where, :], 0.0) + jnp.where(m1, ss[1, where, :], 0.0)
                found.append(x + half_turn(x))
            fterm[rows, lanes] = jnp.where(low, found[0], found[1]).astype(BF)
            base = (t % 2) * 8 + pair * 2
            y0 = ls[t // 2, pl.ds(base, 128, stride=16), :]
            y1 = ls[t // 2, pl.ds(base + 1, 128, stride=16), :]
            lterm[rows, lanes] = jnp.where(low, y0, y1).astype(BF)

    source = iota((512, 512), 0)
    perm = one_hot(iota((512, 512), 1) == (source % 64) * 8 + source // 64)
    lterm[...] = dot(lterm[...], perm).astype(BF)

    def index_row(digit):
        return jnp.concatenate([flipped[pl.ds(digit * 8 + half * 4 + t, 1), :] for t in range(4)], axis=1)

    first_row = index_row(0)
    last_row = index_row(2)

    @pl.when(half == 0)
    def _():
        middle_out[...] = middle_part
        first_acc[...] = jnp.zeros_like(first_acc)
        last_acc[...] = jnp.zeros_like(last_acc)

    @pl.when(half == 1)
    def _():
        middle_out[...] += middle_part

    def scatter_first(i, carry):
        at = pl.ds(pl.multiple_of(i * 256, 256), 256)
        place = one_hot(iota((256, 512), 0) + i * 256 == first_row)
        first_acc[at, :] += dot(place, fterm[...])
        return carry

    def scatter_last(i, carry):
        at = pl.ds(pl.multiple_of(i * 256, 256), 256)
        place = one_hot(iota((256, 512), 0) + i * 256 == last_row)
        last_acc[at, :] += dot(place, lterm[...])
        return carry

    lax.fori_loop(0, 8, scatter_first, 0)
    lax.fori_loop(0, 4, scatter_last, 0)

    @pl.when(half == 1)
    def _():
        first_out[...] = first_acc[...].astype(BF)
        last_out[...] = last_acc[...].astype(BF)


def core_grads(arrived, tiles, spread, part, lt, middle_core):
    vm = pltpu.VMEM
    return pl.pallas_call(
        core_grad_kernel,
        grid=(2,),
        in_specs=[
            pl.BlockSpec((OWNERS, 1, 128), lambda h: (0, 0, 0)),
            pl.BlockSpec((OWNERS, 1, 16, 128), lambda h: (0, h, 0, 0)),
            pl.BlockSpec((4096, 256), lambda h: (h, 0)),
            pl.BlockSpec((OWNERS, 64, 256), lambda h: (h, 0, 0)),
            pl.BlockSpec((OWNERS, 32, 256), lambda h: (h, 0, 0)),
            pl.BlockSpec((256, 512), lambda h: (0, 0)),
        ],
        out_specs=(
            pl.BlockSpec((2048, 512), lambda h: (0, 0)),
            pl.BlockSpec((256, 512), lambda h: (0, 0)),
            pl.BlockSpec((1024, 512), lambda h: (0, 0)),
        ),
        out_shape=(
            jax.ShapeDtypeStruct((2048, 512), BF),
            jax.ShapeDtypeStruct((256, 512), F32),
            jax.ShapeDtypeStruct((1024, 512), BF),
        ),
        scratch_shapes=[
            vm((128, 128), I32),
            vm((4096, 512), BF),
            vm((2, 2048, 128), F32),
            vm((2, 1024, 128), F32),
            vm((512, 512), BF),
            vm((512, 512), BF),
            vm((2048, 512), F32),
            vm((1024, 512), F32),
        ],
        compiler_params=pltpu.CompilerParams(vmem_limit_bytes=VMEM_LIMIT),
        name="core_grads",
    )(arrived, tiles, spread, part, lt, middle_core)


class Place:
    def __init__(self):
        dp = lax.axis_index("dp")
        cores = lax.axis_index("cores")
        self.at = (cores // 2, dp // 4, lax.rem(dp, 4))
        self.core = lax.rem(cores, 2)

    def along(self, dim, offset):
        at = list(self.at)
        at[dim] = lax.rem(at[dim] + offset, 4)
        return at[dim], (at[1] * 4 + at[2], at[0] * 2 + self.core)

    def sibling(self):
        x, y, z = self.at
        return (y * 4 + z, x * 2 + 1 - self.core)


ORDERS = ((0, 1, 2), (1, 2, 0), (2, 0, 1))
SIZES = (256, 64, 16)


def reduce_kernel(
    with_rows, *refs,
):
    if with_rows:
        rows_ref, refs = refs[0], refs[1:]
    wide_ref, extra_ref = refs[:2]
    refs = refs[2:]
    if with_rows:
        landed_ref, refs = refs[0], refs[1:]
    total0, total1, total2, rest, pair0, pair1, pair2, sum0, sum1, sum2 = refs[:10]
    got00, got01, got02, got10, got11, got12, got20, got21, got22 = refs[10:19]
    halves0, halves1, halves2, send_sem, recv_sem = refs[19:24]
    place = Place()
    core = place.core
    barrier = pltpu.get_barrier_semaphore()
    if with_rows:
        row_send, row_recv, own_sem = refs[24:]
        me = lax.axis_index("dp") * 8 + lax.axis_index("cores")

        def partner(i):
            other = lax.rem(me + i, OWNERS)
            return other, (other // 8, lax.rem(other, 8))

        def greet(i, carry):
            pl.semaphore_signal(barrier, inc=1, device_id=partner(i)[1], device_id_type=MESH)
            return carry

        lax.fori_loop(1, OWNERS, greet, 0)
        expected = OWNERS - 1
    else:
        partners = [place.sibling()] + [place.along(d, o)[1] for d in range(3) for o in (1, 2, 3)]
        for who in partners:
            pl.semaphore_signal(barrier, inc=1, device_id=who, device_id_type=MESH)
        expected = len(partners)
    width = rest.shape[1]
    for block in range(4):
        if with_rows:
            value = extra_ref[:, block * 128 : (block + 1) * 128]
        else:
            value = extra_ref[(block // 2) * 512 : (block // 2 + 1) * 512, (block % 2) * 256 : (block % 2 + 1) * 256]
        rest[block * 512 : (block + 1) * 512, :] = value
    total = (total0, total1, total2)
    pair = (pair0, pair1, pair2)
    sums = (sum0, sum1, sum2)
    got = ((got00, got01, got02), (got10, got11, got12), (got20, got21, got22))

    def source(part, where):
        if part == 2:
            return rest.at[where]
        return wide_ref.at[where, slice(part * 256, (part + 1) * 256)]

    halves = (halves0, halves1, halves2)
    pl.semaphore_wait(barrier, expected)
    pending = []

    def start(part, stage, slot, src, dst, who):
        copy = pltpu.make_async_remote_copy(
            src_ref=src,
            dst_ref=dst,
            send_sem=send_sem.at[part, stage, slot],
            recv_sem=recv_sem.at[part, stage, slot],
            device_id=who,
            device_id_type=MESH,
        )
        copy.start()
        pending.append(copy)
        return copy

    def rows(start_row, size):
        return pl.ds(pl.multiple_of(start_row, 16), size)

    base = [core * 1024 for _ in range(3)]
    flight = {}
    for slot in (2, 1, 3, 0):
        for part in range(3):
            quarter, _ = place.along(ORDERS[part][0], slot)
            flight[part, slot] = start(
                part, 0, slot,
                source(part, rows((1 - core) * 1024 + quarter * 256, 256)),
                pair[part].at[rows(quarter * 256, 256)],
                place.sibling(),
            )
    if with_rows:
        own = pltpu.make_async_copy(rows_ref.at[me], landed_ref.at[me], own_sem)
        own.start()

        def send(i, carry):
            other, where = partner(i)
            pltpu.make_async_remote_copy(
                src_ref=rows_ref.at[other],
                dst_ref=landed_ref.at[me],
                send_sem=row_send,
                recv_sem=row_recv,
                device_id=where,
                device_id_type=MESH,
            ).start()
            return carry

        lax.fori_loop(1, OWNERS, send, 0)
    moving = {}

    def pair_sum(part, slot):
        quarter, _ = place.along(ORDERS[part][0], slot)
        flight[part, slot].wait_recv()
        at = rows(quarter * 256, 256)
        mine = source(part, rows(core * 1024 + quarter * 256, 256))[...].astype(F32)
        sums[part][at, :] = (mine + pair[part][at, :].astype(F32)).astype(BF)
        return quarter * 256

    for part in range(3):
        at = pair_sum(part, 2)
        for slot, lead, way in ((0, 0, 1), (2, 128, 3)):
            who = place.along(ORDERS[part][0], way)[1]
            src = sums[part].at[rows(at + lead, 128)]
            moving[part, slot] = start(part, 1, slot, src, halves[part].at[slot // 2], who)
    for way in (1, 3):
        for part in range(3):
            at = pair_sum(part, way)
            slot, lead = (0, 0) if way == 1 else (2, 128)
            moving[part, slot].wait_recv()
            piece = rows(at + lead, 128)
            more = halves[part][slot // 2].astype(F32)
            sums[part][piece, :] = (sums[part][piece, :].astype(F32) + more).astype(BF)
            who = place.along(ORDERS[part][0], way)[1]
            src = sums[part].at[rows(at, 256)]
            moving[part, way] = start(part, 1, way, src, got[part][0].at[way // 2], who)
    for part in range(3):
        pair_sum(part, 0)
    offset = [0, 0, 0]
    for level in range(3):
        size = SIZES[level]
        following = {}
        for part in range(3):
            mine = place.at[ORDERS[part][level]]
            offset[part] = offset[part] + mine * size
            ways = (1, 3) if level == 0 else (1, 2, 3)
            for slot in ways:
                moving[part, slot].wait_recv()
            at = rows(offset[part], size)
            value = sums[part][at, :].astype(F32)
            for slot in range(len(ways)):
                value = value + got[part][level][slot].astype(F32)
            if level < 2:
                sums[part][at, :] = value.astype(BF)
                for slot in (1, 2, 3):
                    quarter, who = place.along(ORDERS[part][level + 1], slot)
                    src = sums[part].at[rows(offset[part] + quarter * SIZES[level + 1], SIZES[level + 1])]
                    following[part, slot] = start(part, level + 2, slot, src, got[part][level + 1].at[slot - 1], who)
            else:
                where = rows(core * 1024 + offset[part], size)
                total[part][where, :] = value.astype(BF)
                for slot in (1, 2, 3):
                    who = place.along(ORDERS[part][2], slot)[1]
                    ref = total[part].at[where]
                    following[part, slot] = start(part, 4, slot, ref, ref, who)
        moving = following
    final = []
    for level in (1, 0):
        following = {}
        for part in range(3):
            mine = place.at[ORDERS[part][level + 1]]
            offset[part] = offset[part] - mine * SIZES[level + 1]
            for slot in (1, 2, 3):
                moving[part, slot].wait_recv()
            where = rows(core * 1024 + offset[part], SIZES[level])
            ref = total[part].at[where]
            for slot in (1, 3) if level == 0 else (1, 2, 3):
                who = place.along(ORDERS[part][level], slot)[1]
                following[part, slot] = start(part, 6 - level, slot, ref, ref, who)
            if level == 0:
                final.append(start(part, 7, 0, ref, ref, place.sibling()))
        moving = following

    def piece_of(part, way, lead, size):
        quarter = place.along(ORDERS[part][0], way)[0]
        return total[part].at[rows(core * 1024 + quarter * 256 + lead, size)]

    for way in (1, 3):
        for part in range(3):
            moving[part, way].wait_recv()
            slot, lead = (0, 0) if way == 1 else (2, 128)
            ref = piece_of(part, 4 - way, lead, 128)
            who = place.along(ORDERS[part][0], way)[1]
            moving[part, slot] = start(part, 6, slot, ref, ref, who)
            ref = piece_of(part, 4 - way, 0, 256)
            final.append(start(part, 7, way, ref, ref, place.sibling()))
    for part in range(3):
        moving[part, 0].wait_recv()
        moving[part, 2].wait_recv()
        ref = piece_of(part, 2, 0, 256)
        final.append(start(part, 7, 2, ref, ref, place.sibling()))
    for copy in final:
        copy.wait_recv()
    for copy in pending:
        copy.wait_send()
    if with_rows:
        whole = pltpu.make_async_remote_copy(
            src_ref=rows_ref.at[pl.ds(0, OWNERS - 1)],
            dst_ref=landed_ref.at[pl.ds(0, OWNERS - 1)],
            send_sem=row_send,
            recv_sem=row_recv,
            device_id=partner(1)[1],
            device_id_type=MESH,
        )
        whole.wait_send()
        whole.wait_recv()
        own.wait()


def reduce_all(wide, extra, ident, row_blocks=None):
    vm = pltpu.VMEM
    with_rows = row_blocks is not None
    widths = (256, 256, 128 if with_rows else 256)
    out_shape = tuple(jax.ShapeDtypeStruct((2048, w), BF) for w in widths)
    scratch = (
        [vm((2048, widths[2]), BF)]
        + [vm((1024, w), BF) for w in widths]
        + [vm((1024, w), BF) for w in widths]
        + [vm((3, size, w), BF) for w in widths for size in SIZES]
        + [vm((2, 128, w), BF) for w in widths]
        + [pltpu.SemaphoreType.DMA((3, 8, 4))] * 2
    )
    operands = (wide, extra)
    if with_rows:
        out_shape = (jax.ShapeDtypeStruct(row_blocks.shape, BF),) + out_shape
        operands = (row_blocks,) + operands
        scratch += [pltpu.SemaphoreType.DMA] * 3
    return pl.pallas_call(
        functools.partial(reduce_kernel, with_rows),
        out_shape=out_shape,
        in_specs=[pl.BlockSpec(memory_space=vm) for _ in operands],
        out_specs=tuple(pl.BlockSpec(memory_space=vm) for _ in out_shape),
        scratch_shapes=scratch,
        compiler_params=pltpu.CompilerParams(
            collective_id=ident, has_side_effects=True, vmem_limit_bytes=VMEM_LIMIT
        ),
        name="rows_and_weights" if with_rows else "reduce_cores",
    )(*operands)


def widen_kernel(p0, p1, p2, c0, c1, c2, first_ref, last_ref, proj_ref, out_ref):
    first_ref[:, 0:256] = c0[...].astype(F32)
    first_ref[:, 256:512] = c1[...].astype(F32)
    for block in range(4):
        lanes = slice(block * 512, block * 512 + 256)
        proj_ref[:, lanes] = p0[block].astype(F32)
        lanes = slice(block * 512 + 256, block * 512 + 512)
        proj_ref[:, lanes] = p1[block].astype(F32)
        out_ref[:, block * 128 : (block + 1) * 128] = p2[block].astype(F32)
        last_ref[block // 2, :, (block % 2) * 256 : (block % 2 + 1) * 256] = c2[block].astype(F32)


def widen(weights, cores):
    steps = 4
    rows = 512 // steps
    p0, p1, p2 = (x.reshape(4, 512, x.shape[1]) for x in weights)
    c0, c1, c2 = cores

    def cut(width):
        return pl.BlockSpec((4, rows, width), lambda i: (0, i, 0))

    flat = pl.BlockSpec((4 * rows, 256), lambda i: (i, 0))
    first, last, proj, out = pl.pallas_call(
        widen_kernel,
        grid=(steps,),
        in_specs=[cut(256), cut(256), cut(128), flat, flat, cut(256)],
        out_specs=(
            pl.BlockSpec((4 * rows, 512), lambda i: (i, 0)),
            pl.BlockSpec((2, rows, 512), lambda i: (0, i, 0)),
            pl.BlockSpec((rows, 2048), lambda i: (i, 0)),
            pl.BlockSpec((rows, 512), lambda i: (i, 0)),
        ),
        out_shape=(
            jax.ShapeDtypeStruct((2048, 512), F32),
            jax.ShapeDtypeStruct((2, 512, 512), F32),
            jax.ShapeDtypeStruct((512, 2048), F32),
            jax.ShapeDtypeStruct((512, 512), F32),
        ),
        compiler_params=pltpu.CompilerParams(vmem_limit_bytes=VMEM_LIMIT),
        name="widen",
    )(p0, p1, p2, c0, c1, c2.reshape(4, 512, 256))
    return first, last.reshape(1024, 512), proj, out


def exchange(x):
    return lax.all_to_all(x, AXES, split_axis=0, concat_axis=0, tiled=True)


def per_device(item_digits, first_core, middle_core, last_core, w_proj, w_out, layer_grad):
    arrived, slot_row, slot_col = prep(item_digits)
    arrived = arrived.reshape(OWNERS, 1, 128)
    built, spread, part, lt = build(arrived, first_core, middle_core, last_core)
    recv = exchange(built)
    layer_rows, sent, proj_grad, out_grad = layer(recv, slot_row, slot_col, w_proj, w_out, layer_grad)
    tiles, *weights = reduce_all(proj_grad, out_grad, 2, sent)
    first_part, grad_middle, last_part = core_grads(arrived, tiles, spread, part, lt, middle_core)
    cores = reduce_all(first_part, last_part, 3)
    grad_first, grad_last, proj_total, out_total = widen(weights, cores)
    return (layer_rows, grad_first, grad_middle, grad_last, proj_total, out_total)


def solution(mesh):
    return jax.shard_map(
        per_device,
        mesh=mesh,
        in_specs=(
            P(None, AXES),
            P(),
            P(AXES, None),
            P(),
            P(),
            P(),
            P(AXES, None),
        ),
        out_specs=(P(AXES, None), P(), P(AXES, None), P(), P(), P()),
        check_vma=False,
    )
```

```python
import functools
import math

import jax
import jax.numpy as jnp
from jax import lax
from jax.experimental import pallas as pl
from jax.experimental.pallas import tpu as pltpu
from jax.sharding import PartitionSpec as P

AXES = ("dp", "cores")
BF = jnp.bfloat16
F32 = jnp.float32
I32 = jnp.int32
EVENTS = 512
OWNERS = 128
VMEM_LIMIT = 56 * 1024 * 1024
MESH = pl.DeviceIdType.MESH


def iota(shape, dim):
    return lax.broadcasted_iota(I32, shape, dim)


def dot(a, b, ca=1, cb=0):
    return lax.dot_general(a, b, (((ca,), (cb,)), ((), ())), preferred_element_type=F32)


def bdot(a, b, ca, cb):
    return lax.dot_general(a, b, (((ca,), (cb,)), ((0,), (0,))), preferred_element_type=F32)


def half_turn(x):
    return pltpu.roll(x, 64, x.ndim - 1)


def low_lanes(shape):
    return iota(shape, len(shape) - 1) % 128 < 64


def one_hot(flag):
    return jnp.where(flag, 1.0, 0.0).astype(BF)


def prep_kernel(dig_ref, arrived_ref, slot_row_ref, slot_col_ref, message, stage, send_sem, recv_sem):
    dp = lax.axis_index("dp")
    cores = lax.axis_index("cores")
    barrier = pltpu.get_barrier_semaphore()
    row_mates = [(lax.rem(cores + i, 8), (dp, lax.rem(cores + i, 8))) for i in range(1, 8)]
    column_mates = [(lax.rem(dp + i, 16), (lax.rem(dp + i, 16), cores)) for i in range(1, 16)]
    for _, who in row_mates + column_mates:
        pl.semaphore_signal(barrier, inc=1, device_id=who, device_id_type=MESH)
    digits = dig_ref[...]
    padded = jnp.concatenate([digits, jnp.zeros((5, EVENTS), I32)], axis=0).astype(F32)
    cols = jnp.transpose(padded).astype(I32)
    owner_row = digits[1:2, :] >> 2
    owner_col = cols[:, 1:2] >> 2
    same = owner_row == owner_col
    sub = iota((EVENTS, EVENTS), 0)
    lane = iota((EVENTS, EVENTS), 1)
    rank_col = jnp.sum(jnp.where(same & (lane < sub), 1.0, 0.0), axis=1, keepdims=True).astype(I32)
    rank_row = jnp.sum(jnp.where(same & (sub < lane), 1.0, 0.0), axis=0, keepdims=True).astype(I32)
    slot_row_ref[...] = jnp.broadcast_to(rank_row * OWNERS + owner_row, (8, EVENTS))
    slot_col_ref[...] = jnp.broadcast_to(rank_col * OWNERS + owner_col, (EVENTS, 128))
    place = iota((EVENTS, 128), 1)
    inner = place % 32
    value = jnp.where(inner < 8, cols[:, 0:1], jnp.where(inner < 16, cols[:, 1:2], cols[:, 2:3])) + 1
    part = jnp.where(place < 32, value >> 4, value & 15)
    ok = (inner % 8 == rank_col) & (inner < 24) & (place < 64)
    table = jnp.where(ok, part, 0).astype(F32).astype(BF)
    pick = one_hot(iota((OWNERS, EVENTS), 0) == (owner_row & 7) * 16 + (owner_row >> 3))
    sums = dot(pick, table)
    whole = sums * 16.0 + pltpu.roll(sums, 96, 1)
    whole = jnp.where(iota((OWNERS, 128), 1) < 24, whole, 0.0).astype(I32)
    message[...] = whole.reshape(8, 16, 1, 128)
    pl.semaphore_wait(barrier, 22)

    def start(number, src, dst, who):
        copy = pltpu.make_async_remote_copy(
            src_ref=src,
            dst_ref=dst,
            send_sem=send_sem.at[number],
            recv_sem=recv_sem.at[number],
            device_id=who,
            device_id_type=MESH,
        )
        copy.start()
        return copy

    first = [start(n, message.at[c], stage.at[cores], who) for n, (c, who) in enumerate(row_mates)]
    stage[cores] = message[cores]
    for copy in first:
        copy.wait_recv()
    second = [
        start(7 + n, stage.at[:, d], arrived_ref.at[dp], who) for n, (d, who) in enumerate(column_mates)
    ]
    arrived_ref[dp] = stage[:, dp]
    for copy in second:
        copy.wait_recv()
    for copy in first + second:
        copy.wait_send()


def prep(digits):
    return pl.pallas_call(
        prep_kernel,
        out_shape=(
            jax.ShapeDtypeStruct((16, 8, 1, 128), I32),
            jax.ShapeDtypeStruct((8, EVENTS), I32),
            jax.ShapeDtypeStruct((EVENTS, 128), I32),
        ),
        scratch_shapes=[
            pltpu.VMEM((8, 16, 1, 128), I32),
            pltpu.VMEM((8, 16, 1, 128), I32),
            pltpu.SemaphoreType.DMA((22,)),
            pltpu.SemaphoreType.DMA((22,)),
        ],
        compiler_params=pltpu.CompilerParams(
            collective_id=1, has_side_effects=True, vmem_limit_bytes=VMEM_LIMIT
        ),
        name="prep",
    )(digits)


def index_columns(arrived, half):
    lane = iota((OWNERS, 128), 1)
    out = []
    for digit in range(3):
        parts = []
        for t in range(4):
            mine = lane == digit * 8 + half * 4 + t
            parts.append(jnp.sum(jnp.where(mine, arrived, 0).astype(F32), axis=1, keepdims=True))
        out.append(jnp.concatenate(parts, axis=0).astype(I32) - 1)
    return out


def slice_masks(middle_col):
    local = jnp.where(middle_col < 0, -1, middle_col & 3)
    group = iota((512, 128), 1) // 64
    return local == group, local == group + 2


def build_kernel(arrived_ref, first_ref, middle_ref, last_ref, built_ref, spread_ref, part_ref, lt_ref, fs, ps, ls):
    half = pl.program_id(0)
    arrived = arrived_ref[...].reshape(OWNERS, 128)
    first_col, middle_col, last_col = index_columns(arrived, half)
    low = low_lanes((128, 128))
    rows = dot(one_hot(first_col == iota((512, 2048), 1)), first_ref[...])
    mask0, mask1 = slice_masks(middle_col)
    for t in range(4):
        m0 = mask0[t * 128 : (t + 1) * 128]
        m1 = mask1[t * 128 : (t + 1) * 128]
        for pair in range(4):
            x = rows[t * 128 : (t + 1) * 128, pair * 128 : (pair + 1) * 128]
            turned = half_turn(x)
            for odd in range(2):
                both = jnp.where(low, turned, x) if odd else jnp.where(low, x, turned)
                at = pl.ds(t * 1024 + pair * 2 + odd, 128, stride=8)
                fs[0, at, :] = jnp.where(m0, both, 0.0)
                fs[1, at, :] = jnp.where(m1, both, 0.0)
    source = iota((512, 512), 0)
    perm = one_hot(iota((512, 512), 1) == (source % 8) * 64 + source // 8)
    rows = dot(one_hot(last_col == iota((512, 1024), 1)), last_ref[...]).astype(BF)
    rows = dot(rows, perm)
    for t in range(4):
        for pair in range(4):
            x = rows[t * 128 : (t + 1) * 128, pair * 128 : (pair + 1) * 128]
            turned = half_turn(x)
            for odd in range(2):
                both = jnp.where(low, turned, x) if odd else jnp.where(low, x, turned)
                keep = jnp.where(low, 0.0, both) if t % 2 else jnp.where(low, both, 0.0)
                ls[t // 2, pl.ds((t % 2) * 8 + pair * 2 + odd, 128, stride=16), :] = keep

    def spread_step(i, carry):
        at = pl.ds(pl.multiple_of(i * 512, 512), 512)
        spread_ref[at, 0:128] = fs[0, at, :].astype(BF)
        spread_ref[at, 128:256] = fs[1, at, :].astype(BF)
        ps[at, :] = dot(spread_ref[at, :], middle_ref[...])
        return carry

    lax.fori_loop(0, 8, spread_step, 0)

    group = 128
    low = low_lanes((group * 8, 128))

    def combine(i, carry):
        srcs = pl.ds(pl.multiple_of(i * group, group), group)
        for pair in range(4):
            lanes = slice(pair * 128, (pair + 1) * 128)
            v = [ps[pl.ds(pl.multiple_of(t * 1024 + i * group * 8, 8), group * 8), lanes] for t in range(4)]
            w = [half_turn(x) for x in v]
            for side in range(2):
                v0, v1 = v[2 * side], v[2 * side + 1]
                w0, w1 = w[2 * side], w[2 * side + 1]
                even = jnp.where(low, v0, w1).reshape(group, 8, 128)
                odd = jnp.where(low, w0, v1).reshape(group, 8, 128)
                part_ref[srcs, pair * 16 : (pair + 1) * 16, side * 128 : (side + 1) * 128] = jnp.concatenate(
                    [even, odd], axis=1
                ).astype(BF)
        wide = pl.ds(pl.multiple_of(i * group * 16, group * 16), group * 16)
        zero = jnp.zeros((group, 16, 128), BF)
        lt_ref[srcs, 0:16, 0:128] = ls[0, wide, :].reshape(group, 16, 128).astype(BF)
        lt_ref[srcs, 0:16, 128:256] = zero
        lt_ref[srcs, 16:32, 0:128] = zero
        lt_ref[srcs, 16:32, 128:256] = ls[1, wide, :].reshape(group, 16, 128).astype(BF)
        out = bdot(lt_ref[srcs], part_ref[srcs], 2, 2)
        tile = jnp.concatenate([out[:, 0:16, :], out[:, 16:32, :]], axis=2)
        built_ref[srcs, 0] = tile.astype(BF)
        return carry

    lax.fori_loop(0, OWNERS // group, combine, 0)


def build(arrived, first_core, middle_core, last_core):
    return pl.pallas_call(
        build_kernel,
        grid=(2,),
        in_specs=[
            pl.BlockSpec((OWNERS, 1, 128), lambda h: (0, 0, 0)),
            pl.BlockSpec((2048, 512), lambda h: (0, 0)),
            pl.BlockSpec((256, 512), lambda h: (0, 0)),
            pl.BlockSpec((1024, 512), lambda h: (0, 0)),
        ],
        out_specs=(
            pl.BlockSpec((OWNERS, 1, 16, 128), lambda h: (0, h, 0, 0)),
            pl.BlockSpec((4096, 256), lambda h: (h, 0)),
            pl.BlockSpec((OWNERS, 64, 256), lambda h: (h, 0, 0)),
            pl.BlockSpec((OWNERS, 32, 256), lambda h: (h, 0, 0)),
        ),
        out_shape=(
            jax.ShapeDtypeStruct((OWNERS, 2, 16, 128), BF),
            jax.ShapeDtypeStruct((8192, 256), BF),
            jax.ShapeDtypeStruct((2 * OWNERS, 64, 256), BF),
            jax.ShapeDtypeStruct((2 * OWNERS, 32, 256), BF),
        ),
        scratch_shapes=[
            pltpu.VMEM((2, 4096, 128), F32),
            pltpu.VMEM((4096, 512), F32),
            pltpu.VMEM((2, 2048, 128), F32),
        ],
        compiler_params=pltpu.CompilerParams(vmem_limit_bytes=VMEM_LIMIT),
        name="build",
    )(arrived, first_core, middle_core, last_core)


def sigmoid(x):
    return 0.5 * jnp.tanh(0.5 * x) + 0.5


def norm_stats(x):
    center = x - jnp.mean(x, axis=-1, keepdims=True)
    spread = jnp.mean(center * center, axis=-1, keepdims=True)
    scale = lax.rsqrt(spread + 1e-05)
    return center * scale, scale


def norm_grad(ct, y, scale):
    return scale * (ct - jnp.mean(ct, axis=-1, keepdims=True) - y * jnp.mean(ct * y, axis=-1, keepdims=True))


def layer_kernel(
    recv_ref, slot_row_ref, slot_col_ref, proj_ref, out_ref, grad_ref,
    rows_ref, sent_ref, dproj_ref, dout_ref,
    tiles, slots, emb, normed, y_in, z, act, mixed, y_mid, gated, dz, dmixed, work, work_v, work_k, sc_in,
):
    low = low_lanes((128, 128))
    step = 256
    tall = 512

    def widen(i, carry):
        srcs = pl.ds(pl.multiple_of(i * 32, 32), 32)
        tiles[pl.ds(pl.multiple_of(i * 1024, 1024), 1024), :] = recv_ref[srcs].reshape(1024, 128).astype(F32)
        return carry

    lax.fori_loop(0, 4, widen, 0)
    for half in range(2):
        for tlo in range(2):
            for pair in range(4):
                base = half * 16 + tlo * 8 + pair * 2
                y0 = tiles[pl.ds(base, 128, stride=32), :]
                y1 = tiles[pl.ds(base + 1, 128, stride=32), :]
                lanes = slice(pair * 128, (pair + 1) * 128)
                k0 = half * 4 + tlo
                slots[k0 * 128 : (k0 + 1) * 128, lanes] = jnp.where(low, y0, half_turn(y1)).astype(BF)
                k1 = k0 + 2
                slots[k1 * 128 : (k1 + 1) * 128, lanes] = jnp.where(low, half_turn(y0), y1).astype(BF)
    source = iota((512, 512), 0)
    target = iota((512, 512), 1)
    flip = one_hot(target == (source % 8) * 64 + ((source // 8) % 8) * 8 + source // 64)
    pick = one_hot(slot_col_ref[:, 0:1] == iota((EVENTS, 1024), 1))
    emb[...] = dot(dot(pick, slots[...]).astype(BF), flip)

    def project(i, carry):
        at = pl.ds(pl.multiple_of(i * tall, tall), tall)
        y, scale = norm_stats(emb[at, :])
        y_in[at, :] = y
        sc_in[at, :] = jnp.broadcast_to(scale, (tall, 128))
        normed[at, :] = y.astype(BF)
        for block in range(4):
            lanes = slice(block * 512, (block + 1) * 512)
            value = dot(normed[at, :], proj_ref[:, lanes])
            z[at, lanes] = value
            act[at, lanes] = (value * sigmoid(value)).astype(BF)
        return carry

    lax.fori_loop(0, EVENTS // tall, project, 0)
    scaling = 1.0 / math.sqrt(128.0)

    def scores_of(head, block):
        end = (block + 1) * step
        q = act[block * step : end, pl.ds(pl.multiple_of(1024 + head * 128, 128), 128)]
        k = act[0:end, pl.ds(pl.multiple_of(1536 + head * 128, 128), 128)]
        s = dot(q, k, 1, 1) * scaling
        causal = block * step + iota((step, end), 0) >= iota((step, end), 1)
        return s, causal

    def attend(head, carry):
        cols = pl.ds(pl.multiple_of(head * 128, 128), 128)
        for block in range(2):
            end = (block + 1) * step
            s, causal = scores_of(head, block)
            weights = jnp.where(causal, s * sigmoid(s), 0.0).astype(BF)
            v = act[0:end, pl.ds(pl.multiple_of(512 + head * 128, 128), 128)]
            mixed[block * step : end, cols] = dot(weights, v)
        return carry

    lax.fori_loop(0, 4, attend, 0)

    def finish(i, carry):
        at = pl.ds(pl.multiple_of(i * tall, tall), tall)
        y, scale = norm_stats(mixed[at, :])
        u = act[at, 0:512].astype(F32)
        gate = (y * u).astype(BF)
        gated[at, :] = gate
        g = grad_ref[at, :]
        rows_ref[at, :] = (dot(gate, out_ref[...]) + emb[at, :]).astype(BF)
        d_gate = dot(g, out_ref[...], 1, 1).astype(BF).astype(F32)
        d_u = (d_gate * y).astype(BF).astype(F32)
        zu = z[at, 0:512]
        sig = sigmoid(zu)
        dz[at, 0:512] = (d_u * (sig * (1.0 + zu * (1.0 - sig)))).astype(BF)
        dmixed[at, :] = norm_grad(d_gate * u, y, scale).astype(BF)
        return carry

    lax.fori_loop(0, EVENTS // tall, finish, 0)
    dout_ref[...] = dot(gated[...], grad_ref[...], 0, 0).astype(BF)

    def attend_grad(head, carry):
        cols = pl.ds(pl.multiple_of(head * 128, 128), 128)
        vcols = pl.ds(pl.multiple_of(512 + head * 128, 128), 128)
        qcols = pl.ds(pl.multiple_of(1024 + head * 128, 128), 128)
        kcols = pl.ds(pl.multiple_of(1536 + head * 128, 128), 128)
        for block in (1, 0):
            end = (block + 1) * step
            rows = slice(block * step, end)
            s, causal = scores_of(head, block)
            sig = sigmoid(s)
            weights = jnp.where(causal, s * sig, 0.0).astype(BF)
            dm = dmixed[rows, cols]
            d_w = dot(dm, act[0:end, vcols], 1, 1).astype(BF).astype(F32)
            d_s = jnp.where(causal, d_w * (sig * (1.0 + s * (1.0 - sig))) * scaling, 0.0).astype(BF)
            v_part = dot(weights, dm, 0, 0)
            k_part = dot(d_s, act[rows, qcols], 0, 0)
            if block == 1:
                work_v[...] = v_part
                work_k[...] = k_part
            else:
                work_v[0:end, :] += v_part
                work_k[0:end, :] += k_part
            work[rows, :] = dot(d_s, act[0:end, kcols])

        def through(ct, where):
            value = z[:, where]
            sig = sigmoid(value)
            dz[:, where] = (ct.astype(BF).astype(F32) * (sig * (1.0 + value * (1.0 - sig)))).astype(BF)

        through(work[...], qcols)
        through(work_v[...], vcols)
        through(work_k[...], kcols)
        return carry

    lax.fori_loop(0, 4, attend_grad, 0)

    for block in range(4):
        lanes = slice(block * 512, (block + 1) * 512)
        dproj_ref[lanes, :] = dot(normed[...], dz[:, lanes], 0, 0).astype(BF)

    back = one_hot(source == (target % 8) * 64 + ((target // 8) % 8) * 8 + target // 64)

    def close(i, carry):
        at = pl.ds(pl.multiple_of(i * tall, tall), tall)
        d_normed = dot(dz[at, :], proj_ref[...], 1, 1).astype(BF).astype(F32)
        d_rows = norm_grad(d_normed, y_in[at, :], sc_in[at, 0:1]) + grad_ref[at, :].astype(F32)
        gated[at, :] = d_rows.astype(BF)
        return carry

    lax.fori_loop(0, EVENTS // tall, close, 0)
    turned = dot(gated[...], back).astype(BF)
    for half in range(2):
        for tlo in range(2):
            found = []
            for thi in range(2):
                k = half * 4 + thi * 2 + tlo
                place = one_hot(iota((128, EVENTS), 0) + k * 128 == slot_row_ref[0:1, :])
                found.append(dot(place, turned))
            for pair in range(4):
                lanes = slice(pair * 128, (pair + 1) * 128)
                x0, x1 = found[0][:, lanes], found[1][:, lanes]
                base = half * 16 + tlo * 8 + pair * 2
                tiles[pl.ds(base, 128, stride=32), :] = jnp.where(low, x0, half_turn(x1))
                tiles[pl.ds(base + 1, 128, stride=32), :] = jnp.where(low, half_turn(x0), x1)

    def narrow(i, carry):
        srcs = pl.ds(pl.multiple_of(i * 32, 32), 32)
        sent_ref[srcs] = tiles[pl.ds(pl.multiple_of(i * 1024, 1024), 1024), :].astype(BF).reshape(32, 2, 16, 128)
        return carry

    lax.fori_loop(0, 4, narrow, 0)


def layer(recv, slot_row, slot_col, w_proj, w_out, layer_grad):
    vm = pltpu.VMEM
    return pl.pallas_call(
        layer_kernel,
        out_shape=(
            jax.ShapeDtypeStruct((EVENTS, 512), BF),
            jax.ShapeDtypeStruct((OWNERS, 2, 16, 128), BF),
            jax.ShapeDtypeStruct((2048, 512), BF),
            jax.ShapeDtypeStruct((512, 512), BF),
        ),
        scratch_shapes=[
            vm((4096, 128), F32),
            vm((1024, 512), BF),
            vm((EVENTS, 512), F32),
            vm((EVENTS, 512), BF),
            vm((EVENTS, 512), F32),
            vm((EVENTS, 2048), F32),
            vm((EVENTS, 2048), BF),
            vm((EVENTS, 512), F32),
            vm((EVENTS, 512), F32),
            vm((EVENTS, 512), BF),
            vm((EVENTS, 2048), BF),
            vm((EVENTS, 512), BF),
            vm((EVENTS, 128), F32),
            vm((EVENTS, 128), F32),
            vm((EVENTS, 128), F32),
            vm((EVENTS, 128), F32),
        ],
        compiler_params=pltpu.CompilerParams(vmem_limit_bytes=VMEM_LIMIT),
        name="layer",
    )(recv, slot_row, slot_col, w_proj, w_out, layer_grad)


def core_grad_kernel(
    arrived_ref, tile_ref, spread_ref, part_ref, lt_ref, middle_ref,
    first_out, middle_out, last_out,
    flipped, pg, ls, ss, fterm, lterm,
):
    half = pl.program_id(0)
    arrived = arrived_ref[...].reshape(OWNERS, 128)
    flipped[...] = jnp.transpose(arrived.astype(F32)).astype(I32) - 1
    _, middle_col, _ = index_columns(arrived, half)
    mask0, mask1 = slice_masks(middle_col)
    group = 128
    low = low_lanes((group, 8, 128))
    own = (iota((group, 16, 128), 1) // 8) == (iota((group, 16, 128), 2) // 64)

    def events(i, carry):
        srcs = pl.ds(pl.multiple_of(i * group, group), group)
        tile = tile_ref[srcs, 0]
        g = jnp.concatenate([tile[:, :, 0:64], tile[:, :, 64:128]], axis=1)
        wide = pl.ds(pl.multiple_of(i * group * 16, group * 16), group * 16)
        terms = bdot(g, part_ref[srcs], 2, 1)
        for side in range(2):
            x = terms[:, side * 16 : (side + 1) * 16, side * 128 : (side + 1) * 128]
            x = jnp.where(own, x, 0.0).reshape(group * 16, 128)
            ls[side, wide, :] = x + half_turn(x)
        grads = bdot(g, lt_ref[srcs], 1, 1)
        for pair in range(4):
            lanes = slice(pair * 128, (pair + 1) * 128)
            for side in range(2):
                even = grads[:, pair * 16 : pair * 16 + 8, side * 128 : (side + 1) * 128]
                odd = grads[:, pair * 16 + 8 : pair * 16 + 16, side * 128 : (side + 1) * 128]
                v0 = jnp.where(low, even, half_turn(odd))
                v1 = jnp.where(low, half_turn(even), odd)
                for t, v in ((2 * side, v0), (2 * side + 1, v1)):
                    at = pl.ds(pl.multiple_of(t * 1024 + i * group * 8, group * 8), group * 8)
                    pg[at, lanes] = v.reshape(group * 8, 128).astype(BF)
        return carry

    lax.fori_loop(0, OWNERS // group, events, 0)
    low = low_lanes((128, 128))
    middle_part = jnp.zeros((256, 512), F32)
    for t in range(4):
        at = slice(t * 1024, (t + 1) * 1024)
        middle_part += dot(spread_ref[at, :], pg[at, :], 0, 0)
        back = dot(pg[at, :], middle_ref[...], 1, 1)
        ss[0] = back[:, 0:128]
        ss[1] = back[:, 128:256]
        rows = slice(t * 128, (t + 1) * 128)
        keep = pl.ds(pl.multiple_of(half * 512 + t * 128, 128), 128)
        m0, m1 = mask0[rows], mask1[rows]
        for pair in range(4):
            lanes = slice(pair * 128, (pair + 1) * 128)
            found = []
            for odd in range(2):
                where = pl.ds(pair * 2 + odd, 128, stride=8)
                x = jnp.where(m0, ss[0, where, :], 0.0) + jnp.where(m1, ss[1, where, :], 0.0)
                found.append(x + half_turn(x))
            fterm[keep, lanes] = jnp.where(low, found[0], found[1]).astype(BF)
            base = (t % 2) * 8 + pair * 2
            y0 = ls[t // 2, pl.ds(base, 128, stride=16), :]
            y1 = ls[t // 2, pl.ds(base + 1, 128, stride=16), :]
            lterm[keep, lanes] = jnp.where(low, y0, y1).astype(BF)

    source = iota((512, 512), 0)
    perm = one_hot(iota((512, 512), 1) == (source % 64) * 8 + source // 64)
    done = pl.ds(pl.multiple_of(half * 512, 512), 512)
    lterm[done, :] = dot(lterm[done, :], perm).astype(BF)

    def index_row(digit):
        return jnp.concatenate([flipped[digit * 8 + t : digit * 8 + t + 1, :] for t in range(8)], axis=1)

    @pl.when(half == 0)
    def _():
        middle_out[...] = middle_part

    @pl.when(half == 1)
    def _():
        middle_out[...] += middle_part

    @pl.when(half == 1)
    def _():
        first_row = index_row(0)
        last_row = index_row(2)

        def scatter_first(i, carry):
            at = pl.ds(pl.multiple_of(i * 256, 256), 256)
            place = one_hot(iota((256, 1024), 0) + i * 256 == first_row)
            first_out[at, :] = dot(place, fterm[...]).astype(BF)
            return carry

        def scatter_last(i, carry):
            at = pl.ds(pl.multiple_of(i * 256, 256), 256)
            place = one_hot(iota((256, 1024), 0) + i * 256 == last_row)
            last_out[at, :] = dot(place, lterm[...]).astype(BF)
            return carry

        lax.fori_loop(0, 8, scatter_first, 0)
        lax.fori_loop(0, 4, scatter_last, 0)


def core_grads(arrived, tiles, spread, part, lt, middle_core):
    vm = pltpu.VMEM
    return pl.pallas_call(
        core_grad_kernel,
        grid=(2,),
        in_specs=[
            pl.BlockSpec((OWNERS, 1, 128), lambda h: (0, 0, 0)),
            pl.BlockSpec((OWNERS, 1, 16, 128), lambda h: (0, h, 0, 0)),
            pl.BlockSpec((4096, 256), lambda h: (h, 0)),
            pl.BlockSpec((OWNERS, 64, 256), lambda h: (h, 0, 0)),
            pl.BlockSpec((OWNERS, 32, 256), lambda h: (h, 0, 0)),
            pl.BlockSpec((256, 512), lambda h: (0, 0)),
        ],
        out_specs=(
            pl.BlockSpec((2048, 512), lambda h: (0, 0)),
            pl.BlockSpec((256, 512), lambda h: (0, 0)),
            pl.BlockSpec((1024, 512), lambda h: (0, 0)),
        ),
        out_shape=(
            jax.ShapeDtypeStruct((2048, 512), BF),
            jax.ShapeDtypeStruct((256, 512), F32),
            jax.ShapeDtypeStruct((1024, 512), BF),
        ),
        scratch_shapes=[
            vm((128, 128), I32),
            vm((4096, 512), BF),
            vm((2, 2048, 128), F32),
            vm((2, 1024, 128), F32),
            vm((1024, 512), BF),
            vm((1024, 512), BF),
        ],
        compiler_params=pltpu.CompilerParams(vmem_limit_bytes=VMEM_LIMIT),
        name="core_grads",
    )(arrived, tiles, spread, part, lt, middle_core)


class Place:
    def __init__(self):
        dp = lax.axis_index("dp")
        cores = lax.axis_index("cores")
        self.at = (cores // 2, dp // 4, lax.rem(dp, 4))
        self.core = lax.rem(cores, 2)

    def along(self, dim, offset):
        at = list(self.at)
        at[dim] = lax.rem(at[dim] + offset, 4)
        return at[dim], (at[1] * 4 + at[2], at[0] * 2 + self.core)

    def sibling(self):
        x, y, z = self.at
        return (y * 4 + z, x * 2 + 1 - self.core)


ORDERS = ((0, 1, 2), (1, 2, 0), (2, 0, 1))
SIZES = (256, 64, 16)


def reduce_kernel(
    first_ref, proj_ref, last_ref, out_ref,
    total0, total1, total2,
    rest, pair0, pair1, pair2, sum0, sum1, sum2,
    got00, got01, got02, got10, got11, got12, got20, got21, got22,
    halves0, halves1, halves2, send_sem, recv_sem,
):
    place = Place()
    core = place.core
    barrier = pltpu.get_barrier_semaphore()
    partners = [place.sibling()] + [place.along(d, o)[1] for d in range(3) for o in (1, 2, 3)]
    for who in partners:
        pl.semaphore_signal(barrier, inc=1, device_id=who, device_id_type=MESH)
    for block in range(12):
        row = (block // 3) * 512
        lanes = slice((block % 3) * 128, (block % 3 + 1) * 128)
        if block < 8:
            value = last_ref[(block // 4) * 512 : (block // 4 + 1) * 512, (block % 4) * 128 : (block % 4 + 1) * 128]
        else:
            value = out_ref[:, (block % 4) * 128 : (block % 4 + 1) * 128]
        rest[row : row + 512, lanes] = value
    source = (first_ref, proj_ref, rest)
    total = (total0, total1, total2)
    pair = (pair0, pair1, pair2)
    sums = (sum0, sum1, sum2)
    got = ((got00, got01, got02), (got10, got11, got12), (got20, got21, got22))
    halves = (halves0, halves1, halves2)
    pl.semaphore_wait(barrier, len(partners))
    pending = []

    def start(part, stage, slot, src, dst, who):
        copy = pltpu.make_async_remote_copy(
            src_ref=src,
            dst_ref=dst,
            send_sem=send_sem.at[part, stage, slot],
            recv_sem=recv_sem.at[part, stage, slot],
            device_id=who,
            device_id_type=MESH,
        )
        copy.start()
        pending.append(copy)
        return copy

    def rows(start_row, size):
        return pl.ds(pl.multiple_of(start_row, 16), size)

    base = [core * 1024 for _ in range(3)]
    flight = {}
    for slot in (2, 1, 3, 0):
        for part in range(3):
            quarter, _ = place.along(ORDERS[part][0], slot)
            flight[part, slot] = start(
                part, 0, slot,
                source[part].at[rows((1 - core) * 1024 + quarter * 256, 256)],
                pair[part].at[rows(quarter * 256, 256)],
                place.sibling(),
            )
    moving = {}

    def pair_sum(part, slot):
        quarter, _ = place.along(ORDERS[part][0], slot)
        flight[part, slot].wait_recv()
        at = rows(quarter * 256, 256)
        mine = source[part][rows(core * 1024 + quarter * 256, 256), :].astype(F32)
        sums[part][at, :] = (mine + pair[part][at, :].astype(F32)).astype(BF)
        return quarter * 256

    for part in range(3):
        at = pair_sum(part, 2)
        for slot, lead, way in ((0, 0, 1), (2, 128, 3)):
            who = place.along(ORDERS[part][0], way)[1]
            src = sums[part].at[rows(at + lead, 128)]
            moving[part, slot] = start(part, 1, slot, src, halves[part].at[slot // 2], who)
    for way in (1, 3):
        for part in range(3):
            at = pair_sum(part, way)
            slot, lead = (0, 0) if way == 1 else (2, 128)
            moving[part, slot].wait_recv()
            piece = rows(at + lead, 128)
            more = halves[part][slot // 2].astype(F32)
            sums[part][piece, :] = (sums[part][piece, :].astype(F32) + more).astype(BF)
            who = place.along(ORDERS[part][0], way)[1]
            src = sums[part].at[rows(at, 256)]
            moving[part, way] = start(part, 1, way, src, got[part][0].at[way // 2], who)
    for part in range(3):
        pair_sum(part, 0)
    offset = [0, 0, 0]
    for level in range(3):
        size = SIZES[level]
        following = {}
        for part in range(3):
            mine = place.at[ORDERS[part][level]]
            offset[part] = offset[part] + mine * size
            ways = (1, 3) if level == 0 else (1, 2, 3)
            for slot in ways:
                moving[part, slot].wait_recv()
            at = rows(offset[part], size)
            value = sums[part][at, :].astype(F32)
            for slot in range(len(ways)):
                value = value + got[part][level][slot].astype(F32)
            if level < 2:
                sums[part][at, :] = value.astype(BF)
                for slot in (1, 2, 3):
                    quarter, who = place.along(ORDERS[part][level + 1], slot)
                    src = sums[part].at[rows(offset[part] + quarter * SIZES[level + 1], SIZES[level + 1])]
                    following[part, slot] = start(part, level + 2, slot, src, got[part][level + 1].at[slot - 1], who)
            else:
                where = rows(core * 1024 + offset[part], size)
                total[part][where, :] = value.astype(BF)
                for slot in (1, 2, 3):
                    who = place.along(ORDERS[part][2], slot)[1]
                    ref = total[part].at[where]
                    following[part, slot] = start(part, 4, slot, ref, ref, who)
        moving = following
    final = []
    for level in (1, 0):
        following = {}
        for part in range(3):
            mine = place.at[ORDERS[part][level + 1]]
            offset[part] = offset[part] - mine * SIZES[level + 1]
            for slot in (1, 2, 3):
                moving[part, slot].wait_recv()
            where = rows(core * 1024 + offset[part], SIZES[level])
            ref = total[part].at[where]
            for slot in (1, 3) if level == 0 else (1, 2, 3):
                who = place.along(ORDERS[part][level], slot)[1]
                following[part, slot] = start(part, 6 - level, slot, ref, ref, who)
            if level == 0:
                final.append(start(part, 7, 0, ref, ref, place.sibling()))
        moving = following

    def piece_of(part, way, lead, size):
        quarter = place.along(ORDERS[part][0], way)[0]
        return total[part].at[rows(core * 1024 + quarter * 256 + lead, size)]

    for way in (1, 3):
        for part in range(3):
            moving[part, way].wait_recv()
            slot, lead = (0, 0) if way == 1 else (2, 128)
            ref = piece_of(part, 4 - way, lead, 128)
            who = place.along(ORDERS[part][0], way)[1]
            moving[part, slot] = start(part, 6, slot, ref, ref, who)
            ref = piece_of(part, 4 - way, 0, 256)
            final.append(start(part, 7, way, ref, ref, place.sibling()))
    for part in range(3):
        moving[part, 0].wait_recv()
        moving[part, 2].wait_recv()
        ref = piece_of(part, 2, 0, 256)
        final.append(start(part, 7, 2, ref, ref, place.sibling()))
    for copy in final:
        copy.wait_recv()
    for copy in pending:
        copy.wait_send()


def reduce_all(first_part, proj_grad, last_part, out_grad, ident):
    vm = pltpu.VMEM
    widths = (512, 512, 384)
    return pl.pallas_call(
        reduce_kernel,
        out_shape=tuple(jax.ShapeDtypeStruct((2048, w), BF) for w in widths),
        in_specs=[pl.BlockSpec(memory_space=vm)] * 4,
        out_specs=tuple(pl.BlockSpec(memory_space=vm) for _ in widths),
        scratch_shapes=[vm((2048, 384), BF)]
        + [vm((1024, w), BF) for w in widths]
        + [vm((1024, w), BF) for w in widths]
        + [vm((3, size, w), BF) for w in widths for size in SIZES]
        + [vm((2, 128, w), BF) for w in widths]
        + [pltpu.SemaphoreType.DMA((3, 8, 4))] * 2,
        compiler_params=pltpu.CompilerParams(
            collective_id=ident, has_side_effects=True, vmem_limit_bytes=VMEM_LIMIT
        ),
        name="reduce_all",
    )(first_part, proj_grad, last_part, out_grad)


def widen_kernel(a_ref, b_ref, c_ref, first_ref, last_ref, proj_ref, out_ref):
    first_ref[...] = a_ref[...].astype(F32)
    for block in range(4):
        lanes = slice(block * 512, (block + 1) * 512)
        proj_ref[:, lanes] = b_ref[block].astype(F32)
    for block in range(12):
        value = c_ref[block // 3, :, (block % 3) * 128 : (block % 3 + 1) * 128].astype(F32)
        lanes = slice((block % 4) * 128, (block % 4 + 1) * 128)
        if block < 8:
            last_ref[block // 4, :, lanes] = value
        else:
            out_ref[:, lanes] = value


def widen(a, b, c):
    steps = 8
    rows = 512 // steps
    first, last, proj, out = pl.pallas_call(
        widen_kernel,
        grid=(steps,),
        in_specs=[
            pl.BlockSpec((4 * rows, 512), lambda i: (i, 0)),
            pl.BlockSpec((4, rows, 512), lambda i: (0, i, 0)),
            pl.BlockSpec((4, rows, 384), lambda i: (0, i, 0)),
        ],
        out_specs=(
            pl.BlockSpec((4 * rows, 512), lambda i: (i, 0)),
            pl.BlockSpec((2, rows, 512), lambda i: (0, i, 0)),
            pl.BlockSpec((rows, 2048), lambda i: (i, 0)),
            pl.BlockSpec((rows, 512), lambda i: (i, 0)),
        ),
        out_shape=(
            jax.ShapeDtypeStruct((2048, 512), F32),
            jax.ShapeDtypeStruct((2, 512, 512), F32),
            jax.ShapeDtypeStruct((512, 2048), F32),
            jax.ShapeDtypeStruct((512, 512), F32),
        ),
        compiler_params=pltpu.CompilerParams(vmem_limit_bytes=VMEM_LIMIT),
        name="widen",
    )(a, b.reshape(4, 512, 512), c.reshape(4, 512, 384))
    return first, last.reshape(1024, 512), proj, out


def exchange(x):
    return lax.all_to_all(x, AXES, split_axis=0, concat_axis=0, tiled=True)


def per_device(item_digits, first_core, middle_core, last_core, w_proj, w_out, layer_grad):
    arrived, slot_row, slot_col = prep(item_digits)
    arrived = arrived.reshape(OWNERS, 1, 128)
    built, spread, part, lt = build(arrived, first_core, middle_core, last_core)
    recv = exchange(built)
    layer_rows, sent, proj_grad, out_grad = layer(recv, slot_row, slot_col, w_proj, w_out, layer_grad)
    tiles = exchange(sent)
    first_part, grad_middle, last_part = core_grads(arrived, tiles, spread, part, lt, middle_core)
    totals = reduce_all(first_part, proj_grad, last_part, out_grad, 2)
    grad_first, grad_last, proj_total, out_total = widen(*totals)
    return (layer_rows, grad_first, grad_middle, grad_last, proj_total, out_total)


def solution(mesh):
    return jax.shard_map(
        per_device,
        mesh=mesh,
        in_specs=(
            P(None, AXES),
            P(),
            P(AXES, None),
            P(),
            P(),
            P(),
            P(AXES, None),
        ),
        out_specs=(P(AXES, None), P(), P(AXES, None), P(), P(), P()),
        check_vma=False,
    )
```

```python
import functools
import math

import jax
import jax.numpy as jnp
from jax import lax
from jax.experimental import pallas as pl
from jax.experimental.pallas import tpu as pltpu
from jax.sharding import PartitionSpec as P

AXES = ("dp", "cores")
BF = jnp.bfloat16
F32 = jnp.float32
I32 = jnp.int32
EVENTS = 512
OWNERS = 128
VMEM_LIMIT = 56 * 1024 * 1024
MESH = pl.DeviceIdType.MESH


def iota(shape, dim):
    return lax.broadcasted_iota(I32, shape, dim)


def dot(a, b, ca=1, cb=0):
    return lax.dot_general(a, b, (((ca,), (cb,)), ((), ())), preferred_element_type=F32)


def bdot(a, b, ca, cb):
    return lax.dot_general(a, b, (((ca,), (cb,)), ((0,), (0,))), preferred_element_type=F32)


def half_turn(x):
    return pltpu.roll(x, 64, x.ndim - 1)


def low_lanes(shape):
    return iota(shape, len(shape) - 1) % 128 < 64


def one_hot(flag):
    return jnp.where(flag, 1.0, 0.0).astype(BF)


def prep_kernel(dig_ref, arrived_ref, slot_row_ref, slot_col_ref, message, stage, send_sem, recv_sem):
    dp = lax.axis_index("dp")
    cores = lax.axis_index("cores")
    barrier = pltpu.get_barrier_semaphore()
    row_mates = [(lax.rem(cores + i, 8), (dp, lax.rem(cores + i, 8))) for i in range(1, 8)]
    column_mates = [(lax.rem(dp + i, 16), (lax.rem(dp + i, 16), cores)) for i in range(1, 16)]
    for _, who in row_mates + column_mates:
        pl.semaphore_signal(barrier, inc=1, device_id=who, device_id_type=MESH)
    digits = dig_ref[...]
    padded = jnp.concatenate([digits, jnp.zeros((5, EVENTS), I32)], axis=0).astype(F32)
    cols = jnp.transpose(padded).astype(I32)
    owner_row = digits[1:2, :] >> 2
    owner_col = cols[:, 1:2] >> 2
    same = owner_row == owner_col
    sub = iota((EVENTS, EVENTS), 0)
    lane = iota((EVENTS, EVENTS), 1)
    rank_col = jnp.sum(jnp.where(same & (lane < sub), 1.0, 0.0), axis=1, keepdims=True).astype(I32)
    rank_row = jnp.sum(jnp.where(same & (sub < lane), 1.0, 0.0), axis=0, keepdims=True).astype(I32)
    slot_row_ref[...] = jnp.broadcast_to(rank_row * OWNERS + owner_row, (8, EVENTS))
    slot_col_ref[...] = jnp.broadcast_to(rank_col * OWNERS + owner_col, (EVENTS, 128))
    place = iota((EVENTS, 128), 1)
    inner = place % 32
    value = jnp.where(inner < 8, cols[:, 0:1], jnp.where(inner < 16, cols[:, 1:2], cols[:, 2:3])) + 1
    part = jnp.where(place < 32, value >> 4, value & 15)
    ok = (inner % 8 == rank_col) & (inner < 24) & (place < 64)
    table = jnp.where(ok, part, 0).astype(F32).astype(BF)
    pick = one_hot(iota((OWNERS, EVENTS), 0) == (owner_row & 7) * 16 + (owner_row >> 3))
    sums = dot(pick, table)
    whole = sums * 16.0 + pltpu.roll(sums, 96, 1)
    whole = jnp.where(iota((OWNERS, 128), 1) < 24, whole, 0.0).astype(I32)
    message[...] = whole.reshape(8, 16, 1, 128)
    pl.semaphore_wait(barrier, 22)

    def start(number, src, dst, who):
        copy = pltpu.make_async_remote_copy(
            src_ref=src,
            dst_ref=dst,
            send_sem=send_sem.at[number],
            recv_sem=recv_sem.at[number],
            device_id=who,
            device_id_type=MESH,
        )
        copy.start()
        return copy

    first = [start(n, message.at[c], stage.at[cores], who) for n, (c, who) in enumerate(row_mates)]
    stage[cores] = message[cores]
    for copy in first:
        copy.wait_recv()
    second = [
        start(7 + n, stage.at[:, d], arrived_ref.at[dp], who) for n, (d, who) in enumerate(column_mates)
    ]
    arrived_ref[dp] = stage[:, dp]
    for copy in second:
        copy.wait_recv()
    for copy in first + second:
        copy.wait_send()


def prep(digits):
    return pl.pallas_call(
        prep_kernel,
        out_shape=(
            jax.ShapeDtypeStruct((16, 8, 1, 128), I32),
            jax.ShapeDtypeStruct((8, EVENTS), I32),
            jax.ShapeDtypeStruct((EVENTS, 128), I32),
        ),
        scratch_shapes=[
            pltpu.VMEM((8, 16, 1, 128), I32),
            pltpu.VMEM((8, 16, 1, 128), I32),
            pltpu.SemaphoreType.DMA((22,)),
            pltpu.SemaphoreType.DMA((22,)),
        ],
        compiler_params=pltpu.CompilerParams(
            collective_id=1, has_side_effects=True, vmem_limit_bytes=16 * 1024 * 1024
        ),
        name="prep",
    )(digits)


def index_columns(arrived, half):
    lane = iota((OWNERS, 128), 1)
    out = []
    for digit in range(3):
        parts = []
        for t in range(4):
            mine = lane == digit * 8 + half * 4 + t
            parts.append(jnp.sum(jnp.where(mine, arrived, 0).astype(F32), axis=1, keepdims=True))
        out.append(jnp.concatenate(parts, axis=0).astype(I32) - 1)
    return out


def slice_masks(middle_col):
    local = jnp.where(middle_col < 0, -1, middle_col & 3)
    group = iota((512, 128), 1) // 64
    return local == group, local == group + 2


def build_kernel(arrived_ref, first_ref, middle_ref, last_ref, built_ref, spread_ref, part_ref, lt_ref, fs, ps, ls):
    half = pl.program_id(0)
    arrived = arrived_ref[...].reshape(OWNERS, 128)
    first_col, middle_col, last_col = index_columns(arrived, half)
    low = low_lanes((128, 128))
    rows = dot(one_hot(first_col == iota((512, 2048), 1)), first_ref[...])
    mask0, mask1 = slice_masks(middle_col)
    for t in range(4):
        m0 = mask0[t * 128 : (t + 1) * 128]
        m1 = mask1[t * 128 : (t + 1) * 128]
        for pair in range(4):
            x = rows[t * 128 : (t + 1) * 128, pair * 128 : (pair + 1) * 128]
            turned = half_turn(x)
            for odd in range(2):
                both = jnp.where(low, turned, x) if odd else jnp.where(low, x, turned)
                at = pl.ds(t * 1024 + pair * 2 + odd, 128, stride=8)
                fs[0, at, :] = jnp.where(m0, both, 0.0)
                fs[1, at, :] = jnp.where(m1, both, 0.0)
    source = iota((512, 512), 0)
    perm = one_hot(iota((512, 512), 1) == (source % 8) * 64 + source // 8)
    rows = dot(one_hot(last_col == iota((512, 1024), 1)), last_ref[...]).astype(BF)
    rows = dot(rows, perm)
    for t in range(4):
        for pair in range(4):
            x = rows[t * 128 : (t + 1) * 128, pair * 128 : (pair + 1) * 128]
            turned = half_turn(x)
            for odd in range(2):
                both = jnp.where(low, turned, x) if odd else jnp.where(low, x, turned)
                keep = jnp.where(low, 0.0, both) if t % 2 else jnp.where(low, both, 0.0)
                ls[t // 2, pl.ds((t % 2) * 8 + pair * 2 + odd, 128, stride=16), :] = keep

    def spread_step(i, carry):
        at = pl.ds(pl.multiple_of(i * 512, 512), 512)
        spread_ref[at, 0:128] = fs[0, at, :].astype(BF)
        spread_ref[at, 128:256] = fs[1, at, :].astype(BF)
        ps[at, :] = dot(spread_ref[at, :], middle_ref[...])
        return carry

    lax.fori_loop(0, 8, spread_step, 0)

    group = 128
    low = low_lanes((group * 8, 128))

    def combine(i, carry):
        srcs = pl.ds(pl.multiple_of(i * group, group), group)
        for pair in range(4):
            lanes = slice(pair * 128, (pair + 1) * 128)
            v = [ps[pl.ds(pl.multiple_of(t * 1024 + i * group * 8, 8), group * 8), lanes] for t in range(4)]
            w = [half_turn(x) for x in v]
            for side in range(2):
                v0, v1 = v[2 * side], v[2 * side + 1]
                w0, w1 = w[2 * side], w[2 * side + 1]
                even = jnp.where(low, v0, w1).reshape(group, 8, 128)
                odd = jnp.where(low, w0, v1).reshape(group, 8, 128)
                part_ref[srcs, pair * 16 : (pair + 1) * 16, side * 128 : (side + 1) * 128] = jnp.concatenate(
                    [even, odd], axis=1
                ).astype(BF)
        wide = pl.ds(pl.multiple_of(i * group * 16, group * 16), group * 16)
        zero = jnp.zeros((group, 16, 128), BF)
        lt_ref[srcs, 0:16, 0:128] = ls[0, wide, :].reshape(group, 16, 128).astype(BF)
        lt_ref[srcs, 0:16, 128:256] = zero
        lt_ref[srcs, 16:32, 0:128] = zero
        lt_ref[srcs, 16:32, 128:256] = ls[1, wide, :].reshape(group, 16, 128).astype(BF)
        out = bdot(lt_ref[srcs], part_ref[srcs], 2, 2)
        tile = jnp.concatenate([out[:, 0:16, :], out[:, 16:32, :]], axis=2)
        built_ref[srcs, 0] = tile.astype(BF)
        return carry

    lax.fori_loop(0, OWNERS // group, combine, 0)


def build(arrived, first_core, middle_core, last_core):
    return pl.pallas_call(
        build_kernel,
        grid=(2,),
        in_specs=[
            pl.BlockSpec((OWNERS, 1, 128), lambda h: (0, 0, 0)),
            pl.BlockSpec((2048, 512), lambda h: (0, 0)),
            pl.BlockSpec((256, 512), lambda h: (0, 0)),
            pl.BlockSpec((1024, 512), lambda h: (0, 0)),
        ],
        out_specs=(
            pl.BlockSpec((OWNERS, 1, 16, 128), lambda h: (0, h, 0, 0)),
            pl.BlockSpec((4096, 256), lambda h: (h, 0)),
            pl.BlockSpec((OWNERS, 64, 256), lambda h: (h, 0, 0)),
            pl.BlockSpec((OWNERS, 32, 256), lambda h: (h, 0, 0)),
        ),
        out_shape=(
            jax.ShapeDtypeStruct((OWNERS, 2, 16, 128), BF),
            jax.ShapeDtypeStruct((8192, 256), BF),
            jax.ShapeDtypeStruct((2 * OWNERS, 64, 256), BF),
            jax.ShapeDtypeStruct((2 * OWNERS, 32, 256), BF),
        ),
        scratch_shapes=[
            pltpu.VMEM((2, 4096, 128), F32),
            pltpu.VMEM((4096, 512), F32),
            pltpu.VMEM((2, 2048, 128), F32),
        ],
        compiler_params=pltpu.CompilerParams(vmem_limit_bytes=46 * 1024 * 1024),
        name="build",
    )(arrived, first_core, middle_core, last_core)


def sigmoid(x):
    return 0.5 * jnp.tanh(0.5 * x) + 0.5


def norm_stats(x):
    center = x - jnp.mean(x, axis=-1, keepdims=True)
    spread = jnp.mean(center * center, axis=-1, keepdims=True)
    scale = lax.rsqrt(spread + 1e-05)
    return center * scale, scale


def norm_grad(ct, y, scale):
    return scale * (ct - jnp.mean(ct, axis=-1, keepdims=True) - y * jnp.mean(ct * y, axis=-1, keepdims=True))


def layer_kernel(
    recv_ref, slot_row_ref, slot_col_ref, proj_ref, out_ref, grad_ref,
    rows_ref, sent_ref, dproj_ref, dout_ref,
    tiles, slots, emb, normed, y_in, z, act, mixed, y_mid, gated, dz, dmixed, work, work_v, work_k, sc_in,
):
    low = low_lanes((128, 128))
    step = 256
    tall = 512

    def widen(i, carry):
        srcs = pl.ds(pl.multiple_of(i * 32, 32), 32)
        tiles[pl.ds(pl.multiple_of(i * 1024, 1024), 1024), :] = recv_ref[srcs].reshape(1024, 128).astype(F32)
        return carry

    lax.fori_loop(0, 4, widen, 0)
    for half in range(2):
        for tlo in range(2):
            for pair in range(4):
                base = half * 16 + tlo * 8 + pair * 2
                y0 = tiles[pl.ds(base, 128, stride=32), :]
                y1 = tiles[pl.ds(base + 1, 128, stride=32), :]
                lanes = slice(pair * 128, (pair + 1) * 128)
                k0 = half * 4 + tlo
                slots[k0 * 128 : (k0 + 1) * 128, lanes] = jnp.where(low, y0, half_turn(y1)).astype(BF)
                k1 = k0 + 2
                slots[k1 * 128 : (k1 + 1) * 128, lanes] = jnp.where(low, half_turn(y0), y1).astype(BF)
    source = iota((512, 512), 0)
    target = iota((512, 512), 1)
    flip = one_hot(target == (source % 8) * 64 + ((source // 8) % 8) * 8 + source // 64)
    pick = one_hot(slot_col_ref[:, 0:1] == iota((EVENTS, 1024), 1))
    emb[...] = dot(dot(pick, slots[...]).astype(BF), flip)

    def project(i, carry):
        at = pl.ds(pl.multiple_of(i * tall, tall), tall)
        y, scale = norm_stats(emb[at, :])
        y_in[at, :] = y
        sc_in[at, :] = jnp.broadcast_to(scale, (tall, 128))
        normed[at, :] = y.astype(BF)
        for block in range(4):
            lanes = slice(block * 512, (block + 1) * 512)
            value = dot(normed[at, :], proj_ref[:, lanes])
            z[at, lanes] = value
            act[at, lanes] = (value * sigmoid(value)).astype(BF)
        return carry

    lax.fori_loop(0, EVENTS // tall, project, 0)
    scaling = 1.0 / math.sqrt(128.0)

    def scores_of(head, block):
        end = (block + 1) * step
        q = act[block * step : end, pl.ds(pl.multiple_of(1024 + head * 128, 128), 128)]
        k = act[0:end, pl.ds(pl.multiple_of(1536 + head * 128, 128), 128)]
        s = dot(q, k, 1, 1) * scaling
        causal = block * step + iota((step, end), 0) >= iota((step, end), 1)
        return s, causal

    def attend(head, carry):
        cols = pl.ds(pl.multiple_of(head * 128, 128), 128)
        for block in range(2):
            end = (block + 1) * step
            s, causal = scores_of(head, block)
            weights = jnp.where(causal, s * sigmoid(s), 0.0).astype(BF)
            v = act[0:end, pl.ds(pl.multiple_of(512 + head * 128, 128), 128)]
            mixed[block * step : end, cols] = dot(weights, v)
        return carry

    lax.fori_loop(0, 4, attend, 0)

    def finish(i, carry):
        at = pl.ds(pl.multiple_of(i * tall, tall), tall)
        y, scale = norm_stats(mixed[at, :])
        u = act[at, 0:512].astype(F32)
        gate = (y * u).astype(BF)
        gated[at, :] = gate
        g = grad_ref[at, :]
        rows_ref[at, :] = (dot(gate, out_ref[...]) + emb[at, :]).astype(BF)
        d_gate = dot(g, out_ref[...], 1, 1).astype(BF).astype(F32)
        d_u = (d_gate * y).astype(BF).astype(F32)
        zu = z[at, 0:512]
        sig = sigmoid(zu)
        dz[at, 0:512] = (d_u * (sig * (1.0 + zu * (1.0 - sig)))).astype(BF)
        dmixed[at, :] = norm_grad(d_gate * u, y, scale).astype(BF)
        return carry

    lax.fori_loop(0, EVENTS // tall, finish, 0)
    dout_ref[...] = dot(gated[...], grad_ref[...], 0, 0).astype(BF)

    def attend_grad(head, carry):
        cols = pl.ds(pl.multiple_of(head * 128, 128), 128)
        vcols = pl.ds(pl.multiple_of(512 + head * 128, 128), 128)
        qcols = pl.ds(pl.multiple_of(1024 + head * 128, 128), 128)
        kcols = pl.ds(pl.multiple_of(1536 + head * 128, 128), 128)
        for block in (1, 0):
            end = (block + 1) * step
            rows = slice(block * step, end)
            s, causal = scores_of(head, block)
            sig = sigmoid(s)
            weights = jnp.where(causal, s * sig, 0.0).astype(BF)
            dm = dmixed[rows, cols]
            d_w = dot(dm, act[0:end, vcols], 1, 1).astype(BF).astype(F32)
            d_s = jnp.where(causal, d_w * (sig * (1.0 + s * (1.0 - sig))) * scaling, 0.0).astype(BF)
            v_part = dot(weights, dm, 0, 0)
            k_part = dot(d_s, act[rows, qcols], 0, 0)
            if block == 1:
                work_v[...] = v_part
                work_k[...] = k_part
            else:
                work_v[0:end, :] += v_part
                work_k[0:end, :] += k_part
            work[rows, :] = dot(d_s, act[0:end, kcols])

        def through(ct, where):
            value = z[:, where]
            sig = sigmoid(value)
            dz[:, where] = (ct.astype(BF).astype(F32) * (sig * (1.0 + value * (1.0 - sig)))).astype(BF)

        through(work[...], qcols)
        through(work_v[...], vcols)
        through(work_k[...], kcols)
        return carry

    lax.fori_loop(0, 4, attend_grad, 0)

    for block in range(4):
        lanes = slice(block * 512, (block + 1) * 512)
        dproj_ref[lanes, :] = dot(normed[...], dz[:, lanes], 0, 0).astype(BF)

    back = one_hot(source == (target % 8) * 64 + ((target // 8) % 8) * 8 + target // 64)

    def close(i, carry):
        at = pl.ds(pl.multiple_of(i * tall, tall), tall)
        d_normed = dot(dz[at, :], proj_ref[...], 1, 1).astype(BF).astype(F32)
        d_rows = norm_grad(d_normed, y_in[at, :], sc_in[at, 0:1]) + grad_ref[at, :].astype(F32)
        gated[at, :] = d_rows.astype(BF)
        return carry

    lax.fori_loop(0, EVENTS // tall, close, 0)
    turned = dot(gated[...], back).astype(BF)
    for half in range(2):
        for tlo in range(2):
            found = []
            for thi in range(2):
                k = half * 4 + thi * 2 + tlo
                place = one_hot(iota((128, EVENTS), 0) + k * 128 == slot_row_ref[0:1, :])
                found.append(dot(place, turned))
            for pair in range(4):
                lanes = slice(pair * 128, (pair + 1) * 128)
                x0, x1 = found[0][:, lanes], found[1][:, lanes]
                base = half * 16 + tlo * 8 + pair * 2
                tiles[pl.ds(base, 128, stride=32), :] = jnp.where(low, x0, half_turn(x1))
                tiles[pl.ds(base + 1, 128, stride=32), :] = jnp.where(low, half_turn(x0), x1)

    def narrow(i, carry):
        srcs = pl.ds(pl.multiple_of(i * 32, 32), 32)
        sent_ref[srcs] = tiles[pl.ds(pl.multiple_of(i * 1024, 1024), 1024), :].astype(BF).reshape(32, 2, 16, 128)
        return carry

    lax.fori_loop(0, 4, narrow, 0)


def layer(recv, slot_row, slot_col, w_proj, w_out, layer_grad):
    vm = pltpu.VMEM
    return pl.pallas_call(
        layer_kernel,
        out_shape=(
            jax.ShapeDtypeStruct((EVENTS, 512), BF),
            jax.ShapeDtypeStruct((OWNERS, 2, 16, 128), BF),
            jax.ShapeDtypeStruct((2048, 512), BF),
            jax.ShapeDtypeStruct((512, 512), BF),
        ),
        scratch_shapes=[
            vm((4096, 128), F32),
            vm((1024, 512), BF),
            vm((EVENTS, 512), F32),
            vm((EVENTS, 512), BF),
            vm((EVENTS, 512), F32),
            vm((EVENTS, 2048), F32),
            vm((EVENTS, 2048), BF),
            vm((EVENTS, 512), F32),
            vm((EVENTS, 512), F32),
            vm((EVENTS, 512), BF),
            vm((EVENTS, 2048), BF),
            vm((EVENTS, 512), BF),
            vm((EVENTS, 128), F32),
            vm((EVENTS, 128), F32),
            vm((EVENTS, 128), F32),
            vm((EVENTS, 128), F32),
        ],
        compiler_params=pltpu.CompilerParams(vmem_limit_bytes=34 * 1024 * 1024),
        name="layer",
    )(recv, slot_row, slot_col, w_proj, w_out, layer_grad)


def core_grad_kernel(
    arrived_ref, tile_ref, spread_ref, part_ref, lt_ref, middle_ref,
    first_out, middle_out, last_out,
    flipped, pg, ls, ss, fterm, lterm,
):
    half = pl.program_id(0)
    arrived = arrived_ref[...].reshape(OWNERS, 128)
    flipped[...] = jnp.transpose(arrived.astype(F32)).astype(I32) - 1
    _, middle_col, _ = index_columns(arrived, half)
    mask0, mask1 = slice_masks(middle_col)
    group = 128
    low = low_lanes((group, 8, 128))
    own = (iota((group, 16, 128), 1) // 8) == (iota((group, 16, 128), 2) // 64)

    def events(i, carry):
        srcs = pl.ds(pl.multiple_of(i * group, group), group)
        tile = tile_ref[srcs, 0]
        g = jnp.concatenate([tile[:, :, 0:64], tile[:, :, 64:128]], axis=1)
        wide = pl.ds(pl.multiple_of(i * group * 16, group * 16), group * 16)
        terms = bdot(g, part_ref[srcs], 2, 1)
        for side in range(2):
            x = terms[:, side * 16 : (side + 1) * 16, side * 128 : (side + 1) * 128]
            x = jnp.where(own, x, 0.0).reshape(group * 16, 128)
            ls[side, wide, :] = x + half_turn(x)
        grads = bdot(g, lt_ref[srcs], 1, 1)
        for pair in range(4):
            lanes = slice(pair * 128, (pair + 1) * 128)
            for side in range(2):
                even = grads[:, pair * 16 : pair * 16 + 8, side * 128 : (side + 1) * 128]
                odd = grads[:, pair * 16 + 8 : pair * 16 + 16, side * 128 : (side + 1) * 128]
                v0 = jnp.where(low, even, half_turn(odd))
                v1 = jnp.where(low, half_turn(even), odd)
                for t, v in ((2 * side, v0), (2 * side + 1, v1)):
                    at = pl.ds(pl.multiple_of(t * 1024 + i * group * 8, group * 8), group * 8)
                    pg[at, lanes] = v.reshape(group * 8, 128).astype(BF)
        return carry

    lax.fori_loop(0, OWNERS // group, events, 0)
    low = low_lanes((128, 128))
    middle_part = jnp.zeros((256, 512), F32)
    for t in range(4):
        at = slice(t * 1024, (t + 1) * 1024)
        middle_part += dot(spread_ref[at, :], pg[at, :], 0, 0)
        back = dot(pg[at, :], middle_ref[...], 1, 1)
        ss[0] = back[:, 0:128]
        ss[1] = back[:, 128:256]
        rows = slice(t * 128, (t + 1) * 128)
        keep = pl.ds(pl.multiple_of(half * 512 + t * 128, 128), 128)
        m0, m1 = mask0[rows], mask1[rows]
        for pair in range(4):
            lanes = slice(pair * 128, (pair + 1) * 128)
            found = []
            for odd in range(2):
                where = pl.ds(pair * 2 + odd, 128, stride=8)
                x = jnp.where(m0, ss[0, where, :], 0.0) + jnp.where(m1, ss[1, where, :], 0.0)
                found.append(x + half_turn(x))
            fterm[keep, lanes] = jnp.where(low, found[0], found[1]).astype(BF)
            base = (t % 2) * 8 + pair * 2
            y0 = ls[t // 2, pl.ds(base, 128, stride=16), :]
            y1 = ls[t // 2, pl.ds(base + 1, 128, stride=16), :]
            lterm[keep, lanes] = jnp.where(low, y0, y1).astype(BF)

    source = iota((512, 512), 0)
    perm = one_hot(iota((512, 512), 1) == (source % 64) * 8 + source // 64)
    done = pl.ds(pl.multiple_of(half * 512, 512), 512)
    lterm[done, :] = dot(lterm[done, :], perm).astype(BF)

    def index_row(digit):
        return jnp.concatenate([flipped[digit * 8 + t : digit * 8 + t + 1, :] for t in range(8)], axis=1)

    @pl.when(half == 0)
    def _():
        middle_out[...] = middle_part

    @pl.when(half == 1)
    def _():
        middle_out[...] += middle_part

    @pl.when(half == 1)
    def _():
        first_row = index_row(0)
        last_row = index_row(2)

        def scatter_first(i, carry):
            at = pl.ds(pl.multiple_of(i * 256, 256), 256)
            place = one_hot(iota((256, 1024), 0) + i * 256 == first_row)
            first_out[at, :] = dot(place, fterm[...]).astype(BF)
            return carry

        def scatter_last(i, carry):
            at = pl.ds(pl.multiple_of(i * 256, 256), 256)
            place = one_hot(iota((256, 1024), 0) + i * 256 == last_row)
            last_out[at, :] = dot(place, lterm[...]).astype(BF)
            return carry

        lax.fori_loop(0, 8, scatter_first, 0)
        lax.fori_loop(0, 4, scatter_last, 0)


def core_grads(arrived, tiles, spread, part, lt, middle_core):
    vm = pltpu.VMEM
    return pl.pallas_call(
        core_grad_kernel,
        grid=(2,),
        in_specs=[
            pl.BlockSpec((OWNERS, 1, 128), lambda h: (0, 0, 0)),
            pl.BlockSpec((OWNERS, 1, 16, 128), lambda h: (0, h, 0, 0)),
            pl.BlockSpec((4096, 256), lambda h: (h, 0)),
            pl.BlockSpec((OWNERS, 64, 256), lambda h: (h, 0, 0)),
            pl.BlockSpec((OWNERS, 32, 256), lambda h: (h, 0, 0)),
            pl.BlockSpec((256, 512), lambda h: (0, 0)),
        ],
        out_specs=(
            pl.BlockSpec((2048, 512), lambda h: (0, 0)),
            pl.BlockSpec((256, 512), lambda h: (0, 0)),
            pl.BlockSpec((1024, 512), lambda h: (0, 0)),
        ),
        out_shape=(
            jax.ShapeDtypeStruct((2048, 512), BF),
            jax.ShapeDtypeStruct((256, 512), F32),
            jax.ShapeDtypeStruct((1024, 512), BF),
        ),
        scratch_shapes=[
            vm((128, 128), I32),
            vm((4096, 512), BF),
            vm((2, 2048, 128), F32),
            vm((2, 1024, 128), F32),
            vm((1024, 512), BF),
            vm((1024, 512), BF),
        ],
        compiler_params=pltpu.CompilerParams(vmem_limit_bytes=46 * 1024 * 1024),
        name="core_grads",
    )(arrived, tiles, spread, part, lt, middle_core)


class Place:
    def __init__(self):
        dp = lax.axis_index("dp")
        cores = lax.axis_index("cores")
        self.at = (cores // 2, dp // 4, lax.rem(dp, 4))
        self.core = lax.rem(cores, 2)

    def along(self, dim, offset):
        at = list(self.at)
        at[dim] = lax.rem(at[dim] + offset, 4)
        return at[dim], (at[1] * 4 + at[2], at[0] * 2 + self.core)

    def sibling(self):
        x, y, z = self.at
        return (y * 4 + z, x * 2 + 1 - self.core)


ORDERS = ((0, 1, 2), (1, 2, 0), (2, 0, 1))
SIZES = (256, 64, 16)


def reduce_kernel(
    first_ref, proj_ref, last_ref, out_ref,
    total0, total1, total2,
    rest, pair0, pair1, pair2, sum0, sum1, sum2,
    got00, got01, got02, got10, got11, got12, got20, got21, got22,
    halves0, halves1, halves2, send_sem, recv_sem,
):
    place = Place()
    core = place.core
    barrier = pltpu.get_barrier_semaphore()
    partners = [place.sibling()] + [place.along(d, o)[1] for d in range(3) for o in (1, 2, 3)]
    for who in partners:
        pl.semaphore_signal(barrier, inc=1, device_id=who, device_id_type=MESH)
    for block in range(12):
        row = (block // 3) * 512
        lanes = slice((block % 3) * 128, (block % 3 + 1) * 128)
        if block < 8:
            value = last_ref[(block // 4) * 512 : (block // 4 + 1) * 512, (block % 4) * 128 : (block % 4 + 1) * 128]
        else:
            value = out_ref[:, (block % 4) * 128 : (block % 4 + 1) * 128]
        rest[row : row + 512, lanes] = value
    source = (first_ref, proj_ref, rest)
    total = (total0, total1, total2)
    pair = (pair0, pair1, pair2)
    sums = (sum0, sum1, sum2)
    got = ((got00, got01, got02), (got10, got11, got12), (got20, got21, got22))
    halves = (halves0, halves1, halves2)
    pl.semaphore_wait(barrier, len(partners))
    pending = []

    def start(part, stage, slot, src, dst, who):
        copy = pltpu.make_async_remote_copy(
            src_ref=src,
            dst_ref=dst,
            send_sem=send_sem.at[part, stage, slot],
            recv_sem=recv_sem.at[part, stage, slot],
            device_id=who,
            device_id_type=MESH,
        )
        copy.start()
        pending.append(copy)
        return copy

    def rows(start_row, size):
        return pl.ds(pl.multiple_of(start_row, 16), size)

    base = [core * 1024 for _ in range(3)]
    flight = {}
    for slot in (2, 1, 3, 0):
        for part in range(3):
            quarter, _ = place.along(ORDERS[part][0], slot)
            flight[part, slot] = start(
                part, 0, slot,
                source[part].at[rows((1 - core) * 1024 + quarter * 256, 256)],
                pair[part].at[rows(quarter * 256, 256)],
                place.sibling(),
            )
    moving = {}

    def pair_sum(part, slot):
        quarter, _ = place.along(ORDERS[part][0], slot)
        flight[part, slot].wait_recv()
        at = rows(quarter * 256, 256)
        mine = source[part][rows(core * 1024 + quarter * 256, 256), :].astype(F32)
        sums[part][at, :] = (mine + pair[part][at, :].astype(F32)).astype(BF)
        return quarter * 256

    for part in range(3):
        at = pair_sum(part, 2)
        for slot, lead, way in ((0, 0, 1), (2, 128, 3)):
            who = place.along(ORDERS[part][0], way)[1]
            src = sums[part].at[rows(at + lead, 128)]
            moving[part, slot] = start(part, 1, slot, src, halves[part].at[slot // 2], who)
    for way in (1, 3):
        for part in range(3):
            at = pair_sum(part, way)
            slot, lead = (0, 0) if way == 1 else (2, 128)
            moving[part, slot].wait_recv()
            piece = rows(at + lead, 128)
            more = halves[part][slot // 2].astype(F32)
            sums[part][piece, :] = (sums[part][piece, :].astype(F32) + more).astype(BF)
            who = place.along(ORDERS[part][0], way)[1]
            src = sums[part].at[rows(at, 256)]
            moving[part, way] = start(part, 1, way, src, got[part][0].at[way // 2], who)
    for part in range(3):
        pair_sum(part, 0)
    offset = [0, 0, 0]
    for level in range(3):
        size = SIZES[level]
        following = {}
        for part in range(3):
            mine = place.at[ORDERS[part][level]]
            offset[part] = offset[part] + mine * size
            ways = (1, 3) if level == 0 else (1, 2, 3)
            for slot in ways:
                moving[part, slot].wait_recv()
            at = rows(offset[part], size)
            value = sums[part][at, :].astype(F32)
            for slot in range(len(ways)):
                value = value + got[part][level][slot].astype(F32)
            if level < 2:
                sums[part][at, :] = value.astype(BF)
                for slot in (1, 2, 3):
                    quarter, who = place.along(ORDERS[part][level + 1], slot)
                    src = sums[part].at[rows(offset[part] + quarter * SIZES[level + 1], SIZES[level + 1])]
                    following[part, slot] = start(part, level + 2, slot, src, got[part][level + 1].at[slot - 1], who)
            else:
                where = rows(core * 1024 + offset[part], size)
                total[part][where, :] = value.astype(BF)
                for slot in (1, 2, 3):
                    who = place.along(ORDERS[part][2], slot)[1]
                    ref = total[part].at[where]
                    following[part, slot] = start(part, 4, slot, ref, ref, who)
        moving = following
    final = []
    for level in (1, 0):
        following = {}
        for part in range(3):
            mine = place.at[ORDERS[part][level + 1]]
            offset[part] = offset[part] - mine * SIZES[level + 1]
            for slot in (1, 2, 3):
                moving[part, slot].wait_recv()
            where = rows(core * 1024 + offset[part], SIZES[level])
            ref = total[part].at[where]
            for slot in (1, 3) if level == 0 else (1, 2, 3):
                who = place.along(ORDERS[part][level], slot)[1]
                following[part, slot] = start(part, 6 - level, slot, ref, ref, who)
            if level == 0:
                final.append(start(part, 7, 0, ref, ref, place.sibling()))
        moving = following

    def piece_of(part, way, lead, size):
        quarter = place.along(ORDERS[part][0], way)[0]
        return total[part].at[rows(core * 1024 + quarter * 256 + lead, size)]

    for way in (1, 3):
        for part in range(3):
            moving[part, way].wait_recv()
            slot, lead = (0, 0) if way == 1 else (2, 128)
            ref = piece_of(part, 4 - way, lead, 128)
            who = place.along(ORDERS[part][0], way)[1]
            moving[part, slot] = start(part, 6, slot, ref, ref, who)
            ref = piece_of(part, 4 - way, 0, 256)
            final.append(start(part, 7, way, ref, ref, place.sibling()))
    for part in range(3):
        moving[part, 0].wait_recv()
        moving[part, 2].wait_recv()
        ref = piece_of(part, 2, 0, 256)
        final.append(start(part, 7, 2, ref, ref, place.sibling()))
    for copy in final:
        copy.wait_recv()
    for copy in pending:
        copy.wait_send()


def reduce_all(first_part, proj_grad, last_part, out_grad, ident):
    vm = pltpu.VMEM
    widths = (512, 512, 384)
    return pl.pallas_call(
        reduce_kernel,
        out_shape=tuple(jax.ShapeDtypeStruct((2048, w), BF) for w in widths),
        in_specs=[pl.BlockSpec(memory_space=vm)] * 4,
        out_specs=tuple(pl.BlockSpec(memory_space=vm) for _ in widths),
        scratch_shapes=[vm((2048, 384), BF)]
        + [vm((1024, w), BF) for w in widths]
        + [vm((1024, w), BF) for w in widths]
        + [vm((3, size, w), BF) for w in widths for size in SIZES]
        + [vm((2, 128, w), BF) for w in widths]
        + [pltpu.SemaphoreType.DMA((3, 8, 4))] * 2,
        compiler_params=pltpu.CompilerParams(
            collective_id=ident, has_side_effects=True, vmem_limit_bytes=28 * 1024 * 1024
        ),
        name="reduce_all",
    )(first_part, proj_grad, last_part, out_grad)


def widen_kernel(a_ref, b_ref, c_ref, first_ref, last_ref, proj_ref, out_ref):
    first_ref[...] = a_ref[...].astype(F32)
    for block in range(4):
        lanes = slice(block * 512, (block + 1) * 512)
        proj_ref[:, lanes] = b_ref[block].astype(F32)
    for block in range(12):
        value = c_ref[block // 3, :, (block % 3) * 128 : (block % 3 + 1) * 128].astype(F32)
        lanes = slice((block % 4) * 128, (block % 4 + 1) * 128)
        if block < 8:
            last_ref[block // 4, :, lanes] = value
        else:
            out_ref[:, lanes] = value


def widen(a, b, c):
    steps = 8
    rows = 512 // steps
    first, last, proj, out = pl.pallas_call(
        widen_kernel,
        grid=(steps,),
        in_specs=[
            pl.BlockSpec((4 * rows, 512), lambda i: (i, 0)),
            pl.BlockSpec((4, rows, 512), lambda i: (0, i, 0)),
            pl.BlockSpec((4, rows, 384), lambda i: (0, i, 0)),
        ],
        out_specs=(
            pl.BlockSpec((4 * rows, 512), lambda i: (i, 0)),
            pl.BlockSpec((2, rows, 512), lambda i: (0, i, 0)),
            pl.BlockSpec((rows, 2048), lambda i: (i, 0)),
            pl.BlockSpec((rows, 512), lambda i: (i, 0)),
        ),
        out_shape=(
            jax.ShapeDtypeStruct((2048, 512), F32),
            jax.ShapeDtypeStruct((2, 512, 512), F32),
            jax.ShapeDtypeStruct((512, 2048), F32),
            jax.ShapeDtypeStruct((512, 512), F32),
        ),
        compiler_params=pltpu.CompilerParams(vmem_limit_bytes=20 * 1024 * 1024),
        name="widen",
    )(a, b.reshape(4, 512, 512), c.reshape(4, 512, 384))
    return first, last.reshape(1024, 512), proj, out


def exchange(x):
    return lax.all_to_all(x, AXES, split_axis=0, concat_axis=0, tiled=True)


def per_device(item_digits, first_core, middle_core, last_core, w_proj, w_out, layer_grad):
    arrived, slot_row, slot_col = prep(item_digits)
    arrived = arrived.reshape(OWNERS, 1, 128)
    built, spread, part, lt = build(arrived, first_core, middle_core, last_core)
    recv = exchange(built)
    layer_rows, sent, proj_grad, out_grad = layer(recv, slot_row, slot_col, w_proj, w_out, layer_grad)
    tiles = exchange(sent)
    first_part, grad_middle, last_part = core_grads(arrived, tiles, spread, part, lt, middle_core)
    totals = reduce_all(first_part, proj_grad, last_part, out_grad, 2)
    grad_first, grad_last, proj_total, out_total = widen(*totals)
    return (layer_rows, grad_first, grad_middle, grad_last, proj_total, out_total)


def solution(mesh):
    return jax.shard_map(
        per_device,
        mesh=mesh,
        in_specs=(
            P(None, AXES),
            P(),
            P(AXES, None),
            P(),
            P(),
            P(),
            P(AXES, None),
        ),
        out_specs=(P(AXES, None), P(), P(AXES, None), P(), P(), P()),
        check_vma=False,
    )
```

```python
import functools
import math

import jax
import jax.numpy as jnp
from jax import lax
from jax.experimental import pallas as pl
from jax.experimental.pallas import tpu as pltpu
from jax.sharding import PartitionSpec as P

AXES = ("dp", "cores")
BF = jnp.bfloat16
F32 = jnp.float32
I32 = jnp.int32
EVENTS = 512
OWNERS = 128
VMEM_LIMIT = 56 * 1024 * 1024
MESH = pl.DeviceIdType.MESH


def iota(shape, dim):
    return lax.broadcasted_iota(I32, shape, dim)


def dot(a, b, ca=1, cb=0):
    return lax.dot_general(a, b, (((ca,), (cb,)), ((), ())), preferred_element_type=F32)


def bdot(a, b, ca, cb):
    return lax.dot_general(a, b, (((ca,), (cb,)), ((0,), (0,))), preferred_element_type=F32)


def half_turn(x):
    return pltpu.roll(x, 64, x.ndim - 1)


def low_lanes(shape):
    return iota(shape, len(shape) - 1) % 128 < 64


def one_hot(flag):
    return jnp.where(flag, 1.0, 0.0).astype(BF)


def prep_kernel(dig_ref, arrived_ref, slot_row_ref, slot_col_ref, message, stage, send_sem, recv_sem):
    dp = lax.axis_index("dp")
    cores = lax.axis_index("cores")
    barrier = pltpu.get_barrier_semaphore()
    row_mates = [(lax.rem(cores + i, 8), (dp, lax.rem(cores + i, 8))) for i in range(1, 8)]
    column_mates = [(lax.rem(dp + i, 16), (lax.rem(dp + i, 16), cores)) for i in range(1, 16)]
    for _, who in row_mates + column_mates:
        pl.semaphore_signal(barrier, inc=1, device_id=who, device_id_type=MESH)
    digits = dig_ref[...]
    padded = jnp.concatenate([digits, jnp.zeros((5, EVENTS), I32)], axis=0).astype(F32)
    cols = jnp.transpose(padded).astype(I32)
    owner_row = digits[1:2, :] >> 2
    owner_col = cols[:, 1:2] >> 2
    same = owner_row == owner_col
    sub = iota((EVENTS, EVENTS), 0)
    lane = iota((EVENTS, EVENTS), 1)
    rank_col = jnp.sum(jnp.where(same & (lane < sub), 1.0, 0.0), axis=1, keepdims=True).astype(I32)
    rank_row = jnp.sum(jnp.where(same & (sub < lane), 1.0, 0.0), axis=0, keepdims=True).astype(I32)
    slot_row_ref[...] = jnp.broadcast_to(rank_row * OWNERS + owner_row, (8, EVENTS))
    slot_col_ref[...] = jnp.broadcast_to(rank_col * OWNERS + owner_col, (EVENTS, 128))
    place = iota((EVENTS, 128), 1)
    inner = place % 32
    value = jnp.where(inner < 8, cols[:, 0:1], jnp.where(inner < 16, cols[:, 1:2], cols[:, 2:3])) + 1
    part = jnp.where(place < 32, value >> 4, value & 15)
    ok = (inner % 8 == rank_col) & (inner < 24) & (place < 64)
    table = jnp.where(ok, part, 0).astype(F32).astype(BF)
    pick = one_hot(iota((OWNERS, EVENTS), 0) == (owner_row & 7) * 16 + (owner_row >> 3))
    sums = dot(pick, table)
    whole = sums * 16.0 + pltpu.roll(sums, 96, 1)
    whole = jnp.where(iota((OWNERS, 128), 1) < 24, whole, 0.0).astype(I32)
    message[...] = whole.reshape(8, 16, 1, 128)
    pl.semaphore_wait(barrier, 22)

    def start(number, src, dst, who):
        copy = pltpu.make_async_remote_copy(
            src_ref=src,
            dst_ref=dst,
            send_sem=send_sem.at[number],
            recv_sem=recv_sem.at[number],
            device_id=who,
            device_id_type=MESH,
        )
        copy.start()
        return copy

    first = [start(n, message.at[c], stage.at[cores], who) for n, (c, who) in enumerate(row_mates)]
    stage[cores] = message[cores]
    for copy in first:
        copy.wait_recv()
    second = [
        start(7 + n, stage.at[:, d], arrived_ref.at[dp], who) for n, (d, who) in enumerate(column_mates)
    ]
    arrived_ref[dp] = stage[:, dp]
    for copy in second:
        copy.wait_recv()
    for copy in first + second:
        copy.wait_send()


def prep(digits):
    return pl.pallas_call(
        prep_kernel,
        out_shape=(
            jax.ShapeDtypeStruct((16, 8, 1, 128), I32),
            jax.ShapeDtypeStruct((8, EVENTS), I32),
            jax.ShapeDtypeStruct((EVENTS, 128), I32),
        ),
        scratch_shapes=[
            pltpu.VMEM((8, 16, 1, 128), I32),
            pltpu.VMEM((8, 16, 1, 128), I32),
            pltpu.SemaphoreType.DMA((22,)),
            pltpu.SemaphoreType.DMA((22,)),
        ],
        compiler_params=pltpu.CompilerParams(
            collective_id=1, has_side_effects=True, vmem_limit_bytes=16 * 1024 * 1024
        ),
        name="prep",
    )(digits)


def index_columns(arrived, half):
    lane = iota((OWNERS, 128), 1)
    out = []
    for digit in range(3):
        parts = []
        for t in range(4):
            mine = lane == digit * 8 + half * 4 + t
            parts.append(jnp.sum(jnp.where(mine, arrived, 0).astype(F32), axis=1, keepdims=True))
        out.append(jnp.concatenate(parts, axis=0).astype(I32) - 1)
    return out


def slice_masks(middle_col):
    local = jnp.where(middle_col < 0, -1, middle_col & 3)
    group = iota((512, 128), 1) // 64
    return local == group, local == group + 2


def build_kernel(arrived_ref, first_ref, middle_ref, last_ref, built_ref, spread_ref, part_ref, lt_ref, fs, ps, ls):
    half = pl.program_id(0)
    arrived = arrived_ref[...].reshape(OWNERS, 128)
    first_col, middle_col, last_col = index_columns(arrived, half)
    low = low_lanes((128, 128))
    rows = dot(one_hot(first_col == iota((512, 2048), 1)), first_ref[...])
    mask0, mask1 = slice_masks(middle_col)
    for t in range(4):
        m0 = mask0[t * 128 : (t + 1) * 128]
        m1 = mask1[t * 128 : (t + 1) * 128]
        for pair in range(4):
            x = rows[t * 128 : (t + 1) * 128, pair * 128 : (pair + 1) * 128]
            turned = half_turn(x)
            for odd in range(2):
                both = jnp.where(low, turned, x) if odd else jnp.where(low, x, turned)
                at = pl.ds(t * 1024 + pair * 2 + odd, 128, stride=8)
                fs[0, at, :] = jnp.where(m0, both, 0.0)
                fs[1, at, :] = jnp.where(m1, both, 0.0)
    source = iota((512, 512), 0)
    perm = one_hot(iota((512, 512), 1) == (source % 8) * 64 + source // 8)
    rows = dot(one_hot(last_col == iota((512, 1024), 1)), last_ref[...]).astype(BF)
    rows = dot(rows, perm)
    for t in range(4):
        for pair in range(4):
            x = rows[t * 128 : (t + 1) * 128, pair * 128 : (pair + 1) * 128]
            turned = half_turn(x)
            for odd in range(2):
                both = jnp.where(low, turned, x) if odd else jnp.where(low, x, turned)
                keep = jnp.where(low, 0.0, both) if t % 2 else jnp.where(low, both, 0.0)
                ls[t // 2, pl.ds((t % 2) * 8 + pair * 2 + odd, 128, stride=16), :] = keep

    def spread_step(i, carry):
        at = pl.ds(pl.multiple_of(i * 512, 512), 512)
        spread_ref[at, 0:128] = fs[0, at, :].astype(BF)
        spread_ref[at, 128:256] = fs[1, at, :].astype(BF)
        ps[at, :] = dot(spread_ref[at, :], middle_ref[...])
        return carry

    lax.fori_loop(0, 8, spread_step, 0)

    group = 128
    low = low_lanes((group * 8, 128))

    def combine(i, carry):
        srcs = pl.ds(pl.multiple_of(i * group, group), group)
        for pair in range(4):
            lanes = slice(pair * 128, (pair + 1) * 128)
            v = [ps[pl.ds(pl.multiple_of(t * 1024 + i * group * 8, 8), group * 8), lanes] for t in range(4)]
            w = [half_turn(x) for x in v]
            for side in range(2):
                v0, v1 = v[2 * side], v[2 * side + 1]
                w0, w1 = w[2 * side], w[2 * side + 1]
                even = jnp.where(low, v0, w1).reshape(group, 8, 128)
                odd = jnp.where(low, w0, v1).reshape(group, 8, 128)
                part_ref[srcs, pair * 16 : (pair + 1) * 16, side * 128 : (side + 1) * 128] = jnp.concatenate(
                    [even, odd], axis=1
                ).astype(BF)
        wide = pl.ds(pl.multiple_of(i * group * 16, group * 16), group * 16)
        zero = jnp.zeros((group, 16, 128), BF)
        lt_ref[srcs, 0:16, 0:128] = ls[0, wide, :].reshape(group, 16, 128).astype(BF)
        lt_ref[srcs, 0:16, 128:256] = zero
        lt_ref[srcs, 16:32, 0:128] = zero
        lt_ref[srcs, 16:32, 128:256] = ls[1, wide, :].reshape(group, 16, 128).astype(BF)
        out = bdot(lt_ref[srcs], part_ref[srcs], 2, 2)
        tile = jnp.concatenate([out[:, 0:16, :], out[:, 16:32, :]], axis=2)
        built_ref[srcs, 0] = tile.astype(BF)
        return carry

    lax.fori_loop(0, OWNERS // group, combine, 0)


def build(arrived, first_core, middle_core, last_core):
    return pl.pallas_call(
        build_kernel,
        grid=(2,),
        in_specs=[
            pl.BlockSpec((OWNERS, 1, 128), lambda h: (0, 0, 0)),
            pl.BlockSpec((2048, 512), lambda h: (0, 0)),
            pl.BlockSpec((256, 512), lambda h: (0, 0)),
            pl.BlockSpec((1024, 512), lambda h: (0, 0)),
        ],
        out_specs=(
            pl.BlockSpec((OWNERS, 1, 16, 128), lambda h: (0, h, 0, 0)),
            pl.BlockSpec((4096, 256), lambda h: (h, 0)),
            pl.BlockSpec((OWNERS, 64, 256), lambda h: (h, 0, 0)),
            pl.BlockSpec((OWNERS, 32, 256), lambda h: (h, 0, 0)),
        ),
        out_shape=(
            jax.ShapeDtypeStruct((OWNERS, 2, 16, 128), BF),
            jax.ShapeDtypeStruct((8192, 256), BF),
            jax.ShapeDtypeStruct((2 * OWNERS, 64, 256), BF),
            jax.ShapeDtypeStruct((2 * OWNERS, 32, 256), BF),
        ),
        scratch_shapes=[
            pltpu.VMEM((2, 4096, 128), F32),
            pltpu.VMEM((4096, 512), F32),
            pltpu.VMEM((2, 2048, 128), F32),
        ],
        compiler_params=pltpu.CompilerParams(vmem_limit_bytes=46 * 1024 * 1024),
        name="build",
    )(arrived, first_core, middle_core, last_core)


def sigmoid(x):
    return 0.5 * jnp.tanh(0.5 * x) + 0.5


def norm_stats(x):
    center = x - jnp.mean(x, axis=-1, keepdims=True)
    spread = jnp.mean(center * center, axis=-1, keepdims=True)
    scale = lax.rsqrt(spread + 1e-05)
    return center * scale, scale


def norm_grad(ct, y, scale):
    return scale * (ct - jnp.mean(ct, axis=-1, keepdims=True) - y * jnp.mean(ct * y, axis=-1, keepdims=True))


def layer_kernel(
    recv_ref, slot_row_ref, slot_col_ref, proj_ref, out_ref, grad_ref,
    rows_ref, sent_ref, dproj_ref, dout_ref,
    tiles, slots, emb, normed, y_in, z, act, mixed, y_mid, gated, dz, dmixed, work, work_v, work_k, sc_in,
):
    low = low_lanes((128, 128))
    step = 256
    tall = 512

    def widen(i, carry):
        srcs = pl.ds(pl.multiple_of(i * 32, 32), 32)
        tiles[pl.ds(pl.multiple_of(i * 1024, 1024), 1024), :] = recv_ref[srcs].reshape(1024, 128).astype(F32)
        return carry

    lax.fori_loop(0, 4, widen, 0)
    for half in range(2):
        for tlo in range(2):
            for pair in range(4):
                base = half * 16 + tlo * 8 + pair * 2
                y0 = tiles[pl.ds(base, 128, stride=32), :]
                y1 = tiles[pl.ds(base + 1, 128, stride=32), :]
                lanes = slice(pair * 128, (pair + 1) * 128)
                k0 = half * 4 + tlo
                slots[k0 * 128 : (k0 + 1) * 128, lanes] = jnp.where(low, y0, half_turn(y1)).astype(BF)
                k1 = k0 + 2
                slots[k1 * 128 : (k1 + 1) * 128, lanes] = jnp.where(low, half_turn(y0), y1).astype(BF)
    source = iota((512, 512), 0)
    target = iota((512, 512), 1)
    flip = one_hot(target == (source % 8) * 64 + ((source // 8) % 8) * 8 + source // 64)
    pick = one_hot(slot_col_ref[:, 0:1] == iota((EVENTS, 1024), 1))
    emb[...] = dot(dot(pick, slots[...]).astype(BF), flip)

    def project(i, carry):
        at = pl.ds(pl.multiple_of(i * tall, tall), tall)
        y, scale = norm_stats(emb[at, :])
        y_in[at, :] = y
        sc_in[at, :] = jnp.broadcast_to(scale, (tall, 128))
        normed[at, :] = y.astype(BF)
        for block in range(4):
            lanes = slice(block * 512, (block + 1) * 512)
            value = dot(normed[at, :], proj_ref[:, lanes])
            z[at, lanes] = value
            act[at, lanes] = (value * sigmoid(value)).astype(BF)
        return carry

    lax.fori_loop(0, EVENTS // tall, project, 0)
    scaling = 1.0 / math.sqrt(128.0)

    def scores_of(head, block):
        end = (block + 1) * step
        q = act[block * step : end, pl.ds(pl.multiple_of(1024 + head * 128, 128), 128)]
        k = act[0:end, pl.ds(pl.multiple_of(1536 + head * 128, 128), 128)]
        s = dot(q, k, 1, 1) * scaling
        causal = block * step + iota((step, end), 0) >= iota((step, end), 1)
        return s, causal

    def attend(head, carry):
        cols = pl.ds(pl.multiple_of(head * 128, 128), 128)
        for block in range(2):
            end = (block + 1) * step
            s, causal = scores_of(head, block)
            weights = jnp.where(causal, s * sigmoid(s), 0.0).astype(BF)
            v = act[0:end, pl.ds(pl.multiple_of(512 + head * 128, 128), 128)]
            mixed[block * step : end, cols] = dot(weights, v)
        return carry

    lax.fori_loop(0, 4, attend, 0)

    def finish(i, carry):
        at = pl.ds(pl.multiple_of(i * tall, tall), tall)
        y, scale = norm_stats(mixed[at, :])
        u = act[at, 0:512].astype(F32)
        gate = (y * u).astype(BF)
        gated[at, :] = gate
        g = grad_ref[at, :]
        rows_ref[at, :] = (dot(gate, out_ref[...]) + emb[at, :]).astype(BF)
        d_gate = dot(g, out_ref[...], 1, 1).astype(BF).astype(F32)
        d_u = (d_gate * y).astype(BF).astype(F32)
        zu = z[at, 0:512]
        sig = sigmoid(zu)
        dz[at, 0:512] = (d_u * (sig * (1.0 + zu * (1.0 - sig)))).astype(BF)
        dmixed[at, :] = norm_grad(d_gate * u, y, scale).astype(BF)
        return carry

    lax.fori_loop(0, EVENTS // tall, finish, 0)
    dout_ref[...] = dot(gated[...], grad_ref[...], 0, 0).astype(BF)

    def attend_grad(head, carry):
        cols = pl.ds(pl.multiple_of(head * 128, 128), 128)
        vcols = pl.ds(pl.multiple_of(512 + head * 128, 128), 128)
        qcols = pl.ds(pl.multiple_of(1024 + head * 128, 128), 128)
        kcols = pl.ds(pl.multiple_of(1536 + head * 128, 128), 128)
        for block in (1, 0):
            end = (block + 1) * step
            rows = slice(block * step, end)
            s, causal = scores_of(head, block)
            sig = sigmoid(s)
            weights = jnp.where(causal, s * sig, 0.0).astype(BF)
            dm = dmixed[rows, cols]
            d_w = dot(dm, act[0:end, vcols], 1, 1).astype(BF).astype(F32)
            d_s = jnp.where(causal, d_w * (sig * (1.0 + s * (1.0 - sig))) * scaling, 0.0).astype(BF)
            v_part = dot(weights, dm, 0, 0)
            k_part = dot(d_s, act[rows, qcols], 0, 0)
            if block == 1:
                work_v[...] = v_part
                work_k[...] = k_part
            else:
                work_v[0:end, :] += v_part
                work_k[0:end, :] += k_part
            work[rows, :] = dot(d_s, act[0:end, kcols])

        def through(ct, where):
            value = z[:, where]
            sig = sigmoid(value)
            dz[:, where] = (ct.astype(BF).astype(F32) * (sig * (1.0 + value * (1.0 - sig)))).astype(BF)

        through(work[...], qcols)
        through(work_v[...], vcols)
        through(work_k[...], kcols)
        return carry

    lax.fori_loop(0, 4, attend_grad, 0)

    for block in range(4):
        lanes = slice(block * 512, (block + 1) * 512)
        dproj_ref[lanes, :] = dot(normed[...], dz[:, lanes], 0, 0).astype(BF)

    back = one_hot(source == (target % 8) * 64 + ((target // 8) % 8) * 8 + target // 64)

    def close(i, carry):
        at = pl.ds(pl.multiple_of(i * tall, tall), tall)
        d_normed = dot(dz[at, :], proj_ref[...], 1, 1).astype(BF).astype(F32)
        d_rows = norm_grad(d_normed, y_in[at, :], sc_in[at, 0:1]) + grad_ref[at, :].astype(F32)
        gated[at, :] = d_rows.astype(BF)
        return carry

    lax.fori_loop(0, EVENTS // tall, close, 0)
    turned = dot(gated[...], back).astype(BF)
    for half in range(2):
        for tlo in range(2):
            found = []
            for thi in range(2):
                k = half * 4 + thi * 2 + tlo
                place = one_hot(iota((128, EVENTS), 0) + k * 128 == slot_row_ref[0:1, :])
                found.append(dot(place, turned))
            for pair in range(4):
                lanes = slice(pair * 128, (pair + 1) * 128)
                x0, x1 = found[0][:, lanes], found[1][:, lanes]
                base = half * 16 + tlo * 8 + pair * 2
                tiles[pl.ds(base, 128, stride=32), :] = jnp.where(low, x0, half_turn(x1))
                tiles[pl.ds(base + 1, 128, stride=32), :] = jnp.where(low, half_turn(x0), x1)

    def narrow(i, carry):
        srcs = pl.ds(pl.multiple_of(i * 32, 32), 32)
        sent_ref[srcs] = tiles[pl.ds(pl.multiple_of(i * 1024, 1024), 1024), :].astype(BF).reshape(32, 2, 16, 128)
        return carry

    lax.fori_loop(0, 4, narrow, 0)


def layer(recv, slot_row, slot_col, w_proj, w_out, layer_grad):
    vm = pltpu.VMEM
    return pl.pallas_call(
        layer_kernel,
        out_shape=(
            jax.ShapeDtypeStruct((EVENTS, 512), BF),
            jax.ShapeDtypeStruct((OWNERS, 2, 16, 128), BF),
            jax.ShapeDtypeStruct((2048, 512), BF),
            jax.ShapeDtypeStruct((512, 512), BF),
        ),
        scratch_shapes=[
            vm((4096, 128), F32),
            vm((1024, 512), BF),
            vm((EVENTS, 512), F32),
            vm((EVENTS, 512), BF),
            vm((EVENTS, 512), F32),
            vm((EVENTS, 2048), F32),
            vm((EVENTS, 2048), BF),
            vm((EVENTS, 512), F32),
            vm((EVENTS, 512), F32),
            vm((EVENTS, 512), BF),
            vm((EVENTS, 2048), BF),
            vm((EVENTS, 512), BF),
            vm((EVENTS, 128), F32),
            vm((EVENTS, 128), F32),
            vm((EVENTS, 128), F32),
            vm((EVENTS, 128), F32),
        ],
        compiler_params=pltpu.CompilerParams(vmem_limit_bytes=34 * 1024 * 1024),
        name="layer",
    )(recv, slot_row, slot_col, w_proj, w_out, layer_grad)


def core_grad_kernel(
    arrived_ref, tile_ref, spread_ref, part_ref, lt_ref, middle_ref,
    first_out, middle_out, last_out,
    flipped, pg, ls, ss, fterm, lterm,
):
    half = pl.program_id(0)
    arrived = arrived_ref[...].reshape(OWNERS, 128)
    flipped[...] = jnp.transpose(arrived.astype(F32)).astype(I32) - 1
    _, middle_col, _ = index_columns(arrived, half)
    mask0, mask1 = slice_masks(middle_col)
    group = 128
    low = low_lanes((group, 8, 128))
    own = (iota((group, 16, 128), 1) // 8) == (iota((group, 16, 128), 2) // 64)

    def events(i, carry):
        srcs = pl.ds(pl.multiple_of(i * group, group), group)
        stored = pl.ds(pl.multiple_of(half * OWNERS + i * group, group), group)
        tile = tile_ref[srcs, 0]
        g = jnp.concatenate([tile[:, :, 0:64], tile[:, :, 64:128]], axis=1)
        wide = pl.ds(pl.multiple_of(i * group * 16, group * 16), group * 16)
        terms = bdot(g, part_ref[srcs], 2, 1)
        for side in range(2):
            x = terms[:, side * 16 : (side + 1) * 16, side * 128 : (side + 1) * 128]
            x = jnp.where(own, x, 0.0).reshape(group * 16, 128)
            ls[side, wide, :] = x + half_turn(x)
        grads = bdot(g, lt_ref[stored], 1, 1)
        for pair in range(4):
            lanes = slice(pair * 128, (pair + 1) * 128)
            for side in range(2):
                even = grads[:, pair * 16 : pair * 16 + 8, side * 128 : (side + 1) * 128]
                odd = grads[:, pair * 16 + 8 : pair * 16 + 16, side * 128 : (side + 1) * 128]
                v0 = jnp.where(low, even, half_turn(odd))
                v1 = jnp.where(low, half_turn(even), odd)
                for t, v in ((2 * side, v0), (2 * side + 1, v1)):
                    at = pl.ds(pl.multiple_of(t * 1024 + i * group * 8, group * 8), group * 8)
                    pg[at, lanes] = v.reshape(group * 8, 128).astype(BF)
        return carry

    lax.fori_loop(0, OWNERS // group, events, 0)
    low = low_lanes((128, 128))
    middle_part = jnp.zeros((256, 512), F32)
    for t in range(4):
        at = slice(t * 1024, (t + 1) * 1024)
        middle_part += dot(spread_ref[pl.ds(pl.multiple_of(half * 4096 + t * 1024, 1024), 1024), :], pg[at, :], 0, 0)
        back = dot(pg[at, :], middle_ref[...], 1, 1)
        ss[0] = back[:, 0:128]
        ss[1] = back[:, 128:256]
        rows = slice(t * 128, (t + 1) * 128)
        keep = pl.ds(pl.multiple_of(half * 512 + t * 128, 128), 128)
        m0, m1 = mask0[rows], mask1[rows]
        for pair in range(4):
            lanes = slice(pair * 128, (pair + 1) * 128)
            found = []
            for odd in range(2):
                where = pl.ds(pair * 2 + odd, 128, stride=8)
                x = jnp.where(m0, ss[0, where, :], 0.0) + jnp.where(m1, ss[1, where, :], 0.0)
                found.append(x + half_turn(x))
            fterm[keep, lanes] = jnp.where(low, found[0], found[1]).astype(BF)
            base = (t % 2) * 8 + pair * 2
            y0 = ls[t // 2, pl.ds(base, 128, stride=16), :]
            y1 = ls[t // 2, pl.ds(base + 1, 128, stride=16), :]
            lterm[keep, lanes] = jnp.where(low, y0, y1).astype(BF)

    source = iota((512, 512), 0)
    perm = one_hot(iota((512, 512), 1) == (source % 64) * 8 + source // 64)
    done = pl.ds(pl.multiple_of(half * 512, 512), 512)
    lterm[done, :] = dot(lterm[done, :], perm).astype(BF)

    def index_row(digit):
        return jnp.concatenate([flipped[digit * 8 + t : digit * 8 + t + 1, :] for t in range(8)], axis=1)

    @pl.when(half == 0)
    def _():
        middle_out[...] = middle_part

    @pl.when(half == 1)
    def _():
        middle_out[...] += middle_part

    @pl.when(half == 1)
    def _():
        first_row = index_row(0)
        last_row = index_row(2)

        def scatter_first(i, carry):
            at = pl.ds(pl.multiple_of(i * 256, 256), 256)
            place = one_hot(iota((256, 1024), 0) + i * 256 == first_row)
            first_out[at, :] = dot(place, fterm[...]).astype(BF)
            return carry

        def scatter_last(i, carry):
            at = pl.ds(pl.multiple_of(i * 256, 256), 256)
            place = one_hot(iota((256, 1024), 0) + i * 256 == last_row)
            last_out[at, :] = dot(place, lterm[...]).astype(BF)
            return carry

        lax.fori_loop(0, 8, scatter_first, 0)
        lax.fori_loop(0, 4, scatter_last, 0)


def core_grads(arrived, tiles, spread, part, lt, middle_core):
    vm = pltpu.VMEM
    return pl.pallas_call(
        core_grad_kernel,
        grid=(2,),
        in_specs=[
            pl.BlockSpec((OWNERS, 1, 128), lambda h: (0, 0, 0)),
            pl.BlockSpec((OWNERS, 1, 16, 128), lambda h: (0, h, 0, 0)),
            pl.BlockSpec(memory_space=pltpu.VMEM),
            pl.BlockSpec((OWNERS, 64, 256), lambda h: (h, 0, 0)),
            pl.BlockSpec(memory_space=pltpu.VMEM),
            pl.BlockSpec((256, 512), lambda h: (0, 0)),
        ],
        out_specs=(
            pl.BlockSpec((2048, 512), lambda h: (0, 0)),
            pl.BlockSpec((256, 512), lambda h: (0, 0)),
            pl.BlockSpec((1024, 512), lambda h: (0, 0)),
        ),
        out_shape=(
            jax.ShapeDtypeStruct((2048, 512), BF),
            jax.ShapeDtypeStruct((256, 512), F32),
            jax.ShapeDtypeStruct((1024, 512), BF),
        ),
        scratch_shapes=[
            vm((128, 128), I32),
            vm((4096, 512), BF),
            vm((2, 2048, 128), F32),
            vm((2, 1024, 128), F32),
            vm((1024, 512), BF),
            vm((1024, 512), BF),
        ],
        compiler_params=pltpu.CompilerParams(vmem_limit_bytes=36 * 1024 * 1024),
        name="core_grads",
    )(arrived, tiles, spread, part, lt, middle_core)


class Place:
    def __init__(self):
        dp = lax.axis_index("dp")
        cores = lax.axis_index("cores")
        self.at = (cores // 2, dp // 4, lax.rem(dp, 4))
        self.core = lax.rem(cores, 2)

    def along(self, dim, offset):
        at = list(self.at)
        at[dim] = lax.rem(at[dim] + offset, 4)
        return at[dim], (at[1] * 4 + at[2], at[0] * 2 + self.core)

    def sibling(self):
        x, y, z = self.at
        return (y * 4 + z, x * 2 + 1 - self.core)


ORDERS = ((0, 1, 2), (1, 2, 0), (2, 0, 1))
SIZES = (256, 64, 16)


def reduce_kernel(
    first_ref, proj_ref, last_ref, out_ref,
    total0, total1, total2,
    rest, pair0, pair1, pair2, sum0, sum1, sum2,
    got00, got01, got02, got10, got11, got12, got20, got21, got22,
    halves0, halves1, halves2, send_sem, recv_sem,
):
    place = Place()
    core = place.core
    barrier = pltpu.get_barrier_semaphore()
    partners = [place.sibling()] + [place.along(d, o)[1] for d in range(3) for o in (1, 2, 3)]
    for who in partners:
        pl.semaphore_signal(barrier, inc=1, device_id=who, device_id_type=MESH)
    for block in range(12):
        row = (block // 3) * 512
        lanes = slice((block % 3) * 128, (block % 3 + 1) * 128)
        if block < 8:
            value = last_ref[(block // 4) * 512 : (block // 4 + 1) * 512, (block % 4) * 128 : (block % 4 + 1) * 128]
        else:
            value = out_ref[:, (block % 4) * 128 : (block % 4 + 1) * 128]
        rest[row : row + 512, lanes] = value
    source = (first_ref, proj_ref, rest)
    total = (total0, total1, total2)
    pair = (pair0, pair1, pair2)
    sums = (sum0, sum1, sum2)
    got = ((got00, got01, got02), (got10, got11, got12), (got20, got21, got22))
    halves = (halves0, halves1, halves2)
    pl.semaphore_wait(barrier, len(partners))
    pending = []

    def start(part, stage, slot, src, dst, who):
        copy = pltpu.make_async_remote_copy(
            src_ref=src,
            dst_ref=dst,
            send_sem=send_sem.at[part, stage, slot],
            recv_sem=recv_sem.at[part, stage, slot],
            device_id=who,
            device_id_type=MESH,
        )
        copy.start()
        pending.append(copy)
        return copy

    def rows(start_row, size):
        return pl.ds(pl.multiple_of(start_row, 16), size)

    base = [core * 1024 for _ in range(3)]
    flight = {}
    for slot in (2, 1, 3, 0):
        for part in range(3):
            quarter, _ = place.along(ORDERS[part][0], slot)
            flight[part, slot] = start(
                part, 0, slot,
                source[part].at[rows((1 - core) * 1024 + quarter * 256, 256)],
                pair[part].at[rows(quarter * 256, 256)],
                place.sibling(),
            )
    moving = {}

    def pair_sum(part, slot):
        quarter, _ = place.along(ORDERS[part][0], slot)
        flight[part, slot].wait_recv()
        at = rows(quarter * 256, 256)
        mine = source[part][rows(core * 1024 + quarter * 256, 256), :].astype(F32)
        sums[part][at, :] = (mine + pair[part][at, :].astype(F32)).astype(BF)
        return quarter * 256

    for part in range(3):
        at = pair_sum(part, 2)
        for slot, lead, way in ((0, 0, 1), (2, 128, 3)):
            who = place.along(ORDERS[part][0], way)[1]
            src = sums[part].at[rows(at + lead, 128)]
            moving[part, slot] = start(part, 1, slot, src, halves[part].at[slot // 2], who)
    for way in (1, 3):
        for part in range(3):
            at = pair_sum(part, way)
            slot, lead = (0, 0) if way == 1 else (2, 128)
            moving[part, slot].wait_recv()
            piece = rows(at + lead, 128)
            more = halves[part][slot // 2].astype(F32)
            sums[part][piece, :] = (sums[part][piece, :].astype(F32) + more).astype(BF)
            who = place.along(ORDERS[part][0], way)[1]
            src = sums[part].at[rows(at, 256)]
            moving[part, way] = start(part, 1, way, src, got[part][0].at[way // 2], who)
    for part in range(3):
        pair_sum(part, 0)
    offset = [0, 0, 0]
    for level in range(3):
        size = SIZES[level]
        following = {}
        for part in range(3):
            mine = place.at[ORDERS[part][level]]
            offset[part] = offset[part] + mine * size
            ways = (1, 3) if level == 0 else (1, 2, 3)
            for slot in ways:
                moving[part, slot].wait_recv()
            at = rows(offset[part], size)
            value = sums[part][at, :].astype(F32)
            for slot in range(len(ways)):
                value = value + got[part][level][slot].astype(F32)
            if level < 2:
                sums[part][at, :] = value.astype(BF)
                for slot in (1, 2, 3):
                    quarter, who = place.along(ORDERS[part][level + 1], slot)
                    src = sums[part].at[rows(offset[part] + quarter * SIZES[level + 1], SIZES[level + 1])]
                    following[part, slot] = start(part, level + 2, slot, src, got[part][level + 1].at[slot - 1], who)
            else:
                where = rows(core * 1024 + offset[part], size)
                total[part][where, :] = value.astype(BF)
                for slot in (1, 2, 3):
                    who = place.along(ORDERS[part][2], slot)[1]
                    ref = total[part].at[where]
                    following[part, slot] = start(part, 4, slot, ref, ref, who)
        moving = following
    final = []
    for level in (1, 0):
        following = {}
        for part in range(3):
            mine = place.at[ORDERS[part][level + 1]]
            offset[part] = offset[part] - mine * SIZES[level + 1]
            for slot in (1, 2, 3):
                moving[part, slot].wait_recv()
            where = rows(core * 1024 + offset[part], SIZES[level])
            ref = total[part].at[where]
            for slot in (1, 3) if level == 0 else (1, 2, 3):
                who = place.along(ORDERS[part][level], slot)[1]
                following[part, slot] = start(part, 6 - level, slot, ref, ref, who)
            if level == 0:
                final.append(start(part, 7, 0, ref, ref, place.sibling()))
        moving = following

    def piece_of(part, way, lead, size):
        quarter = place.along(ORDERS[part][0], way)[0]
        return total[part].at[rows(core * 1024 + quarter * 256 + lead, size)]

    for way in (1, 3):
        for part in range(3):
            moving[part, way].wait_recv()
            slot, lead = (0, 0) if way == 1 else (2, 128)
            ref = piece_of(part, 4 - way, lead, 128)
            who = place.along(ORDERS[part][0], way)[1]
            moving[part, slot] = start(part, 6, slot, ref, ref, who)
            ref = piece_of(part, 4 - way, 0, 256)
            final.append(start(part, 7, way, ref, ref, place.sibling()))
    for part in range(3):
        moving[part, 0].wait_recv()
        moving[part, 2].wait_recv()
        ref = piece_of(part, 2, 0, 256)
        final.append(start(part, 7, 2, ref, ref, place.sibling()))
    for copy in final:
        copy.wait_recv()
    for copy in pending:
        copy.wait_send()


def reduce_all(first_part, proj_grad, last_part, out_grad, ident):
    vm = pltpu.VMEM
    widths = (512, 512, 384)
    return pl.pallas_call(
        reduce_kernel,
        out_shape=tuple(jax.ShapeDtypeStruct((2048, w), BF) for w in widths),
        in_specs=[pl.BlockSpec(memory_space=vm)] * 4,
        out_specs=tuple(pl.BlockSpec(memory_space=vm) for _ in widths),
        scratch_shapes=[vm((2048, 384), BF)]
        + [vm((1024, w), BF) for w in widths]
        + [vm((1024, w), BF) for w in widths]
        + [vm((3, size, w), BF) for w in widths for size in SIZES]
        + [vm((2, 128, w), BF) for w in widths]
        + [pltpu.SemaphoreType.DMA((3, 8, 4))] * 2,
        compiler_params=pltpu.CompilerParams(
            collective_id=ident, has_side_effects=True, vmem_limit_bytes=28 * 1024 * 1024
        ),
        name="reduce_all",
    )(first_part, proj_grad, last_part, out_grad)


def widen_kernel(a_ref, b_ref, c_ref, first_ref, last_ref, proj_ref, out_ref):
    first_ref[...] = a_ref[...].astype(F32)
    for block in range(4):
        lanes = slice(block * 512, (block + 1) * 512)
        proj_ref[:, lanes] = b_ref[block].astype(F32)
    for block in range(12):
        value = c_ref[block // 3, :, (block % 3) * 128 : (block % 3 + 1) * 128].astype(F32)
        lanes = slice((block % 4) * 128, (block % 4 + 1) * 128)
        if block < 8:
            last_ref[block // 4, :, lanes] = value
        else:
            out_ref[:, lanes] = value


def widen(a, b, c):
    steps = 8
    rows = 512 // steps
    first, last, proj, out = pl.pallas_call(
        widen_kernel,
        grid=(steps,),
        in_specs=[
            pl.BlockSpec((4 * rows, 512), lambda i: (i, 0)),
            pl.BlockSpec((4, rows, 512), lambda i: (0, i, 0)),
            pl.BlockSpec((4, rows, 384), lambda i: (0, i, 0)),
        ],
        out_specs=(
            pl.BlockSpec((4 * rows, 512), lambda i: (i, 0)),
            pl.BlockSpec((2, rows, 512), lambda i: (0, i, 0)),
            pl.BlockSpec((rows, 2048), lambda i: (i, 0)),
            pl.BlockSpec((rows, 512), lambda i: (i, 0)),
        ),
        out_shape=(
            jax.ShapeDtypeStruct((2048, 512), F32),
            jax.ShapeDtypeStruct((2, 512, 512), F32),
            jax.ShapeDtypeStruct((512, 2048), F32),
            jax.ShapeDtypeStruct((512, 512), F32),
        ),
        compiler_params=pltpu.CompilerParams(vmem_limit_bytes=20 * 1024 * 1024),
        name="widen",
    )(a, b.reshape(4, 512, 512), c.reshape(4, 512, 384))
    return first, last.reshape(1024, 512), proj, out


def exchange(x):
    return lax.all_to_all(x, AXES, split_axis=0, concat_axis=0, tiled=True)


def per_device(item_digits, first_core, middle_core, last_core, w_proj, w_out, layer_grad):
    arrived, slot_row, slot_col = prep(item_digits)
    arrived = arrived.reshape(OWNERS, 1, 128)
    built, spread, part, lt = build(arrived, first_core, middle_core, last_core)
    recv = exchange(built)
    layer_rows, sent, proj_grad, out_grad = layer(recv, slot_row, slot_col, w_proj, w_out, layer_grad)
    tiles = exchange(sent)
    first_part, grad_middle, last_part = core_grads(arrived, tiles, spread, part, lt, middle_core)
    totals = reduce_all(first_part, proj_grad, last_part, out_grad, 2)
    grad_first, grad_last, proj_total, out_total = widen(*totals)
    return (layer_rows, grad_first, grad_middle, grad_last, proj_total, out_total)


def solution(mesh):
    return jax.shard_map(
        per_device,
        mesh=mesh,
        in_specs=(
            P(None, AXES),
            P(),
            P(AXES, None),
            P(),
            P(),
            P(),
            P(AXES, None),
        ),
        out_specs=(P(AXES, None), P(), P(AXES, None), P(), P(), P()),
        check_vma=False,
    )
```
